32 devices in a mesh: dom: 4 (over y, core), fsdp: 8 (over z, x).
Axes of the slice: x: 2, y: 2, z: 4, core: 2. Of those that a mesh axis runs over, the one named last changes fastest.
Arguments:
- tokens: bfloat16 [8192, 1536], P(('dom', 'fsdp')), may hold values from -6 to 6
- gain: bfloat16 [1536], P('fsdp'), may hold values from 0.099609375 to 1.8984375
- kv_weight: bfloat16 [1536, 512], P('fsdp'), may hold values from -0.15625 to 0.15625
- positions: int32 [8192], P(('dom', 'fsdp')), may hold values from 0 to 4095
- cotangent: bfloat16 [8192, 512], P(('dom', 'fsdp')), may hold values from -6 to 6
- counts: int32 [4, 8], replicated, may hold values from 0 to 2, as said below
- ratios: int32 [4], replicated, may hold values from 1 to 8
Outputs:
- keys_values: bfloat16 [8192, 512], P(('dom', 'fsdp'))
- weight_grad: float32 [1536, 512], P('fsdp')
- gain_grad: float32 [1536], P('fsdp')
The draws below stay inside these ranges and needn't reach their ends.
Inputs may be any that keep to these rules, and one draw needn't show every extreme that they name: counts gives each device's live rows in blocks of 128; every domain has a device with one or more live blocks, and some device holds 2 live blocks in every draw.
All inputs are finite; a program needn't handle non-finite values.
Results may differ from the reference program's by a relative error of at most 0.0051.
Values may be sent and summed in bfloat16 or wider, within the bound.
No kernel may reach another device: no remote copies, remote signals or barrier semaphores. Data moves between devices by JAX's collectives and lax.ppermute only.
A program may use at most 64 MiB of HBM per device.

```python
import jax
import jax.numpy as jnp
from jax import lax

D = 1536
KVH = 2
HD = 128
BLOCK = 128
BLK = 2
ROWS_DEV = 256
DOMAINS = 4
GROUP = 8
TOKENS = 8192


def draw_counts(key, part):
    keys = jax.random.split(key, 5)
    levels = jax.random.randint(keys[0], (DOMAINS, 1), 1, BLK + 1)
    raw = jax.random.randint(keys[1], (DOMAINS, GROUP), 0, 1048576)
    blocks = raw % (levels + 1)
    anchor = jax.random.randint(keys[2], (DOMAINS, 1), 0, GROUP)
    anchored = jnp.arange(GROUP)[None, :] == anchor
    blocks = jnp.where(anchored, jnp.maximum(blocks, 1), blocks)
    domain_pick = jax.random.randint(keys[3], (), 0, DOMAINS)
    member_pick = jax.random.randint(keys[4], (), 0, GROUP)
    chosen = (jnp.arange(DOMAINS)[:, None] == domain_pick) & (jnp.arange(GROUP)[None, :] == member_pick)
    return jnp.where(chosen, BLK, blocks).astype(jnp.int32)


def set_ends(result, own_key, least, high):
    longest = result.shape.index(max(result.shape))
    spots = []
    for shift in (0, 1):
        where = [jax.random.randint(jax.random.fold_in(own_key, axis), (), 0, length) for axis, length in enumerate(result.shape)]
        where[longest] = (where[longest] + shift) % result.shape[longest]
        spots.append(tuple(where))
    return result.at[spots[0]].set(least).at[spots[1]].set(high)


def with_spikes(entries, stream_key, source, target, shards_of, factor):
    def block_of(axis_at):
        return (jnp.arange(entries.shape[axis_at]) // (entries.shape[axis_at] // shards_of)).reshape((-1,) + (1,) * (entries.ndim - 1 - axis_at))

    one_side = jax.random.permutation(stream_key, shards_of)[block_of(target)]
    far = (block_of(target) + shards_of // 2) % shards_of
    return jnp.where((block_of(source) == one_side) | (block_of(source) == far), factor * entries, entries)


def block_scale(key, extent, shards, low, high):
    level = 1.0
    for axis_at, shards_of in shards:
        heights = jax.random.uniform(jax.random.fold_in(jax.random.fold_in(key, 6), axis_at), (shards_of,), jnp.float32, low / len(shards), high / len(shards))
        level = level * jnp.repeat(jnp.exp(heights), extent[axis_at] // shards_of).reshape((-1,) + (1,) * (len(extent) - 1 - axis_at))
    return level


def bell_draw(rng, shape, spread, most, cuts=(), kind=jnp.bfloat16):
    entries = jax.random.normal(rng, shape, jnp.float32) * spread
    if len(cuts) > 0:
        entries = block_scale(rng, shape, cuts, -0.22, 0.18) * entries
    return jnp.clip(entries, min=-most, max=most).astype(kind)


def heavy_noise(stream_key, dims, deviation, most, cuts, heavy, kind=jnp.bfloat16):
    entries = deviation * jax.random.normal(stream_key, dims, jnp.float32)
    if cuts:
        entries = entries * block_scale(stream_key, dims, cuts, -0.22, 0.18)
    return jnp.clip(with_spikes(entries, jax.random.fold_in(stream_key, 3), *heavy), -most, most).astype(kind)


def setup_inputs(seed: int = 0) -> dict:
    seeds = jax.random.split(jax.random.key(seed), 8)
    tokens = heavy_noise(seeds[0], (TOKENS, D), 1.0, 6.0, ((0, 32),), (0, 1, 32, 2.75))
    gain = jnp.clip(1.0 + 0.18 * jax.random.normal(seeds[1], (D,), jnp.float32), 0.099609375, 1.8984375).astype(jnp.bfloat16)
    kv_weight = bell_draw(seeds[2], (D, 2 * KVH * HD), D ** -0.5, 0.15625, ((0, 8),))
    positions = set_ends(jax.random.randint(seeds[3], (TOKENS,), 0, 4096), jax.random.fold_in(seeds[3], 1), 0, 4095).astype(jnp.int32)
    cotangent = bell_draw(seeds[4], (TOKENS, 2 * KVH * HD), 1.0, 6.0, ((0, 32),))
    counts = draw_counts(jax.random.fold_in(seeds[7], 71), 0)
    ratios = set_ends(jax.random.randint(seeds[6], (DOMAINS,), 1, 9), jax.random.fold_in(seeds[6], 1), 1, 8).astype(jnp.int32)
    return dict(tokens=tokens, gain=gain, kv_weight=kv_weight, positions=positions, cotangent=cotangent, counts=counts, ratios=ratios)


def rotary_tables(position_ids, half_width, head_size):
    exponents = jnp.arange(half_width, dtype=jnp.float32) * (2.0 / head_size)
    frequency = jnp.power(jnp.float32(1000000.0), -exponents)
    angles = position_ids.astype(jnp.float32)[:, None] * frequency[None, :]
    return (jnp.cos(angles)[:, None, :], jnp.sin(angles)[:, None, :])

def rotate_heads(values, cosines, sines, heads, head_size, direction):
    rows = values.shape[0]
    half_width = head_size // 2
    shaped = values.reshape(rows, heads, head_size)
    first = shaped[:, :, :half_width]
    second = shaped[:, :, half_width:]
    turned = jnp.concatenate([first * cosines - direction * second * sines, second * cosines + direction * first * sines], axis=2)
    return turned.reshape(rows, heads * head_size)

def normalize(token_rows, gain):
    token_float = token_rows.astype(jnp.float32)
    mean_square = lax.optimization_barrier(jnp.mean(token_float * token_float, axis=1, keepdims=True))
    normed = token_float * lax.rsqrt(mean_square + 1e-06)
    scaled = (normed * gain.astype(jnp.float32)[None, :]).astype(jnp.bfloat16)
    return (normed, scaled)

def reference(tokens, gain, kv_weight, positions, cotangent, counts, ratios):
    devices_all = DOMAINS * GROUP
    key_width = KVH * HD
    domain_rows = (BLOCK * lax.optimization_barrier(jnp.sum(counts, axis=1))).astype(jnp.float32)
    live_total = jnp.sum(domain_rows)
    ratio_float = ratios.astype(jnp.float32)
    factor = ratio_float / jnp.sum(ratio_float) * live_total / domain_rows
    row_ids = jnp.arange(ROWS_DEV, dtype=jnp.int32)

    def one_device(running, inputs):
        token_rows, position_ids, cot_rows, device = inputs
        domain_index = device // GROUP
        member = device % GROUP
        normed, scaled = normalize(token_rows, gain)
        projected = jnp.dot(scaled, kv_weight, preferred_element_type=jnp.float32)
        cosines, sines = rotary_tables(position_ids, HD // 2, HD)
        keys_out = jnp.concatenate([rotate_heads(projected[:, :key_width], cosines, sines, KVH, HD, 1.0), projected[:, key_width:]], axis=1).astype(jnp.bfloat16)
        live_rows = row_ids < BLOCK * counts[domain_index, member]
        row_factor = jnp.where(live_rows, factor[domain_index], jnp.float32(0.0))
        weighted = cot_rows.astype(jnp.float32) * row_factor[:, None]
        upstream = jnp.concatenate([rotate_heads(weighted[:, :key_width], cosines, sines, KVH, HD, -1.0), weighted[:, key_width:]], axis=1).astype(jnp.bfloat16)
        weight_term = jnp.dot(scaled.T, upstream, preferred_element_type=jnp.float32)
        scaled_grad = jnp.dot(upstream, kv_weight.T, preferred_element_type=jnp.float32)
        gain_term = lax.optimization_barrier(jnp.sum(scaled_grad * normed, axis=0))
        return ((running[0] + weight_term, running[1] + gain_term), keys_out)
    initial = (jnp.zeros((D, 2 * key_width), jnp.float32), jnp.zeros((D,), jnp.float32))
    inputs = (tokens.reshape(devices_all, ROWS_DEV, D), positions.reshape(devices_all, ROWS_DEV), cotangent.reshape(devices_all, ROWS_DEV, 2 * key_width), jnp.arange(devices_all, dtype=jnp.int32))
    sums, outputs = lax.scan(one_device, initial, inputs)
    root = jnp.sqrt(live_total)
    return (outputs.reshape(TOKENS, 2 * key_width), sums[0] / root, sums[1] / root)
```

```python
import jax
import jax.numpy as jnp
from jax import lax
from jax.sharding import Mesh
from jax.sharding import PartitionSpec as P

KVH = 2
HD = 128
BLOCK = 128


def rotary_tables(position_ids, half_width, head_size):
    exponents = jnp.arange(half_width, dtype=jnp.float32) * (2.0 / head_size)
    frequency = jnp.power(jnp.float32(1000000.0), -exponents)
    angles = position_ids.astype(jnp.float32)[:, None] * frequency[None, :]
    return (jnp.cos(angles)[:, None, :], jnp.sin(angles)[:, None, :])


def rotate_heads(values, cosines, sines, heads, head_size, direction):
    rows = values.shape[0]
    half_width = head_size // 2
    shaped = values.reshape(rows, heads, head_size)
    first = shaped[:, :, :half_width]
    second = shaped[:, :, half_width:]
    turned = jnp.concatenate(
        [
            first * cosines - direction * second * sines,
            second * cosines + direction * first * sines,
        ],
        axis=2,
    )
    return turned.reshape(rows, heads * head_size)


def body(outer, members, tokens, gain, kv_weight, positions, cotangent, counts, ratios):
    domains = 2 * outer
    core = lax.axis_index("core")
    domain_index = lax.axis_index("outer") * 2 + core
    member = lax.axis_index("fsdp")
    gain_float = gain.astype(jnp.float32)
    gained = (kv_weight.astype(jnp.float32) * gain_float[:, None]).astype(jnp.bfloat16)
    weights = lax.all_gather(gained, "fsdp", axis=0, tiled=True)

    row_count, width = tokens.shape
    shard_rows, columns = kv_weight.shape
    key_width = KVH * HD
    token_float = tokens.astype(jnp.float32)
    mean_square = jnp.mean(token_float * token_float, axis=1, keepdims=True)
    normed = (token_float * lax.rsqrt(mean_square + 1e-06)).astype(jnp.bfloat16)
    cosines, sines = rotary_tables(positions, HD // 2, HD)

    domain_rows = (BLOCK * jnp.sum(counts, axis=1)).astype(jnp.float32)
    live_total = jnp.sum(domain_rows)
    ratio_float = ratios.astype(jnp.float32)
    factor = ratio_float / jnp.sum(ratio_float) * live_total / domain_rows
    domain_hits = jnp.arange(counts.shape[0]) == domain_index
    own_factor = jnp.sum(jnp.where(domain_hits, factor, jnp.float32(0.0)))
    member_hits = domain_hits[:, None] & (jnp.arange(counts.shape[1]) == member)[None, :]
    own_blocks = jnp.sum(jnp.where(member_hits, counts, 0))
    live_rows = jnp.arange(row_count, dtype=jnp.int32) < BLOCK * own_blocks
    row_factor = jnp.where(live_rows, own_factor, jnp.float32(0.0))
    weighted = cotangent.astype(jnp.float32) * row_factor[:, None]
    upstream = jnp.concatenate(
        [
            rotate_heads(weighted[:, :key_width], cosines, sines, KVH, HD, -1.0),
            weighted[:, key_width:],
        ],
        axis=1,
    ).astype(jnp.bfloat16)

    term = lax.dot_general(
        normed, upstream, (((0,), (0,)), ((), ())), preferred_element_type=jnp.float32
    )
    half = columns // 2
    low, high = term[:, :half], term[:, half:]
    own = jnp.where(core == 0, low, high)
    given = jnp.where(core == 0, high, low).astype(jnp.bfloat16)
    taken = lax.ppermute(given, "core", [(0, 1), (1, 0)])
    pair = (own + taken.astype(jnp.float32)).astype(jnp.bfloat16)
    piece = half // outer
    parts = pair.reshape(members, shard_rows, outer, piece).transpose(2, 0, 1, 3)
    parts = parts.reshape(outer * members, shard_rows, piece)
    parts = lax.all_to_all(parts, ("outer", "fsdp"), 0, 0, tiled=True)
    mine = jnp.sum(parts.astype(jnp.float32), axis=0)
    root = jnp.sqrt(live_total)
    place = core * outer + lax.axis_index("outer")
    gathered = jnp.zeros((domains, shard_rows, piece), jnp.float32)
    gathered = lax.dynamic_update_slice(gathered, mine[None], (place, 0, 0))
    for shift in range(1, domains):
        pairs = []
        for source in range(domains):
            pairs.append((source, (source + shift) % domains))
        got = lax.ppermute(mine, ("outer", "core"), pairs)
        source = lax.rem(domain_index + (domains - shift), domains)
        at = lax.rem(source, 2) * outer + source // 2
        gathered = lax.dynamic_update_slice(gathered, got[None], (at, 0, 0))
    total = gathered.transpose(1, 0, 2).reshape(shard_rows, columns)
    weight_grad = total * (gain_float[:, None] / root)
    gain_grad = jnp.sum(total * kv_weight.astype(jnp.float32), axis=1) / root

    projected = jnp.dot(normed, weights, preferred_element_type=jnp.float32)
    keys_out = jnp.concatenate(
        [
            rotate_heads(projected[:, :key_width], cosines, sines, KVH, HD, 1.0),
            projected[:, key_width:],
        ],
        axis=1,
    ).astype(jnp.bfloat16)
    return (keys_out, weight_grad, gain_grad)


def solution(mesh):
    domains, members = mesh.shape["dom"], mesh.shape["fsdp"]
    outer = domains // 2
    split = Mesh(mesh.devices.reshape(outer, 2, members), ("outer", "core", "fsdp"))
    everything = ("outer", "core", "fsdp")

    def whole(*args):
        return body(outer, members, *args)

    return jax.shard_map(
        whole,
        mesh=split,
        in_specs=(
            P(everything, None),
            P("fsdp"),
            P("fsdp", None),
            P(everything),
            P(everything, None),
            P(),
            P(),
        ),
        out_specs=(P(everything, None), P("fsdp", None), P("fsdp")),
        check_vma=False,
    )
```

```python
import functools

import jax
import jax.numpy as jnp
import numpy as np
from jax import lax
from jax.experimental import pallas as pl
from jax.experimental.pallas import tpu as pltpu
from jax.sharding import Mesh
from jax.sharding import PartitionSpec as P

KVH = 2
HD = 128
BLOCK = 128
EVERY = ("outer", "core", "fsdp")
VMEM_BYTES = 40 * 1024 * 1024


def to_column(line):
    n = line.shape[1]
    rows = lax.broadcasted_iota(jnp.int32, (n, n), 0)
    lanes = lax.broadcasted_iota(jnp.int32, (n, n), 1)
    spread = jnp.broadcast_to(line, (n, n))
    return jnp.sum(jnp.where(rows == lanes, spread, 0.0), axis=1, keepdims=True)


def full_sum(values):
    return jnp.sum(jnp.sum(values, axis=1, keepdims=True), axis=0, keepdims=True)


def call(kernel, out_shape, args, flops=0, bytes_accessed=1000000):
    return pl.pallas_call(
        kernel,
        out_shape=out_shape,
        in_specs=[pl.BlockSpec(memory_space=pltpu.VMEM)] * len(args),
        out_specs=jax.tree.map(lambda _: pl.BlockSpec(memory_space=pltpu.VMEM), out_shape),
        compiler_params=pltpu.CompilerParams(vmem_limit_bytes=VMEM_BYTES),
        cost_estimate=pl.CostEstimate(
            flops=flops, bytes_accessed=bytes_accessed, transcendentals=0
        ),
    )(*args)


def fold_kernel(weight_ref, gain_ref, half_ref):
    half = half_ref.shape[1]
    core = lax.axis_index("core")
    gains = to_column(gain_ref[...].astype(jnp.float32))
    columns = pl.ds(pl.multiple_of(core * half, half), half)
    half_ref[...] = (weight_ref[:, columns].astype(jnp.float32) * gains).astype(jnp.bfloat16)


def backward_kernel(
    tokens_ref, positions_ref, frequency_ref, cotangent_ref, counts_ref, ratios_ref,
    normed_ref, cosines_ref, sines_ref, own_ref, given_ref,
):
    rows, width = tokens_ref.shape
    core = lax.axis_index("core")
    domain = lax.axis_index("outer") * 2 + core
    member = lax.axis_index("fsdp")

    step = 32
    for start in range(0, rows, step):
        block = tokens_ref[start : start + step, :].astype(jnp.float32)
        mean_square = jnp.sum(block * block, axis=1, keepdims=True) * (1.0 / width)
        normed_ref[start : start + step, :] = (
            block * lax.rsqrt(mean_square + 1e-06)
        ).astype(jnp.bfloat16)

    lines = positions_ref[...].astype(jnp.float32)
    place = jnp.concatenate(
        [to_column(lines[i : i + 1, :]) for i in range(lines.shape[0])], axis=0
    )
    angles = place * frequency_ref[...]
    cosines = jnp.cos(angles)
    lanes = lax.broadcasted_iota(jnp.int32, (rows, HD), 1)
    sines = jnp.sin(angles)
    sines = jnp.where(lanes < HD // 2, -sines, sines)
    cosines_ref[...] = cosines
    sines_ref[...] = sines

    counts = counts_ref[...].astype(jnp.float32)
    ratios = ratios_ref[...].astype(jnp.float32)
    at_domain = lax.broadcasted_iota(jnp.int32, counts.shape, 0) == domain
    at_member = lax.broadcasted_iota(jnp.int32, counts.shape, 1) == member
    ratio_at = lax.broadcasted_iota(jnp.int32, ratios.shape, 1) == domain
    live_total = full_sum(counts) * float(BLOCK)
    own_rows = full_sum(jnp.where(at_domain, counts, 0.0)) * float(BLOCK)
    own_live = full_sum(jnp.where(at_domain & at_member, counts, 0.0)) * float(BLOCK)
    own_ratio = full_sum(jnp.where(ratio_at, ratios, 0.0))
    factor = own_ratio / full_sum(ratios) * live_total / own_rows
    row_ids = lax.broadcasted_iota(jnp.int32, (rows, 1), 0).astype(jnp.float32)
    row_factor = jnp.where(row_ids < own_live, factor, 0.0)

    weighted = cotangent_ref[...].astype(jnp.float32) * row_factor
    key_width = KVH * HD
    turned = []
    for head in range(KVH):
        part = weighted[:, head * HD : (head + 1) * HD]
        turned.append(part * cosines - pltpu.roll(part, HD // 2, 1) * sines)
    keys = jnp.concatenate(turned, axis=1).astype(jnp.bfloat16)
    values = weighted[:, key_width:].astype(jnp.bfloat16)
    keep = jnp.where(core == 0, keys, values)
    give = jnp.where(core == 0, values, keys)
    chunk = 256
    for start in range(0, width, chunk):
        block = normed_ref[:, start : start + chunk]
        dims = (((0,), (0,)), ((), ()))
        own_ref[start : start + chunk, :] = lax.dot_general(
            block, keep, dims, preferred_element_type=jnp.float32
        )
        given_ref[start : start + chunk, :] = lax.dot_general(
            block, give, dims, preferred_element_type=jnp.float32
        ).astype(jnp.bfloat16)


def pair_kernel(own_ref, taken_ref, kept_ref, given_ref):
    piece = kept_ref.shape[1]
    outer = lax.axis_index("outer")
    mine = pl.ds(pl.multiple_of(outer * piece, piece), piece)
    other = pl.ds(pl.multiple_of((1 - outer) * piece, piece), piece)
    kept_ref[...] = own_ref[:, mine] + taken_ref[:, mine].astype(jnp.float32)
    given_ref[...] = (
        own_ref[:, other] + taken_ref[:, other].astype(jnp.float32)
    ).astype(jnp.bfloat16)


def spread_kernel(kept_ref, taken_ref, first_ref, *part_refs):
    rows = first_ref.shape[0]
    member = lax.axis_index("fsdp")
    for shift, part_ref in enumerate((first_ref,) + part_refs):
        at = pl.ds(pl.multiple_of(jnp.bitwise_xor(member, shift) * rows, rows), rows)
        total = kept_ref[at, :] + taken_ref[at, :].astype(jnp.float32)
        part_ref[...] = total.astype(part_ref.dtype)


def gather_kernel(*refs):
    out_ref = refs[-1]
    rows = refs[0].shape[0]
    member = lax.axis_index("fsdp")
    for shift, part_ref in enumerate(refs[:-1]):
        at = pl.ds(pl.multiple_of(jnp.bitwise_xor(member, shift) * rows, rows), rows)
        out_ref[at, :] = part_ref[...]


def sum_kernel(*refs):
    total = refs[0][...]
    for part_ref in refs[1:-1]:
        total = total + part_ref[...].astype(jnp.float32)
    refs[-1][...] = total


def finish_kernel(outer, counts_ref, gain_ref, weight_ref, *refs):
    weight_grad_ref, gain_grad_ref = refs[-2:]
    parts = refs[:-2]
    piece = parts[0].shape[1]
    domain = lax.axis_index("outer") * 2 + lax.axis_index("core")
    live_total = full_sum(counts_ref[...].astype(jnp.float32)) * float(BLOCK)
    scale = 1.0 / jnp.sqrt(live_total)
    gains = to_column(gain_ref[...].astype(jnp.float32)) * scale
    dots = jnp.zeros((parts[0].shape[0], 1), jnp.float32)
    for shift, part_ref in enumerate(parts):
        source = jnp.bitwise_xor(domain, shift)
        block = lax.rem(source, 2) * outer + lax.div(source, 2)
        at = pl.ds(pl.multiple_of(block * piece, piece), piece)
        part = part_ref[...]
        weight_grad_ref[:, at] = part * gains
        dots = dots + jnp.sum(
            part * weight_ref[:, at].astype(jnp.float32), axis=1, keepdims=True
        )
    gain_grad_ref[...] = dots * scale


def forward_kernel(normed_ref, own_ref, other_ref, cosines_ref, sines_ref, out_ref):
    core = lax.axis_index("core")
    normed = normed_ref[...]
    own = jnp.dot(normed, own_ref[...], preferred_element_type=jnp.float32)
    other = jnp.dot(normed, other_ref[...], preferred_element_type=jnp.float32)
    keys = jnp.where(core == 0, own, other)
    values = jnp.where(core == 0, other, own)
    cosines, sines = cosines_ref[...], sines_ref[...]
    for head in range(KVH):
        part = keys[:, head * HD : (head + 1) * HD]
        out_ref[:, head * HD : (head + 1) * HD] = (
            part * cosines + pltpu.roll(part, HD // 2, 1) * sines
        ).astype(jnp.bfloat16)
    out_ref[:, KVH * HD :] = values.astype(jnp.bfloat16)


def exchange(value, axes, count, shift):
    return lax.ppermute(value, axes, [(i, i ^ shift) for i in range(count)])


def body(outer, members, tokens, gain, kv_weight, positions, cotangent, counts, ratios):
    domains = 2 * outer
    rows, width = tokens.shape
    shard, columns = kv_weight.shape
    half = columns // 2
    piece = half // outer
    f32, bf16 = jnp.float32, jnp.bfloat16
    shape = jax.ShapeDtypeStruct
    gain_line = gain.reshape(1, shard)
    member = lax.axis_index("fsdp")

    folded = call(fold_kernel, shape((shard, half), bf16), (kv_weight, gain_line))
    weight_parts = [folded]
    for shift in range(1, members):
        weight_parts.append(exchange(folded, "fsdp", members, shift))

    exponents = np.arange(HD, dtype=np.float64) % (HD // 2) * (2.0 / HD)
    frequency = jnp.asarray(np.power(1000000.0, -exponents).astype(np.float32))
    normed, cosines, sines, own, given = call(
        backward_kernel,
        (
            shape((rows, width), bf16),
            shape((rows, HD), f32),
            shape((rows, HD), f32),
            shape((width, half), f32),
            shape((width, half), bf16),
        ),
        (
            tokens,
            positions.reshape(rows // 128, 128),
            frequency.reshape(1, HD),
            cotangent,
            counts,
            ratios.reshape(1, domains),
        ),
        flops=2 * rows * width * columns,
        bytes_accessed=8000000,
    )
    taken = exchange(given, "core", 2, 1)
    if outer == 2:
        kept, given = call(
            pair_kernel, (shape((width, piece), f32), shape((width, piece), bf16)), (own, taken)
        )
        taken = exchange(given, "outer", 2, 1)
    else:
        pair = (own + taken.astype(f32)).reshape(width, outer, piece)
        kept = lax.psum_scatter(pair, "outer", scatter_dimension=1)
        taken = jnp.zeros((width, piece), bf16)
    parts = call(
        spread_kernel,
        (shape((shard, piece), f32),) + (shape((shard, piece), bf16),) * (members - 1),
        (kept, taken),
    )
    arrived = [parts[0]]
    for shift in range(1, members):
        arrived.append(exchange(parts[shift], "fsdp", members, shift))
    mine = call(sum_kernel, shape((shard, piece), f32), tuple(arrived))
    pieces = [mine]
    for shift in range(1, domains):
        pieces.append(exchange(mine, ("outer", "core"), domains, shift))
    if piece % 128 == 0:
        weight_grad, gain_grad = call(
            functools.partial(finish_kernel, outer),
            (shape((shard, columns), f32), shape((shard, 1), f32)),
            (counts, gain_line, kv_weight) + tuple(pieces),
        )
        gain_grad = gain_grad.reshape(shard)
    else:
        domain = lax.axis_index("outer") * 2 + lax.axis_index("core")
        order = jnp.arange(domains)
        order = (order % outer) * 2 + order // outer
        total = jnp.stack(pieces)[order ^ domain].transpose(1, 0, 2).reshape(shard, columns)
        scale = 1.0 / jnp.sqrt((BLOCK * jnp.sum(counts)).astype(f32))
        weight_grad = total * (gain.astype(f32)[:, None] * scale)
        gain_grad = jnp.sum(total * kv_weight.astype(f32), axis=1) * scale

    if shard % 16 == 0:
        own_half = call(gather_kernel, shape((width, half), bf16), tuple(weight_parts))
    else:
        own_half = jnp.stack(weight_parts)[jnp.arange(members) ^ member].reshape(width, half)
    other_half = exchange(own_half, "core", 2, 1)
    keys_out = call(
        forward_kernel,
        shape((rows, columns), bf16),
        (normed, own_half, other_half, cosines, sines),
        flops=2 * rows * width * columns,
        bytes_accessed=3000000,
    )
    return (keys_out, weight_grad, gain_grad)


def solution(mesh):
    domains, members = mesh.shape["dom"], mesh.shape["fsdp"]
    outer = domains // 2
    split = Mesh(mesh.devices.reshape(outer, 2, members), EVERY)
    return jax.shard_map(
        functools.partial(body, outer, members),
        mesh=split,
        in_specs=(
            P(EVERY, None),
            P("fsdp"),
            P("fsdp", None),
            P(EVERY),
            P(EVERY, None),
            P(),
            P(),
        ),
        out_specs=(P(EVERY, None), P("fsdp", None), P("fsdp")),
        check_vma=False,
    )
```

```python
import functools

import jax
import jax.numpy as jnp
import numpy as np
from jax import lax
from jax.experimental import pallas as pl
from jax.experimental.pallas import tpu as pltpu
from jax.sharding import Mesh
from jax.sharding import PartitionSpec as P

KVH = 2
HD = 128
BLOCK = 128
EVERY = ("outer", "core", "fsdp")
VMEM_BYTES = 32 * 1024 * 1024
WIDE_BYTES = 56 * 1024 * 1024


def to_column(line):
    n = line.shape[1]
    rows = lax.broadcasted_iota(jnp.int32, (n, n), 0)
    lanes = lax.broadcasted_iota(jnp.int32, (n, n), 1)
    spread = jnp.broadcast_to(line, (n, n))
    return jnp.sum(jnp.where(rows == lanes, spread, 0.0), axis=1, keepdims=True)


def to_line(column):
    n = column.shape[0]
    rows = lax.broadcasted_iota(jnp.int32, (n, n), 0)
    lanes = lax.broadcasted_iota(jnp.int32, (n, n), 1)
    spread = jnp.broadcast_to(column, (n, n))
    return jnp.sum(jnp.where(rows == lanes, spread, 0.0), axis=0, keepdims=True)


def full_sum(values):
    return jnp.sum(jnp.sum(values, axis=1, keepdims=True), axis=0, keepdims=True)


def fetch(sources, buffers, semaphores):
    copies = []
    for i, (source, buffer) in enumerate(zip(sources, buffers)):
        copy = pltpu.make_async_copy(source, buffer, semaphores.at[i])
        copy.start()
        copies.append(copy)
    return copies


def call(kernel, out_shape, args, fetched=0, flops=0, bytes_accessed=1000000):
    spaces = [pl.ANY] * fetched + [pltpu.VMEM] * (len(args) - fetched)
    scratch = [pltpu.VMEM(arg.shape, arg.dtype) for arg in args[:fetched]]
    if fetched:
        scratch.append(pltpu.SemaphoreType.DMA((fetched,)))
    return pl.pallas_call(
        kernel,
        out_shape=out_shape,
        in_specs=[pl.BlockSpec(memory_space=space) for space in spaces],
        scratch_shapes=scratch,
        out_specs=jax.tree.map(lambda _: pl.BlockSpec(memory_space=pltpu.VMEM), out_shape),
        compiler_params=pltpu.CompilerParams(vmem_limit_bytes=WIDE_BYTES if fetched else VMEM_BYTES),
        cost_estimate=pl.CostEstimate(
            flops=flops, bytes_accessed=bytes_accessed, transcendentals=0
        ),
    )(*args)


def fold_kernel(weight_hbm, gain_hbm, parts_ref, weight_ref, gain_ref, semaphores):
    members, _, half = parts_ref.shape
    copies = fetch((weight_hbm, gain_hbm), (weight_ref, gain_ref), semaphores)
    core = lax.axis_index("core")
    columns = pl.ds(pl.multiple_of(core * half, half), half)
    copies[1].wait()
    gains = to_column(gain_ref[...].astype(jnp.float32).reshape(1, -1))
    copies[0].wait()
    folded = (weight_ref[:, columns].astype(jnp.float32) * gains).astype(jnp.bfloat16)
    for i in range(members):
        parts_ref[i, :, :] = folded


def backward_kernel(
    tokens_hbm, positions_hbm, frequency_hbm, cotangent_hbm, counts_hbm, ratios_hbm,
    normed_ref, cosines_ref, sines_ref, own_ref, given_ref,
    tokens_ref, positions_ref, frequency_ref, cotangent_ref, counts_ref, ratios_ref,
    semaphores,
):
    copies = fetch(
        (tokens_hbm, positions_hbm, frequency_hbm, cotangent_hbm, counts_hbm, ratios_hbm),
        (tokens_ref, positions_ref, frequency_ref, cotangent_ref, counts_ref, ratios_ref),
        semaphores,
    )
    for copy in copies:
        copy.wait()
    rows, width = tokens_ref.shape
    core = lax.axis_index("core")
    domain = lax.axis_index("outer") * 2 + core
    member = lax.axis_index("fsdp")

    step = 32
    for start in range(0, rows, step):
        block = tokens_ref[start : start + step, :].astype(jnp.float32)
        mean_square = jnp.sum(block * block, axis=1, keepdims=True) * (1.0 / width)
        normed_ref[start : start + step, :] = (
            block * lax.rsqrt(mean_square + 1e-06)
        ).astype(jnp.bfloat16)

    lines = positions_ref[...].astype(jnp.float32)
    place = jnp.concatenate(
        [to_column(lines[i : i + 1, :]) for i in range(lines.shape[0])], axis=0
    )
    angles = place * frequency_ref[...]
    cosines = jnp.cos(angles)
    lanes = lax.broadcasted_iota(jnp.int32, (rows, HD), 1)
    sines = jnp.sin(angles)
    sines = jnp.where(lanes < HD // 2, -sines, sines)
    cosines_ref[...] = cosines
    sines_ref[...] = sines

    counts = counts_ref[...].astype(jnp.float32)
    ratios = ratios_ref[...].astype(jnp.float32)
    at_domain = lax.broadcasted_iota(jnp.int32, counts.shape, 0) == domain
    at_member = lax.broadcasted_iota(jnp.int32, counts.shape, 1) == member
    ratio_at = lax.broadcasted_iota(jnp.int32, ratios.shape, 1) == domain
    live_total = full_sum(counts) * float(BLOCK)
    own_rows = full_sum(jnp.where(at_domain, counts, 0.0)) * float(BLOCK)
    own_live = full_sum(jnp.where(at_domain & at_member, counts, 0.0)) * float(BLOCK)
    own_ratio = full_sum(jnp.where(ratio_at, ratios, 0.0))
    factor = own_ratio / full_sum(ratios) * live_total / own_rows
    row_ids = lax.broadcasted_iota(jnp.int32, (rows, 1), 0).astype(jnp.float32)
    row_factor = jnp.where(row_ids < own_live, factor, 0.0)

    weighted = cotangent_ref[...].astype(jnp.float32) * row_factor
    key_width = KVH * HD
    turned = []
    for head in range(KVH):
        part = weighted[:, head * HD : (head + 1) * HD]
        turned.append(part * cosines - pltpu.roll(part, HD // 2, 1) * sines)
    keys = jnp.concatenate(turned, axis=1).astype(jnp.bfloat16)
    values = weighted[:, key_width:].astype(jnp.bfloat16)
    keep = jnp.where(core == 0, keys, values)
    give = jnp.where(core == 0, values, keys)
    chunk = 256
    for start in range(0, width, chunk):
        block = normed_ref[:, start : start + chunk]
        dims = (((0,), (0,)), ((), ()))
        own_ref[start : start + chunk, :] = lax.dot_general(
            block, keep, dims, preferred_element_type=jnp.float32
        )
        given_ref[start : start + chunk, :] = lax.dot_general(
            block, give, dims, preferred_element_type=jnp.float32
        ).astype(jnp.bfloat16)


def pair_kernel(own_ref, taken_ref, kept_ref, given_ref):
    piece = kept_ref.shape[1]
    outer = lax.axis_index("outer")
    mine = pl.ds(pl.multiple_of(outer * piece, piece), piece)
    other = pl.ds(pl.multiple_of((1 - outer) * piece, piece), piece)
    kept_ref[...] = own_ref[:, mine] + taken_ref[:, mine].astype(jnp.float32)
    given_ref[...] = (
        own_ref[:, other] + taken_ref[:, other].astype(jnp.float32)
    ).astype(jnp.bfloat16)


def spread_kernel(kept_ref, taken_ref, parts_ref):
    total = kept_ref[...] + taken_ref[...].astype(jnp.float32)
    parts_ref[...] = total.astype(jnp.bfloat16).reshape(parts_ref.shape)


def sum_kernel(parts_ref, out_ref):
    total = parts_ref[0].astype(jnp.float32)
    for i in range(1, parts_ref.shape[0]):
        total = total + parts_ref[i].astype(jnp.float32)
    out_ref[...] = total


def finish_kernel(outer, counts_ref, gain_ref, weight_ref, *refs):
    parts, (weight_grad_ref, gain_grad_ref) = refs[:-2], refs[-2:]
    rows, piece = parts[0].shape
    domain = lax.axis_index("outer") * 2 + lax.axis_index("core")
    live_total = full_sum(counts_ref[...].astype(jnp.float32)) * float(BLOCK)
    scale = 1.0 / jnp.sqrt(live_total)
    gains = to_column(gain_ref[...].astype(jnp.float32).reshape(1, -1)) * scale
    dots = jnp.zeros((rows, 1), jnp.float32)
    for shift, part_ref in enumerate(parts):
        source = jnp.bitwise_xor(domain, shift)
        block = lax.rem(source, 2) * outer + lax.div(source, 2)
        at = pl.ds(pl.multiple_of(block * piece, piece), piece)
        part = part_ref[...]
        weight_grad_ref[:, at] = part * gains
        dots = dots + jnp.sum(
            part * weight_ref[:, at].astype(jnp.float32), axis=1, keepdims=True
        )
    gain_grad_ref[...] = to_line(dots * scale).reshape(rows)


def forward_kernel(normed_ref, own_ref, other_ref, cosines_ref, sines_ref, out_ref):
    core = lax.axis_index("core")
    normed = normed_ref[...]
    own = jnp.dot(normed, own_ref[...], preferred_element_type=jnp.float32)
    other = jnp.dot(normed, other_ref[...], preferred_element_type=jnp.float32)
    keys = jnp.where(core == 0, own, other)
    values = jnp.where(core == 0, other, own)
    cosines, sines = cosines_ref[...], sines_ref[...]
    for head in range(KVH):
        part = keys[:, head * HD : (head + 1) * HD]
        out_ref[:, head * HD : (head + 1) * HD] = (
            part * cosines + pltpu.roll(part, HD // 2, 1) * sines
        ).astype(jnp.bfloat16)
    out_ref[:, KVH * HD :] = values.astype(jnp.bfloat16)


def exchange(value, axes, count, shift):
    return lax.ppermute(value, axes, [(i, i ^ shift) for i in range(count)])


def body(outer, members, tokens, gain, kv_weight, positions, cotangent, counts, ratios):
    domains = 2 * outer
    rows, width = tokens.shape
    shard, columns = kv_weight.shape
    half = columns // 2
    piece = half // outer
    f32, bf16 = jnp.float32, jnp.bfloat16
    shape = jax.ShapeDtypeStruct
    weight_parts = call(
        fold_kernel, shape((members, shard, half), bf16), (kv_weight, gain), fetched=2
    )
    own_half = lax.all_to_all(weight_parts, "fsdp", 0, 0, tiled=True).reshape(width, half)
    other_half = exchange(own_half, "core", 2, 1)

    exponents = np.arange(HD, dtype=np.float64) % (HD // 2) * (2.0 / HD)
    frequency = jnp.asarray(np.power(1000000.0, -exponents).astype(np.float32))
    normed, cosines, sines, own, given = call(
        backward_kernel,
        (
            shape((rows, width), bf16),
            shape((rows, HD), f32),
            shape((rows, HD), f32),
            shape((width, half), f32),
            shape((width, half), bf16),
        ),
        (
            tokens,
            positions.reshape(rows // 128, 128),
            frequency.reshape(1, HD),
            cotangent,
            counts,
            ratios.reshape(1, domains),
        ),
        fetched=6,
        flops=2 * rows * width * columns,
        bytes_accessed=8000000,
    )
    taken = exchange(given, "core", 2, 1)
    if outer == 2:
        kept, given = call(
            pair_kernel, (shape((width, piece), f32), shape((width, piece), bf16)), (own, taken)
        )
        taken = exchange(given, "outer", 2, 1)
    else:
        pair = (own + taken.astype(f32)).reshape(width, outer, piece)
        kept = lax.psum_scatter(pair, "outer", scatter_dimension=1)
        taken = jnp.zeros((width, piece), bf16)
    parts = call(spread_kernel, shape((members, shard, piece), bf16), (kept, taken))
    parts = lax.all_to_all(parts, "fsdp", 0, 0, tiled=True)
    mine = call(sum_kernel, shape((shard, piece), f32), (parts,))
    if outer == 2:
        beside = exchange(mine, "core", 2, 1)
        across = exchange(mine, "outer", 2, 1)
        pieces = [mine, beside, across, exchange(across, "core", 2, 1)]
    else:
        pieces = [mine]
        for shift in range(1, domains):
            pieces.append(exchange(mine, ("outer", "core"), domains, shift))
    if piece % 128 == 0:
        weight_grad, gain_grad = call(
            functools.partial(finish_kernel, outer),
            (shape((shard, columns), f32), shape((shard,), f32)),
            (counts, gain, kv_weight) + tuple(pieces),
        )
    else:
        domain = lax.axis_index("outer") * 2 + lax.axis_index("core")
        order = jnp.arange(domains)
        order = (order % outer) * 2 + order // outer
        total = jnp.stack(pieces)[order ^ domain].transpose(1, 0, 2).reshape(shard, columns)
        scale = 1.0 / jnp.sqrt((BLOCK * jnp.sum(counts)).astype(f32))
        weight_grad = total * (gain.astype(f32)[:, None] * scale)
        gain_grad = jnp.sum(total * kv_weight.astype(f32), axis=1) * scale

    keys_out = call(
        forward_kernel,
        shape((rows, columns), bf16),
        (normed, own_half, other_half, cosines, sines),
        flops=2 * rows * width * columns,
        bytes_accessed=3000000,
    )
    return (keys_out, weight_grad, gain_grad)


def solution(mesh):
    domains, members = mesh.shape["dom"], mesh.shape["fsdp"]
    outer = domains // 2
    split = Mesh(mesh.devices.reshape(outer, 2, members), EVERY)
    return jax.shard_map(
        functools.partial(body, outer, members),
        mesh=split,
        in_specs=(
            P(EVERY, None),
            P("fsdp"),
            P("fsdp", None),
            P(EVERY),
            P(EVERY, None),
            P(),
            P(),
        ),
        out_specs=(P(EVERY, None), P("fsdp", None), P("fsdp")),
        check_vma=False,
    )
```

```python
import functools

import jax
import jax.numpy as jnp
import numpy as np
from jax import lax
from jax.experimental import pallas as pl
from jax.experimental.pallas import tpu as pltpu
from jax.sharding import Mesh
from jax.sharding import PartitionSpec as P

KVH = 2
HD = 128
BLOCK = 128
CHUNK = 256
EVERY = ("outer", "core", "fsdp")
VMEM_BYTES = 32 * 1024 * 1024
WIDE_BYTES = 56 * 1024 * 1024


def to_column(line):
    n = line.shape[1]
    rows = lax.broadcasted_iota(jnp.int32, (n, n), 0)
    lanes = lax.broadcasted_iota(jnp.int32, (n, n), 1)
    spread = jnp.broadcast_to(line, (n, n))
    return jnp.sum(jnp.where(rows == lanes, spread, 0.0), axis=1, keepdims=True)


def to_line(column):
    n = column.shape[0]
    rows = lax.broadcasted_iota(jnp.int32, (n, n), 0)
    lanes = lax.broadcasted_iota(jnp.int32, (n, n), 1)
    spread = jnp.broadcast_to(column, (n, n))
    return jnp.sum(jnp.where(rows == lanes, spread, 0.0), axis=0, keepdims=True)


def transposed_dot(left, right):
    return lax.dot_general(
        left, right, (((0,), (0,)), ((), ())), preferred_element_type=jnp.float32
    )


def full_sum(values):
    return jnp.sum(jnp.sum(values, axis=1, keepdims=True), axis=0, keepdims=True)


def fetch(sources, buffers, semaphores):
    copies = []
    for i, (source, buffer) in enumerate(zip(sources, buffers)):
        copy = pltpu.make_async_copy(source, buffer, semaphores.at[i])
        copy.start()
        copies.append(copy)
    return copies


def call(kernel, out_shape, args, after=None, fetched=0, sent=0, flops=0, bytes_accessed=1000000):
    count = len(args)
    spaces = [pl.ANY] * fetched + [pltpu.VMEM] * (count - fetched)
    run = kernel
    if after is not None:
        args, spaces = tuple(args) + (after,), spaces + [pl.ANY]

        def run(*refs):
            kernel(*refs[:count], *refs[count + 1 :])

    out_space = pltpu.VMEM
    if sent:
        out_space = pl.ANY
        scratch_out = [pltpu.VMEM(out.shape, out.dtype) for out in out_shape]
        scratch_out.append(pltpu.SemaphoreType.DMA((sent,)))
    else:
        scratch_out = []
    scratch = [pltpu.VMEM(arg.shape, arg.dtype) for arg in args[:fetched]]
    if fetched:
        scratch.append(pltpu.SemaphoreType.DMA((fetched,)))
    return pl.pallas_call(
        run,
        out_shape=out_shape,
        in_specs=[pl.BlockSpec(memory_space=space) for space in spaces],
        scratch_shapes=scratch + scratch_out,
        out_specs=jax.tree.map(lambda _: pl.BlockSpec(memory_space=out_space), out_shape),
        compiler_params=pltpu.CompilerParams(
            vmem_limit_bytes=WIDE_BYTES if fetched else VMEM_BYTES
        ),
        cost_estimate=pl.CostEstimate(
            flops=flops, bytes_accessed=bytes_accessed, transcendentals=0
        ),
    )(*args)


def fold_kernel(weight_ref, gain_ref, half_ref):
    half = half_ref.shape[1]
    core = lax.axis_index("core")
    columns = pl.ds(pl.multiple_of(core * half, half), half)
    gains = to_column(gain_ref[...].astype(jnp.float32).reshape(1, -1))
    half_ref[...] = (weight_ref[:, columns].astype(jnp.float32) * gains).astype(jnp.bfloat16)


def join_kernel(first_ref, second_ref, out_ref):
    count = first_ref.shape[0]
    out_ref[:count] = first_ref[...]
    out_ref[count:] = second_ref[...]


def order_kernel(order, first_ref, second_ref, out_ref):
    count, rows, _ = first_ref.shape
    member = lax.axis_index("fsdp")
    for i, shift in enumerate(order):
        at = pl.ds(pl.multiple_of(jnp.bitwise_xor(member, shift) * rows, rows), rows)
        out_ref[at, :] = first_ref[i] if i < count else second_ref[i - count]


def backward_kernel(
    tokens_hbm, positions_hbm, frequency_hbm, cotangent_hbm, counts_hbm, ratios_hbm,
    normed_out, cosines_out, sines_out, keep_out, given_out,
    tokens_ref, positions_ref, frequency_ref, cotangent_ref, counts_ref, ratios_ref,
    semaphores,
    normed_ref, cosines_ref, sines_ref, keep_ref, given_ref, sent_semaphores,
):
    sent = []

    def send(source, target):
        copy = pltpu.make_async_copy(source, target, sent_semaphores.at[len(sent)])
        copy.start()
        sent.append(copy)

    copies = fetch(
        (tokens_hbm, positions_hbm, frequency_hbm, cotangent_hbm, counts_hbm, ratios_hbm),
        (tokens_ref, positions_ref, frequency_ref, cotangent_ref, counts_ref, ratios_ref),
        semaphores,
    )
    for copy in copies:
        copy.wait()
    rows, width = tokens_ref.shape
    core = lax.axis_index("core")
    domain = lax.axis_index("outer") * 2 + core
    member = lax.axis_index("fsdp")

    step = 32
    for start in range(0, rows, step):
        block = tokens_ref[start : start + step, :].astype(jnp.float32)
        mean_square = jnp.sum(block * block, axis=1, keepdims=True) * (1.0 / width)
        normed_ref[start : start + step, :] = (
            block * lax.rsqrt(mean_square + 1e-06)
        ).astype(jnp.bfloat16)
    send(normed_ref, normed_out)

    lines = positions_ref[...].astype(jnp.float32)
    place = jnp.concatenate(
        [to_column(lines[i : i + 1, :]) for i in range(lines.shape[0])], axis=0
    )
    angles = place * frequency_ref[...]
    cosines = jnp.cos(angles)
    lanes = lax.broadcasted_iota(jnp.int32, (rows, HD), 1)
    sines = jnp.sin(angles)
    sines = jnp.where(lanes < HD // 2, -sines, sines)
    cosines_ref[...] = cosines
    sines_ref[...] = sines
    send(cosines_ref, cosines_out)
    send(sines_ref, sines_out)

    counts = counts_ref[...].astype(jnp.float32)
    ratios = ratios_ref[...].astype(jnp.float32)
    at_domain = lax.broadcasted_iota(jnp.int32, counts.shape, 0) == domain
    at_member = lax.broadcasted_iota(jnp.int32, counts.shape, 1) == member
    ratio_at = lax.broadcasted_iota(jnp.int32, ratios.shape, 1) == domain
    live_total = full_sum(counts) * float(BLOCK)
    own_rows = full_sum(jnp.where(at_domain, counts, 0.0)) * float(BLOCK)
    own_live = full_sum(jnp.where(at_domain & at_member, counts, 0.0)) * float(BLOCK)
    own_ratio = full_sum(jnp.where(ratio_at, ratios, 0.0))
    factor = own_ratio / full_sum(ratios) * live_total / own_rows
    row_ids = lax.broadcasted_iota(jnp.int32, (rows, 1), 0).astype(jnp.float32)
    row_factor = jnp.where(row_ids < own_live, factor, 0.0)

    weighted = cotangent_ref[...].astype(jnp.float32) * row_factor
    key_width = KVH * HD
    turned = []
    for head in range(KVH):
        part = weighted[:, head * HD : (head + 1) * HD]
        turned.append(part * cosines - pltpu.roll(part, HD // 2, 1) * sines)
    keys = jnp.concatenate(turned, axis=1).astype(jnp.bfloat16)
    values = weighted[:, key_width:].astype(jnp.bfloat16)
    keep_ref[...] = jnp.where(core == 0, keys, values)
    send(keep_ref, keep_out)
    give = jnp.where(core == 0, values, keys)
    for start in range(0, width, CHUNK):
        at = slice(start, start + CHUNK)
        given_ref[at, :] = transposed_dot(normed_ref[:, at], give).astype(jnp.bfloat16)
        send(given_ref.at[at, :], given_out.at[at, :])
    for copy in sent:
        copy.wait()


def own_kernel(normed_ref, keep_ref, own_ref):
    for start in range(0, own_ref.shape[0], CHUNK):
        at = slice(start, start + CHUNK)
        own_ref[at, :] = transposed_dot(normed_ref[:, at], keep_ref[...])


def aligned(index, size):
    return pl.ds(pl.multiple_of(index * size, size), size)


def total(kept, taken):
    return kept + taken.astype(jnp.float32)


def pair_kernel(own_ref, taken_ref, kept_y_ref, given_y_ref, kept_x_ref, given_x_ref):
    members, rows, columns = kept_y_ref.shape
    left, right = slice(0, columns), slice(columns, 2 * columns)
    y, x = lax.axis_index("outer"), lax.axis_index("fsdp") % 2
    for i in range(members):
        at = aligned(2 * i + y, rows)
        kept_y_ref[i] = total(own_ref[at, left], taken_ref[at, left])
        at = aligned(2 * i + 1 - y, rows)
        given_y_ref[i] = total(own_ref[at, left], taken_ref[at, left]).astype(jnp.bfloat16)
    for i in range(members // 2):
        at = aligned(2 * i + x, 2 * rows)
        kept_x_ref[i] = total(own_ref[at, right], taken_ref[at, right])
        at = aligned(2 * i + 1 - x, 2 * rows)
        given_x_ref[i] = total(own_ref[at, right], taken_ref[at, right]).astype(jnp.bfloat16)


def cross_kernel(
    kept_y_ref, taken_y_ref, kept_x_ref, taken_x_ref,
    next_x_ref, given_x_ref, next_y_ref, given_y_ref,
):
    count, rows, _ = next_x_ref.shape
    y, x = lax.axis_index("outer"), lax.axis_index("fsdp") % 2
    for i in range(count):
        at = 2 * i + x
        next_x_ref[i] = total(kept_y_ref[at], taken_y_ref[at])
        at = 2 * i + 1 - x
        given_x_ref[i] = total(kept_y_ref[at], taken_y_ref[at]).astype(jnp.bfloat16)
        at = aligned(y, rows)
        next_y_ref[i] = total(kept_x_ref[i, at, :], taken_x_ref[i, at, :])
        at = aligned(1 - y, rows)
        given_y_ref[i] = total(kept_x_ref[i, at, :], taken_x_ref[i, at, :]).astype(jnp.bfloat16)


def near_kernel(kept_x_ref, taken_x_ref, kept_y_ref, taken_y_ref, next_ref, given_ref):
    columns = kept_x_ref.shape[2]
    left, right = slice(0, columns), slice(columns, 2 * columns)
    low = lax.axis_index("fsdp") // 2 % 2
    for i in range(next_ref.shape[0]):
        at = 2 * i + low
        next_ref[i, :, left] = total(kept_x_ref[at], taken_x_ref[at])
        next_ref[i, :, right] = total(kept_y_ref[at], taken_y_ref[at])
        at = 2 * i + 1 - low
        given_ref[i, :, left] = total(kept_x_ref[at], taken_x_ref[at]).astype(jnp.bfloat16)
        given_ref[i, :, right] = total(kept_y_ref[at], taken_y_ref[at]).astype(jnp.bfloat16)


def far_kernel(kept_ref, taken_ref, next_ref, given_ref):
    high = lax.axis_index("fsdp") // 4
    next_ref[...] = total(kept_ref[high], taken_ref[high])
    given_ref[...] = total(kept_ref[1 - high], taken_ref[1 - high]).astype(jnp.bfloat16)


def last_kernel(kept_ref, taken_ref, out_ref):
    out_ref[...] = total(kept_ref[...], taken_ref[...]).astype(jnp.bfloat16)


def rows_kernel(mine_ref, across_ref, out_ref):
    rows = mine_ref.shape[0]
    y = lax.axis_index("outer")
    out_ref[aligned(y, rows), :] = mine_ref[...]
    out_ref[aligned(1 - y, rows), :] = across_ref[...]


def finish_kernel(
    counts_ref, gain_ref, weight_ref, own_ref, other_ref, weight_grad_ref, gain_grad_ref
):
    rows, half = own_ref.shape
    core = lax.axis_index("core")
    live_total = full_sum(counts_ref[...].astype(jnp.float32)) * float(BLOCK)
    scale = 1.0 / jnp.sqrt(live_total)
    gains = to_column(gain_ref[...].astype(jnp.float32).reshape(1, -1)) * scale
    own, other = own_ref[...].astype(jnp.float32), other_ref[...].astype(jnp.float32)
    dots = jnp.zeros((rows, 1), jnp.float32)
    for side in range(2):
        at = slice(side * half, (side + 1) * half)
        part = jnp.where(core == side, own, other)
        weight_grad_ref[:, at] = part * gains
        weight = weight_ref[:, at].astype(jnp.float32)
        dots = dots + jnp.sum(part * weight, axis=1, keepdims=True)
    gain_grad_ref[...] = to_line(dots * scale).reshape(rows)


def forward_kernel(normed_ref, own_ref, other_ref, cosines_ref, sines_ref, out_ref):
    core = lax.axis_index("core")
    normed = normed_ref[...]
    own = jnp.dot(normed, own_ref[...], preferred_element_type=jnp.float32)
    other = jnp.dot(normed, other_ref[...], preferred_element_type=jnp.float32)
    keys = jnp.where(core == 0, own, other)
    values = jnp.where(core == 0, other, own)
    cosines, sines = cosines_ref[...], sines_ref[...]
    for head in range(KVH):
        part = keys[:, head * HD : (head + 1) * HD]
        out_ref[:, head * HD : (head + 1) * HD] = (
            part * cosines + pltpu.roll(part, HD // 2, 1) * sines
        ).astype(jnp.bfloat16)
    out_ref[:, KVH * HD :] = values.astype(jnp.bfloat16)


def exchange(value, axes, count, shift):
    return lax.ppermute(value, axes, [(i, i ^ shift) for i in range(count)])


def sum_on_cube(own, taken, shard):
    width, half = own.shape
    f32, bf16 = jnp.float32, jnp.bfloat16
    shape = jax.ShapeDtypeStruct
    rows, columns = shard // 2, half // 2

    def both(*dims):
        return (shape(dims, f32), shape(dims, bf16))

    kept_y, given_y, kept_x, given_x = call(
        pair_kernel, both(8, rows, columns) + both(4, shard, columns), (own, taken)
    )
    taken_y = exchange(given_y, "outer", 2, 1)
    taken_x = exchange(given_x, "fsdp", 8, 1)
    kept_x, given_x, kept_y, given_y = call(
        cross_kernel,
        both(4, rows, columns) + both(4, rows, columns),
        (kept_y, taken_y, kept_x, taken_x),
    )
    cross_done = kept_x
    taken_x = exchange(given_x, "fsdp", 8, 1)
    taken_y = exchange(given_y, "outer", 2, 1)
    kept, given = call(near_kernel, both(2, rows, half), (kept_x, taken_x, kept_y, taken_y))
    near_done = kept
    taken = exchange(given, "fsdp", 8, 2)
    kept, given = call(far_kernel, both(rows, half), (kept, taken))
    taken = exchange(given, "fsdp", 8, 4)
    mine = call(last_kernel, shape((rows, half), bf16), (kept, taken))
    across = exchange(mine, "outer", 2, 1)
    own_sum = call(rows_kernel, shape((shard, half), bf16), (mine, across))
    return own_sum, (cross_done, near_done, mine)


def gather_on_cube(folded, steps):
    shard, half = folded.shape
    parts, order = folded.reshape(1, shard, half), [0]
    for shift, after in zip((4, 2), steps):
        came = exchange(parts, "fsdp", 8, shift)
        order = order + [shift ^ i for i in order]
        out = jax.ShapeDtypeStruct((len(order), shard, half), folded.dtype)
        parts = call(join_kernel, out, (parts, came), after=after)
    came = exchange(parts, "fsdp", 8, 1)
    order = order + [1 ^ i for i in order]
    out = jax.ShapeDtypeStruct((8 * shard, half), folded.dtype)
    return call(functools.partial(order_kernel, order), out, (parts, came), after=steps[2])


def body(outer, members, tokens, gain, kv_weight, positions, cotangent, counts, ratios):
    domains = 2 * outer
    rows, width = tokens.shape
    shard, columns = kv_weight.shape
    half = columns // 2
    f32, bf16 = jnp.float32, jnp.bfloat16
    shape = jax.ShapeDtypeStruct
    on_cube = outer == 2 and members == 8 and shard % 32 == 0

    exponents = np.arange(HD, dtype=np.float64) % (HD // 2) * (2.0 / HD)
    frequency = jnp.asarray(np.power(1000000.0, -exponents).astype(np.float32))
    normed, cosines, sines, keep, given = call(
        backward_kernel,
        (
            shape((rows, width), bf16),
            shape((rows, HD), f32),
            shape((rows, HD), f32),
            shape((rows, half), bf16),
            shape((width, half), bf16),
        ),
        (
            tokens,
            positions.reshape(rows // 128, 128),
            frequency.reshape(1, HD),
            cotangent,
            counts,
            ratios.reshape(1, domains),
        ),
        fetched=6,
        sent=4 + width // CHUNK,
        flops=2 * rows * width * columns,
        bytes_accessed=8000000,
    )
    folded = call(fold_kernel, shape((shard, half), bf16), (kv_weight, gain), after=normed)
    taken = exchange(given, "core", 2, 1)
    own = call(own_kernel, shape((width, half), f32), (normed, keep))
    if on_cube:
        own_sum, steps = sum_on_cube(own, taken, shard)
        own_half = gather_on_cube(folded, steps)
    else:
        pair = own + taken.astype(f32)
        pair = lax.psum_scatter(pair, "fsdp", scatter_dimension=0, tiled=True)
        own_sum = lax.psum(pair, "outer")
        own_half = lax.all_gather(folded, "fsdp", axis=0, tiled=True)
    other_sum = exchange(own_sum, "core", 2, 1)
    weight_grad, gain_grad = call(
        finish_kernel,
        (shape((shard, columns), f32), shape((shard,), f32)),
        (counts, gain, kv_weight, own_sum, other_sum),
    )
    other_half = exchange(own_half, "core", 2, 1)
    keys_out = call(
        forward_kernel,
        shape((rows, columns), bf16),
        (normed, own_half, other_half, cosines, sines),
        flops=2 * rows * width * columns,
        bytes_accessed=3000000,
    )
    return (keys_out, weight_grad, gain_grad)


def solution(mesh):
    domains, members = mesh.shape["dom"], mesh.shape["fsdp"]
    outer = domains // 2
    split = Mesh(mesh.devices.reshape(outer, 2, members), EVERY)
    return jax.shard_map(
        functools.partial(body, outer, members),
        mesh=split,
        in_specs=(
            P(EVERY, None),
            P("fsdp"),
            P("fsdp", None),
            P(EVERY),
            P(EVERY, None),
            P(),
            P(),
        ),
        out_specs=(P(EVERY, None), P("fsdp", None), P("fsdp")),
        check_vma=False,
    )
```

```python
import functools

import jax
import jax.numpy as jnp
import numpy as np
from jax import lax
from jax.experimental import pallas as pl
from jax.experimental.pallas import tpu as pltpu
from jax.sharding import Mesh
from jax.sharding import PartitionSpec as P

KVH = 2
HD = 128
BLOCK = 128
CHUNK = 256
LONG = 40000000
EVERY = ("outer", "core", "fsdp")
VMEM_BYTES = 32 * 1024 * 1024


def to_column(line):
    n = line.shape[1]
    rows = lax.broadcasted_iota(jnp.int32, (n, n), 0)
    lanes = lax.broadcasted_iota(jnp.int32, (n, n), 1)
    spread = jnp.broadcast_to(line, (n, n))
    return jnp.sum(jnp.where(rows == lanes, spread, 0.0), axis=1, keepdims=True)


def to_line(column):
    n = column.shape[0]
    rows = lax.broadcasted_iota(jnp.int32, (n, n), 0)
    lanes = lax.broadcasted_iota(jnp.int32, (n, n), 1)
    spread = jnp.broadcast_to(column, (n, n))
    return jnp.sum(jnp.where(rows == lanes, spread, 0.0), axis=0, keepdims=True)


def transposed_dot(left, right):
    return lax.dot_general(
        left, right, (((0,), (0,)), ((), ())), preferred_element_type=jnp.float32
    )


def full_sum(values):
    return jnp.sum(jnp.sum(values, axis=1, keepdims=True), axis=0, keepdims=True)


def fetch(sources, buffers, semaphores):
    copies = []
    for i, (source, buffer) in enumerate(zip(sources, buffers)):
        copy = pltpu.make_async_copy(source, buffer, semaphores.at[i])
        copy.start()
        copies.append(copy)
    return copies


def call(kernel, out_shape, args, after=None, in_hbm=False, fetched=0, cost=1000000):
    count = len(args)
    args = [
        pltpu.with_memory_space_constraint(arg, pltpu.HBM) if i < fetched else arg
        for i, arg in enumerate(args)
    ]
    spaces = [pl.ANY] * fetched + [pltpu.VMEM] * (count - fetched)
    run = kernel
    if after is not None:
        if in_hbm:
            after = pltpu.with_memory_space_constraint(after, pltpu.HBM)
        args, spaces = args + [after], spaces + [pl.ANY]

        def run(*refs):
            kernel(*refs[:count], *refs[count + 1 :])

    scratch = [pltpu.VMEM(arg.shape, arg.dtype) for arg in args[:fetched]]
    if fetched:
        scratch.append(pltpu.SemaphoreType.DMA((fetched,)))
    return pl.pallas_call(
        run,
        out_shape=out_shape,
        in_specs=[pl.BlockSpec(memory_space=space) for space in spaces],
        scratch_shapes=scratch,
        out_specs=jax.tree.map(lambda _: pl.BlockSpec(memory_space=pltpu.VMEM), out_shape),
        compiler_params=pltpu.CompilerParams(vmem_limit_bytes=VMEM_BYTES),
        cost_estimate=pl.CostEstimate(flops=0, bytes_accessed=cost, transcendentals=0),
    )(*args)


def join_kernel(first_ref, second_ref, out_ref):
    count = first_ref.shape[0]
    out_ref[:count] = first_ref[...]
    out_ref[count:] = second_ref[...]


def order_kernel(order, first_ref, second_ref, out_ref):
    count, rows, _ = first_ref.shape
    member = lax.axis_index("fsdp")
    for i, shift in enumerate(order):
        at = pl.ds(pl.multiple_of(jnp.bitwise_xor(member, shift) * rows, rows), rows)
        out_ref[at, :] = first_ref[i] if i < count else second_ref[i - count]


def backward_kernel(
    positions_hbm, frequency_hbm, counts_hbm, ratios_hbm, cotangent_hbm, tokens_hbm,
    gain_hbm, weight_hbm,
    normed_ref, cosines_ref, sines_ref, own_ref, given_ref, folded_ref,
    positions_ref, frequency_ref, counts_ref, ratios_ref, cotangent_ref, tokens_ref,
    gain_ref, weight_ref,
    semaphores,
):
    copies = fetch(
        (
            positions_hbm, frequency_hbm, counts_hbm, ratios_hbm, cotangent_hbm, tokens_hbm,
            gain_hbm, weight_hbm,
        ),
        (
            positions_ref, frequency_ref, counts_ref, ratios_ref, cotangent_ref, tokens_ref,
            gain_ref, weight_ref,
        ),
        semaphores,
    )
    rows, width = tokens_ref.shape
    core = lax.axis_index("core")
    domain = lax.axis_index("outer") * 2 + core
    member = lax.axis_index("fsdp")

    for copy in copies[:5]:
        copy.wait()
    lines = positions_ref[...].astype(jnp.float32)
    place = jnp.concatenate(
        [to_column(lines[i : i + 1, :]) for i in range(lines.shape[0])], axis=0
    )
    angles = place * frequency_ref[...]
    cosines = jnp.cos(angles)
    lanes = lax.broadcasted_iota(jnp.int32, (rows, HD), 1)
    sines = jnp.sin(angles)
    sines = jnp.where(lanes < HD // 2, -sines, sines)
    cosines_ref[...] = cosines
    sines_ref[...] = sines

    counts = counts_ref[...].astype(jnp.float32)
    ratios = ratios_ref[...].astype(jnp.float32)
    at_domain = lax.broadcasted_iota(jnp.int32, counts.shape, 0) == domain
    at_member = lax.broadcasted_iota(jnp.int32, counts.shape, 1) == member
    ratio_at = lax.broadcasted_iota(jnp.int32, ratios.shape, 1) == domain
    live_total = full_sum(counts) * float(BLOCK)
    own_rows = full_sum(jnp.where(at_domain, counts, 0.0)) * float(BLOCK)
    own_live = full_sum(jnp.where(at_domain & at_member, counts, 0.0)) * float(BLOCK)
    own_ratio = full_sum(jnp.where(ratio_at, ratios, 0.0))
    factor = own_ratio / full_sum(ratios) * live_total / own_rows
    row_ids = lax.broadcasted_iota(jnp.int32, (rows, 1), 0).astype(jnp.float32)
    row_factor = jnp.where(row_ids < own_live, factor, 0.0)

    weighted = cotangent_ref[...].astype(jnp.float32) * row_factor
    key_width = KVH * HD
    turned = []
    for head in range(KVH):
        part = weighted[:, head * HD : (head + 1) * HD]
        turned.append(part * cosines - pltpu.roll(part, HD // 2, 1) * sines)
    keys = jnp.concatenate(turned, axis=1).astype(jnp.bfloat16)
    values = weighted[:, key_width:].astype(jnp.bfloat16)
    keep = jnp.where(core == 0, keys, values)
    give = jnp.where(core == 0, values, keys)

    copies[5].wait()
    step = 32
    for start in range(0, rows, step):
        block = tokens_ref[start : start + step, :].astype(jnp.float32)
        mean_square = jnp.sum(block * block, axis=1, keepdims=True) * (1.0 / width)
        normed_ref[start : start + step, :] = (
            block * lax.rsqrt(mean_square + 1e-06)
        ).astype(jnp.bfloat16)

    for start in range(0, width, CHUNK):
        at = slice(start, start + CHUNK)
        block = normed_ref[:, at]
        given_ref[at, :] = transposed_dot(block, give).astype(jnp.bfloat16)
        own_ref[at, :] = transposed_dot(block, keep)

    half = folded_ref.shape[1]
    columns = pl.ds(pl.multiple_of(core * half, half), half)
    copies[6].wait()
    gains = to_column(gain_ref[...].astype(jnp.float32).reshape(1, -1))
    copies[7].wait()
    folded = weight_ref[:, columns].astype(jnp.float32) * gains
    folded_ref[...] = folded.astype(jnp.bfloat16)


def aligned(index, size):
    return pl.ds(pl.multiple_of(index * size, size), size)


def total(kept, taken):
    return kept + taken.astype(jnp.float32)


def pair_kernel(own_ref, taken_ref, kept_y_ref, given_y_ref, kept_x_ref, given_x_ref):
    members, rows, columns = kept_y_ref.shape
    left, right = slice(0, columns), slice(columns, 2 * columns)
    y, x = lax.axis_index("outer"), lax.axis_index("fsdp") % 2
    for i in range(members):
        at = aligned(2 * i + y, rows)
        kept_y_ref[i] = total(own_ref[at, left], taken_ref[at, left])
        at = aligned(2 * i + 1 - y, rows)
        given_y_ref[i] = total(own_ref[at, left], taken_ref[at, left]).astype(jnp.bfloat16)
    for i in range(members // 2):
        at = aligned(2 * i + x, 2 * rows)
        kept_x_ref[i] = total(own_ref[at, right], taken_ref[at, right])
        at = aligned(2 * i + 1 - x, 2 * rows)
        given_x_ref[i] = total(own_ref[at, right], taken_ref[at, right]).astype(jnp.bfloat16)


def cross_kernel(
    kept_y_ref, taken_y_ref, kept_x_ref, taken_x_ref,
    next_x_ref, given_x_ref, next_y_ref, given_y_ref,
):
    count, rows, _ = next_x_ref.shape
    y, x = lax.axis_index("outer"), lax.axis_index("fsdp") % 2
    for i in range(count):
        at = 2 * i + x
        next_x_ref[i] = total(kept_y_ref[at], taken_y_ref[at])
        at = 2 * i + 1 - x
        given_x_ref[i] = total(kept_y_ref[at], taken_y_ref[at]).astype(jnp.bfloat16)
        at = aligned(y, rows)
        next_y_ref[i] = total(kept_x_ref[i, at, :], taken_x_ref[i, at, :])
        at = aligned(1 - y, rows)
        given_y_ref[i] = total(kept_x_ref[i, at, :], taken_x_ref[i, at, :]).astype(jnp.bfloat16)


def z_kernel(kept_x_ref, taken_x_ref, kept_y_ref, taken_y_ref, own_ref, *given_refs):
    columns = kept_x_ref.shape[2]
    left, right = slice(0, columns), slice(columns, 2 * columns)
    z = lax.axis_index("fsdp") // 2
    for shift, out_ref in enumerate((own_ref,) + given_refs):
        at = jnp.bitwise_xor(z, shift)
        out_ref[:, left] = total(kept_x_ref[at], taken_x_ref[at]).astype(out_ref.dtype)
        out_ref[:, right] = total(kept_y_ref[at], taken_y_ref[at]).astype(out_ref.dtype)


def last_kernel(own_ref, *refs):
    result = own_ref[...]
    for taken_ref in refs[:-1]:
        result = total(result, taken_ref[...])
    refs[-1][...] = result.astype(jnp.bfloat16)


def rows_kernel(mine_ref, across_ref, out_ref):
    rows = mine_ref.shape[0]
    y = lax.axis_index("outer")
    out_ref[aligned(y, rows), :] = mine_ref[...]
    out_ref[aligned(1 - y, rows), :] = across_ref[...]


def finish_kernel(
    counts_ref, gain_ref, weight_ref, own_ref, other_ref, weight_grad_ref, gain_grad_ref
):
    rows, half = own_ref.shape
    core = lax.axis_index("core")
    live_total = full_sum(counts_ref[...].astype(jnp.float32)) * float(BLOCK)
    scale = 1.0 / jnp.sqrt(live_total)
    gains = to_column(gain_ref[...].astype(jnp.float32).reshape(1, -1)) * scale
    own, other = own_ref[...].astype(jnp.float32), other_ref[...].astype(jnp.float32)
    dots = jnp.zeros((rows, 1), jnp.float32)
    for side in range(2):
        at = slice(side * half, (side + 1) * half)
        part = jnp.where(core == side, own, other)
        weight_grad_ref[:, at] = part * gains
        weight = weight_ref[:, at].astype(jnp.float32)
        dots = dots + jnp.sum(part * weight, axis=1, keepdims=True)
    gain_grad_ref[...] = to_line(dots * scale).reshape(rows)


def forward_kernel(normed_ref, own_ref, other_ref, cosines_ref, sines_ref, out_ref):
    core = lax.axis_index("core")
    normed = normed_ref[...]
    own = jnp.dot(normed, own_ref[...], preferred_element_type=jnp.float32)
    other = jnp.dot(normed, other_ref[...], preferred_element_type=jnp.float32)
    keys = jnp.where(core == 0, own, other)
    values = jnp.where(core == 0, other, own)
    cosines, sines = cosines_ref[...], sines_ref[...]
    for head in range(KVH):
        part = keys[:, head * HD : (head + 1) * HD]
        out_ref[:, head * HD : (head + 1) * HD] = (
            part * cosines + pltpu.roll(part, HD // 2, 1) * sines
        ).astype(jnp.bfloat16)
    out_ref[:, KVH * HD :] = values.astype(jnp.bfloat16)


def exchange(value, axes, count, shift):
    return lax.ppermute(value, axes, [(i, i ^ shift) for i in range(count)])


def sum_on_cube(own, taken, shard):
    width, half = own.shape
    f32, bf16 = jnp.float32, jnp.bfloat16
    shape = jax.ShapeDtypeStruct
    rows, columns = shard // 2, half // 2

    def both(*dims):
        return (shape(dims, f32), shape(dims, bf16))

    kept_y, given_y, kept_x, given_x = call(
        pair_kernel, both(8, rows, columns) + both(4, shard, columns), (own, taken)
    )
    pair_done = kept_x
    taken_y = exchange(given_y, "outer", 2, 1)
    taken_x = exchange(given_x, "fsdp", 8, 1)
    kept_x, given_x, kept_y, given_y = call(
        cross_kernel,
        both(4, rows, columns) + both(4, rows, columns),
        (kept_y, taken_y, kept_x, taken_x),
    )
    cross_done = kept_x
    taken_x = exchange(given_x, "fsdp", 8, 1)
    taken_y = exchange(given_y, "outer", 2, 1)
    kept, *given = call(
        z_kernel,
        (shape((rows, half), f32),) + (shape((rows, half), bf16),) * 3,
        (kept_x, taken_x, kept_y, taken_y),
        cost=LONG,
    )
    taken = [exchange(given[i], "fsdp", 8, 2 * i + 2) for i in range(3)]
    mine = call(last_kernel, shape((rows, half), bf16), (kept, *taken), cost=LONG)
    across = exchange(mine, "outer", 2, 1)
    own_sum = call(rows_kernel, shape((shard, half), bf16), (mine, across))
    return own_sum, (pair_done, cross_done, kept), mine


def gather_on_cube(folded, steps):
    shard, half = folded.shape
    parts, order = folded.reshape(1, shard, half), [0]
    for shift, after in zip((4, 2), steps):
        came = exchange(parts, "fsdp", 8, shift)
        order = order + [shift ^ i for i in order]
        out = jax.ShapeDtypeStruct((len(order), shard, half), folded.dtype)
        parts = call(join_kernel, out, (parts, came), after=after, cost=LONG)
    came = exchange(parts, "fsdp", 8, 1)
    order = order + [1 ^ i for i in order]
    out = jax.ShapeDtypeStruct((8 * shard, half), folded.dtype)
    return call(
        functools.partial(order_kernel, order), out, (parts, came), after=steps[2], cost=LONG
    )


def body(outer, members, tokens, gain, kv_weight, positions, cotangent, counts, ratios):
    domains = 2 * outer
    rows, width = tokens.shape
    shard, columns = kv_weight.shape
    half = columns // 2
    f32, bf16 = jnp.float32, jnp.bfloat16
    shape = jax.ShapeDtypeStruct
    on_cube = outer == 2 and members == 8 and shard % 32 == 0

    exponents = np.arange(HD, dtype=np.float64) % (HD // 2) * (2.0 / HD)
    frequency = jnp.asarray(np.power(1000000.0, -exponents).astype(np.float32))
    normed, cosines, sines, own, given, folded = call(
        backward_kernel,
        (
            shape((rows, width), bf16),
            shape((rows, HD), f32),
            shape((rows, HD), f32),
            shape((width, half), f32),
            shape((width, half), bf16),
            shape((shard, half), bf16),
        ),
        (
            positions.reshape(rows // 128, 128),
            frequency.reshape(1, HD),
            counts,
            ratios.reshape(1, domains),
            cotangent,
            tokens,
            gain,
            kv_weight,
        ),
        fetched=8,
    )
    taken = exchange(given, "core", 2, 1)
    if on_cube:
        own_sum, steps, mine = sum_on_cube(own, taken, shard)
        own_half = gather_on_cube(folded, steps)
    else:
        pair = own + taken.astype(f32)
        pair = lax.psum_scatter(pair, "fsdp", scatter_dimension=0, tiled=True)
        own_sum = mine = lax.psum(pair, "outer")
        own_half = lax.all_gather(folded, "fsdp", axis=0, tiled=True)
    other_sum = exchange(own_sum, "core", 2, 1)
    other_half = exchange(own_half, "core", 2, 1)
    keys_out = call(
        forward_kernel,
        shape((rows, columns), bf16),
        (normed, own_half, other_half, cosines, sines),
        after=mine,
        cost=LONG,
    )
    weight_grad, gain_grad = call(
        finish_kernel,
        (shape((shard, columns), f32), shape((shard,), f32)),
        (counts, gain, kv_weight, own_sum, other_sum),
        after=keys_out,
        in_hbm=True,
    )
    return (keys_out, weight_grad, gain_grad)


def solution(mesh):
    domains, members = mesh.shape["dom"], mesh.shape["fsdp"]
    outer = domains // 2
    split = Mesh(mesh.devices.reshape(outer, 2, members), EVERY)
    return jax.shard_map(
        functools.partial(body, outer, members),
        mesh=split,
        in_specs=(
            P(EVERY, None),
            P("fsdp"),
            P("fsdp", None),
            P(EVERY),
            P(EVERY, None),
            P(),
            P(),
        ),
        out_specs=(P(EVERY, None), P("fsdp", None), P("fsdp")),
        check_vma=False,
    )
```

```python
import functools

import jax
import jax.numpy as jnp
import numpy as np
from jax import lax
from jax.experimental import pallas as pl
from jax.experimental.pallas import tpu as pltpu
from jax.sharding import Mesh
from jax.sharding import PartitionSpec as P

KVH = 2
HD = 128
BLOCK = 128
CHUNK = 256
EVERY = ("outer", "core", "fsdp")
VMEM_BYTES = 32 * 1024 * 1024


def to_column(line):
    n = line.shape[1]
    rows = lax.broadcasted_iota(jnp.int32, (n, n), 0)
    lanes = lax.broadcasted_iota(jnp.int32, (n, n), 1)
    spread = jnp.broadcast_to(line, (n, n))
    return jnp.sum(jnp.where(rows == lanes, spread, 0.0), axis=1, keepdims=True)


def to_line(column):
    n = column.shape[0]
    rows = lax.broadcasted_iota(jnp.int32, (n, n), 0)
    lanes = lax.broadcasted_iota(jnp.int32, (n, n), 1)
    spread = jnp.broadcast_to(column, (n, n))
    return jnp.sum(jnp.where(rows == lanes, spread, 0.0), axis=0, keepdims=True)


def transposed_dot(left, right):
    return lax.dot_general(
        left, right, (((0,), (0,)), ((), ())), preferred_element_type=jnp.float32
    )


def full_sum(values):
    return jnp.sum(jnp.sum(values, axis=1, keepdims=True), axis=0, keepdims=True)


def fetch(sources, buffers, semaphores):
    copies = []
    for i, (source, buffer) in enumerate(zip(sources, buffers)):
        copy = pltpu.make_async_copy(source, buffer, semaphores.at[i])
        copy.start()
        copies.append(copy)
    return copies


def call(kernel, out_shape, args, after=None, in_hbm=False, fetched=0, cost=1000000):
    count = len(args)
    args = [
        pltpu.with_memory_space_constraint(arg, pltpu.HBM) if i < fetched else arg
        for i, arg in enumerate(args)
    ]
    spaces = [pl.ANY] * fetched + [pltpu.VMEM] * (count - fetched)
    run = kernel
    if after is not None:
        if in_hbm:
            after = pltpu.with_memory_space_constraint(after, pltpu.HBM)
        args, spaces = args + [after], spaces + [pl.ANY]

        def run(*refs):
            kernel(*refs[:count], *refs[count + 1 :])

    scratch = [pltpu.VMEM(arg.shape, arg.dtype) for arg in args[:fetched]]
    if fetched:
        scratch.append(pltpu.SemaphoreType.DMA((fetched,)))
    return pl.pallas_call(
        run,
        out_shape=out_shape,
        in_specs=[pl.BlockSpec(memory_space=space) for space in spaces],
        scratch_shapes=scratch,
        out_specs=jax.tree.map(lambda _: pl.BlockSpec(memory_space=pltpu.VMEM), out_shape),
        compiler_params=pltpu.CompilerParams(vmem_limit_bytes=VMEM_BYTES),
        cost_estimate=pl.CostEstimate(flops=0, bytes_accessed=cost, transcendentals=0),
    )(*args)


def copy_kernel(part_ref, out_ref):
    out_ref[...] = part_ref[...]


def stack_kernel(*refs):
    for i, part_ref in enumerate(refs[:-1]):
        refs[-1][i] = part_ref[...]


def order_kernel(order, first_ref, second_ref, out_ref):
    count, rows, _ = first_ref.shape
    member = lax.axis_index("fsdp")
    for i, shift in enumerate(order):
        at = pl.ds(pl.multiple_of(jnp.bitwise_xor(member, shift) * rows, rows), rows)
        out_ref[at, :] = first_ref[i] if i < count else second_ref[i - count]


def backward_kernel(
    positions_hbm, frequency_hbm, counts_hbm, ratios_hbm, cotangent_hbm, tokens_hbm,
    gain_hbm, weight_hbm,
    normed_ref, cosines_ref, sines_ref, own_ref, given_ref, folded_ref,
    positions_ref, frequency_ref, counts_ref, ratios_ref, cotangent_ref, tokens_ref,
    gain_ref, weight_ref,
    semaphores,
):
    copies = fetch(
        (
            positions_hbm, frequency_hbm, counts_hbm, ratios_hbm, cotangent_hbm, tokens_hbm,
            gain_hbm, weight_hbm,
        ),
        (
            positions_ref, frequency_ref, counts_ref, ratios_ref, cotangent_ref, tokens_ref,
            gain_ref, weight_ref,
        ),
        semaphores,
    )
    rows, width = tokens_ref.shape
    core = lax.axis_index("core")
    domain = lax.axis_index("outer") * 2 + core
    member = lax.axis_index("fsdp")

    for copy in copies[:5]:
        copy.wait()
    lines = positions_ref[...].astype(jnp.float32)
    place = jnp.concatenate(
        [to_column(lines[i : i + 1, :]) for i in range(lines.shape[0])], axis=0
    )
    angles = place * frequency_ref[...]
    cosines = jnp.cos(angles)
    lanes = lax.broadcasted_iota(jnp.int32, (rows, HD), 1)
    sines = jnp.sin(angles)
    sines = jnp.where(lanes < HD // 2, -sines, sines)
    cosines_ref[...] = cosines
    sines_ref[...] = sines

    counts = counts_ref[...].astype(jnp.float32)
    ratios = ratios_ref[...].astype(jnp.float32)
    at_domain = lax.broadcasted_iota(jnp.int32, counts.shape, 0) == domain
    at_member = lax.broadcasted_iota(jnp.int32, counts.shape, 1) == member
    ratio_at = lax.broadcasted_iota(jnp.int32, ratios.shape, 1) == domain
    live_total = full_sum(counts) * float(BLOCK)
    own_rows = full_sum(jnp.where(at_domain, counts, 0.0)) * float(BLOCK)
    own_live = full_sum(jnp.where(at_domain & at_member, counts, 0.0)) * float(BLOCK)
    own_ratio = full_sum(jnp.where(ratio_at, ratios, 0.0))
    factor = own_ratio / full_sum(ratios) * live_total / own_rows
    row_ids = lax.broadcasted_iota(jnp.int32, (rows, 1), 0).astype(jnp.float32)
    row_factor = jnp.where(row_ids < own_live, factor, 0.0)

    weighted = cotangent_ref[...].astype(jnp.float32) * row_factor
    key_width = KVH * HD
    turned = []
    for head in range(KVH):
        part = weighted[:, head * HD : (head + 1) * HD]
        turned.append(part * cosines - pltpu.roll(part, HD // 2, 1) * sines)
    keys = jnp.concatenate(turned, axis=1).astype(jnp.bfloat16)
    values = weighted[:, key_width:].astype(jnp.bfloat16)
    keep = jnp.where(core == 0, keys, values)
    give = jnp.where(core == 0, values, keys)

    copies[5].wait()
    step = 32
    for start in range(0, rows, step):
        block = tokens_ref[start : start + step, :].astype(jnp.float32)
        mean_square = jnp.sum(block * block, axis=1, keepdims=True) * (1.0 / width)
        normed_ref[start : start + step, :] = (
            block * lax.rsqrt(mean_square + 1e-06)
        ).astype(jnp.bfloat16)

    for start in range(0, width, CHUNK):
        at = slice(start, start + CHUNK)
        block = normed_ref[:, at]
        given_ref[at, :] = transposed_dot(block, give).astype(jnp.bfloat16)
        own_ref[at, :] = transposed_dot(block, keep)

    half = folded_ref.shape[1]
    columns = pl.ds(pl.multiple_of(core * half, half), half)
    copies[6].wait()
    gains = to_column(gain_ref[...].astype(jnp.float32).reshape(1, -1))
    copies[7].wait()
    folded = weight_ref[:, columns].astype(jnp.float32) * gains
    folded_ref[...] = folded.astype(jnp.bfloat16)


def aligned(index, size):
    return pl.ds(pl.multiple_of(index * size, size), size)


def total(kept, taken):
    return kept + taken.astype(jnp.float32)


def pair_kernel(own_ref, taken_ref, kept_y_ref, given_y_ref, kept_x_ref, given_x_ref):
    members, rows, columns = kept_y_ref.shape
    left, right = slice(0, columns), slice(columns, 2 * columns)
    y, x = lax.axis_index("outer"), lax.axis_index("fsdp") % 2
    for i in range(members):
        at = aligned(2 * i + y, rows)
        kept_y_ref[i] = total(own_ref[at, left], taken_ref[at, left])
        at = aligned(2 * i + 1 - y, rows)
        given_y_ref[i] = total(own_ref[at, left], taken_ref[at, left]).astype(jnp.bfloat16)
    for i in range(members // 2):
        at = aligned(2 * i + x, 2 * rows)
        kept_x_ref[i] = total(own_ref[at, right], taken_ref[at, right])
        at = aligned(2 * i + 1 - x, 2 * rows)
        given_x_ref[i] = total(own_ref[at, right], taken_ref[at, right]).astype(jnp.bfloat16)


def cross_kernel(
    kept_y_ref, taken_y_ref, kept_x_ref, taken_x_ref,
    next_x_ref, given_x_ref, next_y_ref, given_y_ref,
):
    count, rows, _ = next_x_ref.shape
    y, x = lax.axis_index("outer"), lax.axis_index("fsdp") % 2
    for i in range(count):
        at = 2 * i + x
        next_x_ref[i] = total(kept_y_ref[at], taken_y_ref[at])
        at = 2 * i + 1 - x
        given_x_ref[i] = total(kept_y_ref[at], taken_y_ref[at]).astype(jnp.bfloat16)
        at = aligned(y, rows)
        next_y_ref[i] = total(kept_x_ref[i, at, :], taken_x_ref[i, at, :])
        at = aligned(1 - y, rows)
        given_y_ref[i] = total(kept_x_ref[i, at, :], taken_x_ref[i, at, :]).astype(jnp.bfloat16)


def z_kernel(kept_x_ref, taken_x_ref, kept_y_ref, taken_y_ref, own_ref, *given_refs):
    columns = kept_x_ref.shape[2]
    left, right = slice(0, columns), slice(columns, 2 * columns)
    z = lax.axis_index("fsdp") // 2
    for shift, out_ref in enumerate((own_ref,) + given_refs):
        at = jnp.bitwise_xor(z, shift)
        out_ref[:, left] = total(kept_x_ref[at], taken_x_ref[at]).astype(out_ref.dtype)
        out_ref[:, right] = total(kept_y_ref[at], taken_y_ref[at]).astype(out_ref.dtype)


def last_kernel(own_ref, *refs):
    result = own_ref[...]
    for taken_ref in refs[:-1]:
        result = total(result, taken_ref[...])
    refs[-1][...] = result.astype(jnp.bfloat16)


def rows_kernel(mine_ref, across_ref, out_ref):
    rows = mine_ref.shape[0]
    y = lax.axis_index("outer")
    out_ref[aligned(y, rows), :] = mine_ref[...]
    out_ref[aligned(1 - y, rows), :] = across_ref[...]


def finish_kernel(
    counts_ref, gain_ref, weight_ref, own_ref, other_ref, weight_grad_ref, gain_grad_ref
):
    rows, half = own_ref.shape
    core = lax.axis_index("core")
    live_total = full_sum(counts_ref[...].astype(jnp.float32)) * float(BLOCK)
    scale = 1.0 / jnp.sqrt(live_total)
    gains = to_column(gain_ref[...].astype(jnp.float32).reshape(1, -1)) * scale
    own, other = own_ref[...].astype(jnp.float32), other_ref[...].astype(jnp.float32)
    dots = jnp.zeros((rows, 1), jnp.float32)
    for side in range(2):
        at = slice(side * half, (side + 1) * half)
        part = jnp.where(core == side, own, other)
        weight_grad_ref[:, at] = part * gains
        weight = weight_ref[:, at].astype(jnp.float32)
        dots = dots + jnp.sum(part * weight, axis=1, keepdims=True)
    gain_grad_ref[...] = to_line(dots * scale).reshape(rows)


def forward_kernel(normed_ref, own_ref, other_ref, cosines_ref, sines_ref, out_ref):
    core = lax.axis_index("core")
    normed = normed_ref[...]
    own = jnp.dot(normed, own_ref[...], preferred_element_type=jnp.float32)
    other = jnp.dot(normed, other_ref[...], preferred_element_type=jnp.float32)
    keys = jnp.where(core == 0, own, other)
    values = jnp.where(core == 0, other, own)
    cosines, sines = cosines_ref[...], sines_ref[...]
    for head in range(KVH):
        part = keys[:, head * HD : (head + 1) * HD]
        out_ref[:, head * HD : (head + 1) * HD] = (
            part * cosines + pltpu.roll(part, HD // 2, 1) * sines
        ).astype(jnp.bfloat16)
    out_ref[:, KVH * HD :] = values.astype(jnp.bfloat16)


def exchange(value, axes, count, shift):
    return lax.ppermute(value, axes, [(i, i ^ shift) for i in range(count)])


def sum_on_cube(own, taken, shard):
    width, half = own.shape
    f32, bf16 = jnp.float32, jnp.bfloat16
    shape = jax.ShapeDtypeStruct
    rows, columns = shard // 2, half // 2

    def both(*dims):
        return (shape(dims, f32), shape(dims, bf16))

    kept_y, given_y, kept_x, given_x = call(
        pair_kernel, both(8, rows, columns) + both(4, shard, columns), (own, taken)
    )
    taken_y = exchange(given_y, "outer", 2, 1)
    taken_x = exchange(given_x, "fsdp", 8, 1)
    kept_x, given_x, kept_y, given_y = call(
        cross_kernel,
        both(4, rows, columns) + both(4, rows, columns),
        (kept_y, taken_y, kept_x, taken_x),
    )
    taken_x = exchange(given_x, "fsdp", 8, 1)
    taken_y = exchange(given_y, "outer", 2, 1)
    cross_done = kept_x
    kept, *given = call(
        z_kernel,
        (shape((rows, half), f32),) + (shape((rows, half), bf16),) * 3,
        (kept_x, taken_x, kept_y, taken_y),
    )
    taken = [exchange(given[i], "fsdp", 8, 2 * i + 2) for i in range(3)]
    mine = call(last_kernel, shape((rows, half), bf16), (kept, *taken))
    across = exchange(mine, "outer", 2, 1)
    own_sum = call(rows_kernel, shape((shard, half), bf16), (mine, across))
    return own_sum, (cross_done, kept, mine), mine


def gather_on_cube(folded, steps):
    shard, half = folded.shape
    shape = jax.ShapeDtypeStruct
    far = exchange(folded, "fsdp", 8, 4)
    near = exchange(folded, "fsdp", 8, 2)
    passed = call(copy_kernel, shape(folded.shape, folded.dtype), (far,), after=steps[0])
    both = exchange(passed, "fsdp", 8, 2)
    out = shape((4, shard, half), folded.dtype)
    parts = call(stack_kernel, out, (folded, far, near, both), after=steps[1])
    came = exchange(parts, "fsdp", 8, 1)
    order = (0, 4, 2, 6, 1, 5, 3, 7)
    out = shape((8 * shard, half), folded.dtype)
    return call(functools.partial(order_kernel, order), out, (parts, came), after=steps[2])


def body(outer, members, tokens, gain, kv_weight, positions, cotangent, counts, ratios):
    domains = 2 * outer
    rows, width = tokens.shape
    shard, columns = kv_weight.shape
    half = columns // 2
    f32, bf16 = jnp.float32, jnp.bfloat16
    shape = jax.ShapeDtypeStruct
    on_cube = outer == 2 and members == 8 and shard % 32 == 0

    exponents = np.arange(HD, dtype=np.float64) % (HD // 2) * (2.0 / HD)
    frequency = jnp.asarray(np.power(1000000.0, -exponents).astype(np.float32))
    normed, cosines, sines, own, given, folded = call(
        backward_kernel,
        (
            shape((rows, width), bf16),
            shape((rows, HD), f32),
            shape((rows, HD), f32),
            shape((width, half), f32),
            shape((width, half), bf16),
            shape((shard, half), bf16),
        ),
        (
            positions.reshape(rows // 128, 128),
            frequency.reshape(1, HD),
            counts,
            ratios.reshape(1, domains),
            cotangent,
            tokens,
            gain,
            kv_weight,
        ),
        fetched=8,
    )
    taken = exchange(given, "core", 2, 1)
    if on_cube:
        own_sum, steps, mine = sum_on_cube(own, taken, shard)
        own_half = gather_on_cube(folded, steps)
    else:
        pair = own + taken.astype(f32)
        pair = lax.psum_scatter(pair, "fsdp", scatter_dimension=0, tiled=True)
        own_sum = mine = lax.psum(pair, "outer")
        own_half = lax.all_gather(folded, "fsdp", axis=0, tiled=True)
    other_sum = exchange(own_sum, "core", 2, 1)
    other_half = exchange(own_half, "core", 2, 1)
    keys_out = call(
        forward_kernel,
        shape((rows, columns), bf16),
        (normed, own_half, other_half, cosines, sines),
        after=mine,
    )
    weight_grad, gain_grad = call(
        finish_kernel,
        (shape((shard, columns), f32), shape((shard,), f32)),
        (counts, gain, kv_weight, own_sum, other_sum),
        after=keys_out,
        in_hbm=True,
    )
    return (keys_out, weight_grad, gain_grad)


def solution(mesh):
    domains, members = mesh.shape["dom"], mesh.shape["fsdp"]
    outer = domains // 2
    split = Mesh(mesh.devices.reshape(outer, 2, members), EVERY)
    return jax.shard_map(
        functools.partial(body, outer, members),
        mesh=split,
        in_specs=(
            P(EVERY, None),
            P("fsdp"),
            P("fsdp", None),
            P(EVERY),
            P(EVERY, None),
            P(),
            P(),
        ),
        out_specs=(P(EVERY, None), P("fsdp", None), P("fsdp")),
        check_vma=False,
    )
```

```python
import functools

import jax
import jax.numpy as jnp
import numpy as np
from jax import lax
from jax.experimental import pallas as pl
from jax.experimental.pallas import tpu as pltpu
from jax.sharding import Mesh
from jax.sharding import PartitionSpec as P

KVH = 2
HD = 128
BLOCK = 128
CHUNK = 256
EVERY = ("outer", "core", "fsdp")
VMEM_BYTES = 32 * 1024 * 1024


def to_column(line):
    n = line.shape[1]
    rows = lax.broadcasted_iota(jnp.int32, (n, n), 0)
    lanes = lax.broadcasted_iota(jnp.int32, (n, n), 1)
    spread = jnp.broadcast_to(line, (n, n))
    return jnp.sum(jnp.where(rows == lanes, spread, 0.0), axis=1, keepdims=True)


def to_line(column):
    n = column.shape[0]
    rows = lax.broadcasted_iota(jnp.int32, (n, n), 0)
    lanes = lax.broadcasted_iota(jnp.int32, (n, n), 1)
    spread = jnp.broadcast_to(column, (n, n))
    return jnp.sum(jnp.where(rows == lanes, spread, 0.0), axis=0, keepdims=True)


def transposed_dot(left, right):
    return lax.dot_general(
        left, right, (((0,), (0,)), ((), ())), preferred_element_type=jnp.float32
    )


def full_sum(values):
    return jnp.sum(jnp.sum(values, axis=1, keepdims=True), axis=0, keepdims=True)


def fetch(sources, buffers, semaphores):
    copies = []
    for i, (source, buffer) in enumerate(zip(sources, buffers)):
        copy = pltpu.make_async_copy(source, buffer, semaphores.at[i])
        copy.start()
        copies.append(copy)
    return copies


def call(kernel, out_shape, args, after=None, in_hbm=False, fetched=0, scratch=(), cost=1000000):
    count = len(args)
    args = [
        pltpu.with_memory_space_constraint(arg, pltpu.HBM) if i < fetched else arg
        for i, arg in enumerate(args)
    ]
    spaces = [pl.ANY] * fetched + [pltpu.VMEM] * (count - fetched)
    run = kernel
    if after is not None:
        if in_hbm:
            after = pltpu.with_memory_space_constraint(after, pltpu.HBM)
        args, spaces = args + [after], spaces + [pl.ANY]

        def run(*refs):
            kernel(*refs[:count], *refs[count + 1 :])

    scratch = list(scratch) + [pltpu.VMEM(arg.shape, arg.dtype) for arg in args[:fetched]]
    if fetched:
        scratch.append(pltpu.SemaphoreType.DMA((fetched,)))
    return pl.pallas_call(
        run,
        out_shape=out_shape,
        in_specs=[pl.BlockSpec(memory_space=space) for space in spaces],
        scratch_shapes=scratch,
        out_specs=jax.tree.map(lambda _: pl.BlockSpec(memory_space=pltpu.VMEM), out_shape),
        compiler_params=pltpu.CompilerParams(vmem_limit_bytes=VMEM_BYTES),
        cost_estimate=pl.CostEstimate(flops=0, bytes_accessed=cost, transcendentals=0),
    )(*args)


def copy_kernel(part_ref, out_ref):
    out_ref[...] = part_ref[...]


def stack_kernel(*refs):
    for i, part_ref in enumerate(refs[:-1]):
        refs[-1][i] = part_ref[...]


def order_kernel(order, first_ref, second_ref, out_ref):
    count, rows, _ = first_ref.shape
    member = lax.axis_index("fsdp")
    for i, shift in enumerate(order):
        at = pl.ds(pl.multiple_of(jnp.bitwise_xor(member, shift) * rows, rows), rows)
        out_ref[at, :] = first_ref[i] if i < count else second_ref[i - count]


def backward_kernel(
    positions_hbm, frequency_hbm, counts_hbm, ratios_hbm, cotangent_hbm, tokens_hbm,
    gain_hbm, weight_hbm,
    normed_ref, cosines_ref, sines_ref, own_ref, given_ref, folded_ref,
    positions_ref, frequency_ref, counts_ref, ratios_ref, cotangent_ref, tokens_ref,
    gain_ref, weight_ref,
    semaphores,
):
    copies = fetch(
        (
            positions_hbm, frequency_hbm, counts_hbm, ratios_hbm, cotangent_hbm, tokens_hbm,
            gain_hbm, weight_hbm,
        ),
        (
            positions_ref, frequency_ref, counts_ref, ratios_ref, cotangent_ref, tokens_ref,
            gain_ref, weight_ref,
        ),
        semaphores,
    )
    rows, width = tokens_ref.shape
    core = lax.axis_index("core")
    domain = lax.axis_index("outer") * 2 + core
    member = lax.axis_index("fsdp")

    for copy in copies[:5]:
        copy.wait()
    lines = positions_ref[...].astype(jnp.float32)
    place = jnp.concatenate(
        [to_column(lines[i : i + 1, :]) for i in range(lines.shape[0])], axis=0
    )
    angles = place * frequency_ref[...]
    cosines = jnp.cos(angles)
    lanes = lax.broadcasted_iota(jnp.int32, (rows, HD), 1)
    sines = jnp.sin(angles)
    sines = jnp.where(lanes < HD // 2, -sines, sines)
    cosines_ref[...] = cosines
    sines_ref[...] = sines

    counts = counts_ref[...].astype(jnp.float32)
    ratios = ratios_ref[...].astype(jnp.float32)
    at_domain = lax.broadcasted_iota(jnp.int32, counts.shape, 0) == domain
    at_member = lax.broadcasted_iota(jnp.int32, counts.shape, 1) == member
    ratio_at = lax.broadcasted_iota(jnp.int32, ratios.shape, 1) == domain
    live_total = full_sum(counts) * float(BLOCK)
    own_rows = full_sum(jnp.where(at_domain, counts, 0.0)) * float(BLOCK)
    own_live = full_sum(jnp.where(at_domain & at_member, counts, 0.0)) * float(BLOCK)
    own_ratio = full_sum(jnp.where(ratio_at, ratios, 0.0))
    factor = own_ratio / full_sum(ratios) * live_total / own_rows
    row_ids = lax.broadcasted_iota(jnp.int32, (rows, 1), 0).astype(jnp.float32)
    row_factor = jnp.where(row_ids < own_live, factor, 0.0)

    weighted = cotangent_ref[...].astype(jnp.float32) * row_factor
    key_width = KVH * HD
    turned = []
    for head in range(KVH):
        part = weighted[:, head * HD : (head + 1) * HD]
        turned.append(part * cosines - pltpu.roll(part, HD // 2, 1) * sines)
    keys = jnp.concatenate(turned, axis=1).astype(jnp.bfloat16)
    values = weighted[:, key_width:].astype(jnp.bfloat16)
    keep = jnp.where(core == 0, keys, values)
    give = jnp.where(core == 0, values, keys)

    copies[5].wait()
    step = 32
    for start in range(0, rows, step):
        block = tokens_ref[start : start + step, :].astype(jnp.float32)
        mean_square = jnp.sum(block * block, axis=1, keepdims=True) * (1.0 / width)
        normed_ref[start : start + step, :] = (
            block * lax.rsqrt(mean_square + 1e-06)
        ).astype(jnp.bfloat16)

    for start in range(0, width, CHUNK):
        at = slice(start, start + CHUNK)
        block = normed_ref[:, at]
        given_ref[at, :] = transposed_dot(block, give).astype(jnp.bfloat16)
        own_ref[at, :] = transposed_dot(block, keep)

    half = folded_ref.shape[1]
    columns = pl.ds(pl.multiple_of(core * half, half), half)
    copies[6].wait()
    gains = to_column(gain_ref[...].astype(jnp.float32).reshape(1, -1))
    copies[7].wait()
    folded = weight_ref[:, columns].astype(jnp.float32) * gains
    folded_ref[...] = folded.astype(jnp.bfloat16)


def aligned(index, size):
    return pl.ds(pl.multiple_of(index * size, size), size)


def total(kept, taken):
    return kept + taken.astype(jnp.float32)


def pair_kernel(own_ref, taken_ref, *out_refs):
    count, rows, _ = out_refs[0].shape
    y, x = lax.axis_index("outer"), lax.axis_index("fsdp") % 2
    for shift, out_ref in enumerate(out_refs):
        to_y, to_x = jnp.bitwise_xor(y, shift % 2), jnp.bitwise_xor(x, shift // 2)
        for i in range(count):
            at = aligned(4 * i + 2 * to_x + to_y, rows)
            out_ref[i] = total(own_ref[at, :], taken_ref[at, :]).astype(out_ref.dtype)


def z_kernel(kept_ref, first_ref, second_ref, third_ref, *out_refs):
    z = lax.axis_index("fsdp") // 2
    for shift, out_ref in enumerate(out_refs):
        at = jnp.bitwise_xor(z, shift)
        result = total(kept_ref[at], first_ref[at])
        result = total(total(result, second_ref[at]), third_ref[at])
        out_ref[...] = result.astype(out_ref.dtype)


def last_kernel(own_ref, *refs):
    result = own_ref[...]
    for taken_ref in refs[:-1]:
        result = total(result, taken_ref[...])
    refs[-1][...] = result.astype(jnp.bfloat16)


def finish_kernel(counts_ref, gain_ref, weight_ref, *refs):
    parts, (weight_grad_ref, gain_grad_ref, sum_ref) = refs[:-3], refs[-3:]
    rows, half = parts[0].shape
    y, core = lax.axis_index("outer"), lax.axis_index("core")
    live_total = full_sum(counts_ref[...].astype(jnp.float32)) * float(BLOCK)
    scale = 1.0 / jnp.sqrt(live_total)
    gains = to_column(gain_ref[...].astype(jnp.float32).reshape(1, -1)) * scale
    for shift, part_ref in enumerate(parts):
        at_y = 0 if len(parts) == 2 else jnp.bitwise_xor(y, shift // 2)
        at = jnp.bitwise_xor(core, shift % 2)
        sum_ref[aligned(at_y, rows), aligned(at, half)] = part_ref[...].astype(jnp.float32)
    result = sum_ref[...]
    weight_grad_ref[...] = result * gains
    dots = jnp.sum(result * weight_ref[...].astype(jnp.float32), axis=1, keepdims=True)
    gain_grad_ref[...] = to_line(dots * scale).reshape(-1)


def forward_kernel(normed_ref, own_ref, other_ref, cosines_ref, sines_ref, out_ref):
    core = lax.axis_index("core")
    normed = normed_ref[...]
    own = jnp.dot(normed, own_ref[...], preferred_element_type=jnp.float32)
    other = jnp.dot(normed, other_ref[...], preferred_element_type=jnp.float32)
    keys = jnp.where(core == 0, own, other)
    values = jnp.where(core == 0, other, own)
    cosines, sines = cosines_ref[...], sines_ref[...]
    for head in range(KVH):
        part = keys[:, head * HD : (head + 1) * HD]
        out_ref[:, head * HD : (head + 1) * HD] = (
            part * cosines + pltpu.roll(part, HD // 2, 1) * sines
        ).astype(jnp.bfloat16)
    out_ref[:, KVH * HD :] = values.astype(jnp.bfloat16)


def exchange(value, axes, count, shift):
    return lax.ppermute(value, axes, [(i, i ^ shift) for i in range(count)])


def sum_on_cube(own, taken, shard):
    width, half = own.shape
    f32, bf16 = jnp.float32, jnp.bfloat16
    shape = jax.ShapeDtypeStruct
    rows = shard // 2
    kept, *given = call(
        pair_kernel,
        (shape((4, rows, half), f32),) + (shape((4, rows, half), bf16),) * 3,
        (own, taken),
    )
    pair_done = kept
    taken = [
        exchange(given[0], "outer", 2, 1),
        exchange(given[1], "fsdp", 8, 1),
        exchange(given[2], ("outer", "fsdp"), 16, 9),
    ]
    kept, *given = call(
        z_kernel,
        (shape((rows, half), f32),) + (shape((rows, half), bf16),) * 3,
        (kept, *taken),
    )
    taken = [exchange(given[i], "fsdp", 8, 2 * i + 2) for i in range(3)]
    mine = call(last_kernel, shape((rows, half), bf16), (kept, *taken))
    return mine, (pair_done, kept, mine)


def gather_on_cube(folded, steps):
    shard, half = folded.shape
    shape = jax.ShapeDtypeStruct
    far = exchange(folded, "fsdp", 8, 4)
    near = exchange(folded, "fsdp", 8, 2)
    passed = call(copy_kernel, shape(folded.shape, folded.dtype), (far,), after=steps[0])
    both = exchange(passed, "fsdp", 8, 2)
    out = shape((4, shard, half), folded.dtype)
    parts = call(stack_kernel, out, (folded, far, near, both), after=steps[1])
    came = exchange(parts, "fsdp", 8, 1)
    order = (0, 4, 2, 6, 1, 5, 3, 7)
    out = shape((8 * shard, half), folded.dtype)
    return call(functools.partial(order_kernel, order), out, (parts, came), after=steps[2])


def body(outer, members, tokens, gain, kv_weight, positions, cotangent, counts, ratios):
    domains = 2 * outer
    rows, width = tokens.shape
    shard, columns = kv_weight.shape
    half = columns // 2
    f32, bf16 = jnp.float32, jnp.bfloat16
    shape = jax.ShapeDtypeStruct
    on_cube = outer == 2 and members == 8 and shard % 32 == 0

    exponents = np.arange(HD, dtype=np.float64) % (HD // 2) * (2.0 / HD)
    frequency = jnp.asarray(np.power(1000000.0, -exponents).astype(np.float32))
    normed, cosines, sines, own, given, folded = call(
        backward_kernel,
        (
            shape((rows, width), bf16),
            shape((rows, HD), f32),
            shape((rows, HD), f32),
            shape((width, half), f32),
            shape((width, half), bf16),
            shape((shard, half), bf16),
        ),
        (
            positions.reshape(rows // 128, 128),
            frequency.reshape(1, HD),
            counts,
            ratios.reshape(1, domains),
            cotangent,
            tokens,
            gain,
            kv_weight,
        ),
        fetched=8,
    )
    taken = exchange(given, "core", 2, 1)
    if on_cube:
        mine, steps = sum_on_cube(own, taken, shard)
        own_half = gather_on_cube(folded, steps)
        sums = [mine] + [exchange(mine, ("outer", "core"), 4, i) for i in (1, 2, 3)]
    else:
        pair = own + taken.astype(f32)
        pair = lax.psum_scatter(pair, "fsdp", scatter_dimension=0, tiled=True)
        mine = lax.psum(pair, "outer")
        own_half = lax.all_gather(folded, "fsdp", axis=0, tiled=True)
        sums = [mine, exchange(mine, "core", 2, 1)]
    other_half = exchange(own_half, "core", 2, 1)
    keys_out = call(
        forward_kernel,
        shape((rows, columns), bf16),
        (normed, own_half, other_half, cosines, sines),
        after=mine,
    )
    weight_grad, gain_grad = call(
        finish_kernel,
        (shape((shard, columns), f32), shape((shard,), f32)),
        (counts, gain, kv_weight, *sums),
        scratch=[pltpu.VMEM((shard, columns), f32)],
        after=keys_out,
        in_hbm=True,
    )
    return (keys_out, weight_grad, gain_grad)


def solution(mesh):
    domains, members = mesh.shape["dom"], mesh.shape["fsdp"]
    outer = domains // 2
    split = Mesh(mesh.devices.reshape(outer, 2, members), EVERY)
    return jax.shard_map(
        functools.partial(body, outer, members),
        mesh=split,
        in_specs=(
            P(EVERY, None),
            P("fsdp"),
            P("fsdp", None),
            P(EVERY),
            P(EVERY, None),
            P(),
            P(),
        ),
        out_specs=(P(EVERY, None), P("fsdp", None), P("fsdp")),
        check_vma=False,
    )
```

```python
import functools

import jax
import jax.numpy as jnp
import numpy as np
from jax import lax
from jax.experimental import pallas as pl
from jax.experimental.pallas import tpu as pltpu
from jax.sharding import Mesh
from jax.sharding import PartitionSpec as P

KVH = 2
HD = 128
BLOCK = 128
CHUNK = 256
EVERY = ("outer", "core", "fsdp")
VMEM_BYTES = 32 * 1024 * 1024


def to_column(line):
    n = line.shape[1]
    rows = lax.broadcasted_iota(jnp.int32, (n, n), 0)
    lanes = lax.broadcasted_iota(jnp.int32, (n, n), 1)
    spread = jnp.broadcast_to(line, (n, n))
    return jnp.sum(jnp.where(rows == lanes, spread, 0.0), axis=1, keepdims=True)


def to_line(column):
    n = column.shape[0]
    rows = lax.broadcasted_iota(jnp.int32, (n, n), 0)
    lanes = lax.broadcasted_iota(jnp.int32, (n, n), 1)
    spread = jnp.broadcast_to(column, (n, n))
    return jnp.sum(jnp.where(rows == lanes, spread, 0.0), axis=0, keepdims=True)


def transposed_dot(left, right):
    return lax.dot_general(
        left, right, (((0,), (0,)), ((), ())), preferred_element_type=jnp.float32
    )


def full_sum(values):
    return jnp.sum(jnp.sum(values, axis=1, keepdims=True), axis=0, keepdims=True)


def fetch(sources, buffers, semaphores):
    copies = []
    for i, (source, buffer) in enumerate(zip(sources, buffers)):
        copy = pltpu.make_async_copy(source, buffer, semaphores.at[i])
        copy.start()
        copies.append(copy)
    return copies


def call(kernel, out_shape, args, after=None, in_hbm=False, fetched=0, scratch=(), cost=1000000):
    count = len(args)
    args = [
        pltpu.with_memory_space_constraint(arg, pltpu.HBM) if i < fetched else arg
        for i, arg in enumerate(args)
    ]
    spaces = [pl.ANY] * fetched + [pltpu.VMEM] * (count - fetched)
    run = kernel
    if after is not None:
        if in_hbm:
            after = pltpu.with_memory_space_constraint(after, pltpu.HBM)
        args, spaces = args + [after], spaces + [pl.ANY]

        def run(*refs):
            kernel(*refs[:count], *refs[count + 1 :])

    scratch = list(scratch) + [pltpu.VMEM(arg.shape, arg.dtype) for arg in args[:fetched]]
    if fetched:
        scratch.append(pltpu.SemaphoreType.DMA((fetched,)))
    return pl.pallas_call(
        run,
        out_shape=out_shape,
        in_specs=[pl.BlockSpec(memory_space=space) for space in spaces],
        scratch_shapes=scratch,
        out_specs=jax.tree.map(lambda _: pl.BlockSpec(memory_space=pltpu.VMEM), out_shape),
        compiler_params=pltpu.CompilerParams(vmem_limit_bytes=VMEM_BYTES),
        cost_estimate=pl.CostEstimate(flops=0, bytes_accessed=cost, transcendentals=0),
    )(*args)


def stack_kernel(*refs):
    for i, part_ref in enumerate(refs[:-1]):
        refs[-1][i] = part_ref[...]


def order_kernel(shifts, *refs):
    out_ref = refs[-1]
    rows = refs[0].shape[1]
    member = lax.axis_index("fsdp")
    parts = [part_ref.at[i] for part_ref in refs[:-1] for i in range(part_ref.shape[0])]
    for shift, part_ref in zip(shifts, parts):
        out_ref[aligned(jnp.bitwise_xor(member, shift), rows), :] = part_ref[...]


def backward_kernel(
    positions_hbm, frequency_hbm, counts_hbm, ratios_hbm, cotangent_hbm, tokens_hbm,
    gain_hbm, weight_hbm,
    normed_ref, cosines_ref, sines_ref, own_ref, given_ref, folded_ref,
    positions_ref, frequency_ref, counts_ref, ratios_ref, cotangent_ref, tokens_ref,
    gain_ref, weight_ref,
    semaphores,
):
    copies = fetch(
        (
            positions_hbm, frequency_hbm, counts_hbm, ratios_hbm, cotangent_hbm, tokens_hbm,
            gain_hbm, weight_hbm,
        ),
        (
            positions_ref, frequency_ref, counts_ref, ratios_ref, cotangent_ref, tokens_ref,
            gain_ref, weight_ref,
        ),
        semaphores,
    )
    rows, width = tokens_ref.shape
    core = lax.axis_index("core")
    domain = lax.axis_index("outer") * 2 + core
    member = lax.axis_index("fsdp")

    for copy in copies[:5]:
        copy.wait()
    lines = positions_ref[...].astype(jnp.float32)
    place = jnp.concatenate(
        [to_column(lines[i : i + 1, :]) for i in range(lines.shape[0])], axis=0
    )
    angles = place * frequency_ref[...]
    cosines = jnp.cos(angles)
    lanes = lax.broadcasted_iota(jnp.int32, (rows, HD), 1)
    sines = jnp.sin(angles)
    sines = jnp.where(lanes < HD // 2, -sines, sines)
    cosines_ref[...] = cosines
    sines_ref[...] = sines

    counts = counts_ref[...].astype(jnp.float32)
    ratios = ratios_ref[...].astype(jnp.float32)
    at_domain = lax.broadcasted_iota(jnp.int32, counts.shape, 0) == domain
    at_member = lax.broadcasted_iota(jnp.int32, counts.shape, 1) == member
    ratio_at = lax.broadcasted_iota(jnp.int32, ratios.shape, 1) == domain
    live_total = full_sum(counts) * float(BLOCK)
    own_rows = full_sum(jnp.where(at_domain, counts, 0.0)) * float(BLOCK)
    own_live = full_sum(jnp.where(at_domain & at_member, counts, 0.0)) * float(BLOCK)
    own_ratio = full_sum(jnp.where(ratio_at, ratios, 0.0))
    factor = own_ratio / full_sum(ratios) * live_total / own_rows
    row_ids = lax.broadcasted_iota(jnp.int32, (rows, 1), 0).astype(jnp.float32)
    row_factor = jnp.where(row_ids < own_live, factor, 0.0)

    weighted = cotangent_ref[...].astype(jnp.float32) * row_factor
    key_width = KVH * HD
    turned = []
    for head in range(KVH):
        part = weighted[:, head * HD : (head + 1) * HD]
        turned.append(part * cosines - pltpu.roll(part, HD // 2, 1) * sines)
    keys = jnp.concatenate(turned, axis=1).astype(jnp.bfloat16)
    values = weighted[:, key_width:].astype(jnp.bfloat16)
    keep = jnp.where(core == 0, keys, values)
    give = jnp.where(core == 0, values, keys)

    copies[5].wait()
    step = 32
    for start in range(0, rows, step):
        block = tokens_ref[start : start + step, :].astype(jnp.float32)
        mean_square = jnp.sum(block * block, axis=1, keepdims=True) * (1.0 / width)
        normed_ref[start : start + step, :] = (
            block * lax.rsqrt(mean_square + 1e-06)
        ).astype(jnp.bfloat16)

    for start in range(0, width, CHUNK):
        at = slice(start, start + CHUNK)
        block = normed_ref[:, at]
        given_ref[at, :] = transposed_dot(block, give).astype(jnp.bfloat16)
        own_ref[at, :] = transposed_dot(block, keep)

    half = folded_ref.shape[1]
    columns = pl.ds(pl.multiple_of(core * half, half), half)
    copies[6].wait()
    gains = to_column(gain_ref[...].astype(jnp.float32).reshape(1, -1))
    copies[7].wait()
    folded = weight_ref[:, columns].astype(jnp.float32) * gains
    folded_ref[...] = folded.astype(jnp.bfloat16)


def aligned(index, size):
    return pl.ds(pl.multiple_of(index * size, size), size)


def total(kept, taken):
    return kept + taken.astype(jnp.float32)


def pair_kernel(own_ref, taken_ref, *out_refs):
    count, rows, _ = out_refs[0].shape
    y, x = lax.axis_index("outer"), lax.axis_index("fsdp") % 2
    for (away_y, away_x), out_ref in zip(((0, 0), (1, 1), (1, 0), (0, 1)), out_refs):
        to_y, to_x = jnp.bitwise_xor(y, away_y), jnp.bitwise_xor(x, away_x)
        for i in range(count):
            at = aligned(4 * i + 2 * to_x + to_y, rows)
            out_ref[i] = total(own_ref[at, :], taken_ref[at, :]).astype(out_ref.dtype)


def z_kernel(kept_ref, first_ref, second_ref, third_ref, *out_refs):
    z = lax.axis_index("fsdp") // 2
    for shift, out_ref in enumerate(out_refs):
        at = jnp.bitwise_xor(z, shift)
        result = total(kept_ref[at], first_ref[at])
        result = total(total(result, second_ref[at]), third_ref[at])
        out_ref[...] = result.astype(out_ref.dtype)


def last_kernel(own_ref, *refs):
    result = own_ref[...]
    for taken_ref in refs[:-1]:
        result = total(result, taken_ref[...])
    refs[-1][...] = result.astype(jnp.bfloat16)


def finish_kernel(counts_ref, gain_ref, weight_ref, *refs):
    parts, (weight_grad_ref, gain_grad_ref, sum_ref) = refs[:-3], refs[-3:]
    rows, half = parts[0].shape
    y, core = lax.axis_index("outer"), lax.axis_index("core")
    live_total = full_sum(counts_ref[...].astype(jnp.float32)) * float(BLOCK)
    scale = 1.0 / jnp.sqrt(live_total)
    gains = to_column(gain_ref[...].astype(jnp.float32).reshape(1, -1)) * scale
    for shift, part_ref in enumerate(parts):
        at_y = 0 if len(parts) == 2 else jnp.bitwise_xor(y, shift // 2)
        at = jnp.bitwise_xor(core, shift % 2)
        sum_ref[aligned(at_y, rows), aligned(at, half)] = part_ref[...].astype(jnp.float32)
    result = sum_ref[...]
    weight_grad_ref[...] = result * gains
    dots = jnp.sum(result * weight_ref[...].astype(jnp.float32), axis=1, keepdims=True)
    gain_grad_ref[...] = to_line(dots * scale).reshape(-1)


def forward_kernel(normed_ref, own_ref, other_ref, cosines_ref, sines_ref, out_ref):
    core = lax.axis_index("core")
    normed = normed_ref[...]
    own = jnp.dot(normed, own_ref[...], preferred_element_type=jnp.float32)
    other = jnp.dot(normed, other_ref[...], preferred_element_type=jnp.float32)
    keys = jnp.where(core == 0, own, other)
    values = jnp.where(core == 0, other, own)
    cosines, sines = cosines_ref[...], sines_ref[...]
    for head in range(KVH):
        part = keys[:, head * HD : (head + 1) * HD]
        out_ref[:, head * HD : (head + 1) * HD] = (
            part * cosines + pltpu.roll(part, HD // 2, 1) * sines
        ).astype(jnp.bfloat16)
    out_ref[:, KVH * HD :] = values.astype(jnp.bfloat16)


def exchange(value, axes, count, shift):
    return lax.ppermute(value, axes, [(i, i ^ shift) for i in range(count)])


def sum_on_cube(own, taken, shard):
    width, half = own.shape
    f32, bf16 = jnp.float32, jnp.bfloat16
    shape = jax.ShapeDtypeStruct
    rows = shard // 2
    kept, *given = call(
        pair_kernel,
        (shape((4, rows, half), f32),) + (shape((4, rows, half), bf16),) * 3,
        (own, taken),
    )
    pair_done = kept
    taken = [
        exchange(given[0], ("outer", "fsdp"), 16, 9),
        exchange(given[1], "outer", 2, 1),
        exchange(given[2], "fsdp", 8, 1),
    ]
    first_xy, second_xy, third_xy = taken
    kept, *given = call(
        z_kernel,
        (shape((rows, half), f32),) + (shape((rows, half), bf16),) * 3,
        (kept, *taken),
    )
    taken = [exchange(given[i], "fsdp", 8, 2 * i + 2) for i in range(3)]
    mine = call(last_kernel, shape((rows, half), bf16), (kept, *taken))
    return mine, (pair_done, pair_done, kept, mine)


def gather_on_cube(folded, steps):
    shard, half = folded.shape
    shape = jax.ShapeDtypeStruct

    def over(part, shift):
        return exchange(part, "fsdp", 8, shift)

    def stack(*parts, after):
        out = shape((len(parts), shard, half), folded.dtype)
        return call(stack_kernel, out, parts, after=after)

    near, far = over(folded, 2), over(folded, 4)
    both = over(stack(far, after=steps[0])[0], 2)
    low = stack(folded, near, after=steps[1])
    high = stack(far, both, after=steps[2])
    shifts = (0, 2, 4, 6, 1, 3, 5, 7)
    return call(
        functools.partial(order_kernel, shifts),
        shape((8 * shard, half), folded.dtype),
        (low, high, over(low, 1), over(high, 1)),
        after=steps[3],
    )


def body(outer, members, tokens, gain, kv_weight, positions, cotangent, counts, ratios):
    domains = 2 * outer
    rows, width = tokens.shape
    shard, columns = kv_weight.shape
    half = columns // 2
    f32, bf16 = jnp.float32, jnp.bfloat16
    shape = jax.ShapeDtypeStruct
    on_cube = outer == 2 and members == 8 and shard % 32 == 0

    exponents = np.arange(HD, dtype=np.float64) % (HD // 2) * (2.0 / HD)
    frequency = jnp.asarray(np.power(1000000.0, -exponents).astype(np.float32))
    normed, cosines, sines, own, given, folded = call(
        backward_kernel,
        (
            shape((rows, width), bf16),
            shape((rows, HD), f32),
            shape((rows, HD), f32),
            shape((width, half), f32),
            shape((width, half), bf16),
            shape((shard, half), bf16),
        ),
        (
            positions.reshape(rows // 128, 128),
            frequency.reshape(1, HD),
            counts,
            ratios.reshape(1, domains),
            cotangent,
            tokens,
            gain,
            kv_weight,
        ),
        fetched=8,
    )
    taken = exchange(given, "core", 2, 1)
    if on_cube:
        mine, steps = sum_on_cube(own, taken, shard)
        own_half = gather_on_cube(folded, steps)
        sums = [mine] + [exchange(mine, ("outer", "core"), 4, i) for i in (1, 2, 3)]
    else:
        pair = own + taken.astype(f32)
        pair = lax.psum_scatter(pair, "fsdp", scatter_dimension=0, tiled=True)
        mine = lax.psum(pair, "outer")
        own_half = lax.all_gather(folded, "fsdp", axis=0, tiled=True)
        sums = [mine, exchange(mine, "core", 2, 1)]
    other_half = exchange(own_half, "core", 2, 1)
    keys_out = call(
        forward_kernel,
        shape((rows, columns), bf16),
        (normed, own_half, other_half, cosines, sines),
        after=mine,
    )
    weight_grad, gain_grad = call(
        finish_kernel,
        (shape((shard, columns), f32), shape((shard,), f32)),
        (counts, gain, kv_weight, *sums),
        scratch=[pltpu.VMEM((shard, columns), f32)],
        after=keys_out,
        in_hbm=True,
    )
    return (keys_out, weight_grad, gain_grad)


def solution(mesh):
    domains, members = mesh.shape["dom"], mesh.shape["fsdp"]
    outer = domains // 2
    split = Mesh(mesh.devices.reshape(outer, 2, members), EVERY)
    return jax.shard_map(
        functools.partial(body, outer, members),
        mesh=split,
        in_specs=(
            P(EVERY, None),
            P("fsdp"),
            P("fsdp", None),
            P(EVERY),
            P(EVERY, None),
            P(),
            P(),
        ),
        out_specs=(P(EVERY, None), P("fsdp", None), P("fsdp")),
        check_vma=False,
    )
```

```python
import functools

import jax
import jax.numpy as jnp
import numpy as np
from jax import lax
from jax.experimental import pallas as pl
from jax.experimental.pallas import tpu as pltpu
from jax.sharding import Mesh
from jax.sharding import PartitionSpec as P

KVH = 2
HD = 128
BLOCK = 128
CHUNK = 256
EVERY = ("outer", "core", "fsdp")
VMEM_BYTES = 32 * 1024 * 1024


def to_column(line):
    n = line.shape[1]
    rows = lax.broadcasted_iota(jnp.int32, (n, n), 0)
    lanes = lax.broadcasted_iota(jnp.int32, (n, n), 1)
    spread = jnp.broadcast_to(line, (n, n))
    return jnp.sum(jnp.where(rows == lanes, spread, 0.0), axis=1, keepdims=True)


def to_line(column):
    n = column.shape[0]
    rows = lax.broadcasted_iota(jnp.int32, (n, n), 0)
    lanes = lax.broadcasted_iota(jnp.int32, (n, n), 1)
    spread = jnp.broadcast_to(column, (n, n))
    return jnp.sum(jnp.where(rows == lanes, spread, 0.0), axis=0, keepdims=True)


def sine_cosine(angles):
    turns = jnp.floor(angles * (2.0 / np.pi) + 0.5)
    rest = angles - turns * 1.5703125
    rest = rest - turns * 4.837512969970703125e-4
    rest = rest - turns * 7.54978995489188216e-8
    square = rest * rest
    sine = (-1.9515295891e-4 * square + 8.3321608736e-3) * square - 1.6666654611e-1
    sine = sine * square * rest + rest
    cosine = (2.443315711809948e-5 * square - 1.388731625493765e-3) * square
    cosine = (cosine + 4.166664568298827e-2) * square * square - 0.5 * square + 1.0
    quarter = turns.astype(jnp.int32) & 3
    odd = (quarter & 1) == 1
    sines, cosines = jnp.where(odd, cosine, sine), jnp.where(odd, sine, cosine)
    sines = jnp.where(quarter >= 2, -sines, sines)
    cosines = jnp.where(((quarter + 1) & 2) == 2, -cosines, cosines)
    return sines, cosines


def transposed_dot(left, right):
    return lax.dot_general(
        left, right, (((0,), (0,)), ((), ())), preferred_element_type=jnp.float32
    )


def full_sum(values):
    return jnp.sum(jnp.sum(values, axis=1, keepdims=True), axis=0, keepdims=True)


def fetch(sources, buffers, semaphores):
    copies = []
    for i, (source, buffer) in enumerate(zip(sources, buffers)):
        copy = pltpu.make_async_copy(source, buffer, semaphores.at[i])
        copy.start()
        copies.append(copy)
    return copies


def call(kernel, out_shape, args, after=None, in_hbm=False, fetched=0, scratch=(), cost=1000000):
    count = len(args)
    args = [
        pltpu.with_memory_space_constraint(arg, pltpu.HBM) if i < fetched else arg
        for i, arg in enumerate(args)
    ]
    spaces = [pl.ANY] * fetched + [pltpu.VMEM] * (count - fetched)
    run = kernel
    if after is not None:
        if in_hbm:
            after = pltpu.with_memory_space_constraint(after, pltpu.HBM)
        args, spaces = args + [after], spaces + [pl.ANY]

        def run(*refs):
            kernel(*refs[:count], *refs[count + 1 :])

    scratch = list(scratch) + [pltpu.VMEM(arg.shape, arg.dtype) for arg in args[:fetched]]
    if fetched:
        scratch.append(pltpu.SemaphoreType.DMA((fetched,)))
    return pl.pallas_call(
        run,
        out_shape=out_shape,
        in_specs=[pl.BlockSpec(memory_space=space) for space in spaces],
        scratch_shapes=scratch,
        out_specs=jax.tree.map(lambda _: pl.BlockSpec(memory_space=pltpu.VMEM), out_shape),
        compiler_params=pltpu.CompilerParams(vmem_limit_bytes=VMEM_BYTES),
        cost_estimate=pl.CostEstimate(flops=0, bytes_accessed=cost, transcendentals=0),
    )(*args)


def stack_kernel(*refs):
    for i, part_ref in enumerate(refs[:-1]):
        refs[-1][i] = part_ref[...]


def order_kernel(shifts, *refs):
    out_ref = refs[-1]
    rows = refs[0].shape[1]
    member = lax.axis_index("fsdp")
    parts = [part_ref.at[i] for part_ref in refs[:-1] for i in range(part_ref.shape[0])]
    for shift, part_ref in zip(shifts, parts):
        out_ref[aligned(jnp.bitwise_xor(member, shift), rows), :] = part_ref[...]


def backward_kernel(
    positions_hbm, frequency_hbm, counts_hbm, ratios_hbm, cotangent_hbm, tokens_hbm,
    gain_hbm, weight_hbm,
    normed_ref, cosines_ref, sines_ref, own_ref, given_ref, folded_ref,
    positions_ref, frequency_ref, counts_ref, ratios_ref, cotangent_ref, tokens_ref,
    gain_ref, weight_ref,
    semaphores,
):
    copies = fetch(
        (
            positions_hbm, frequency_hbm, counts_hbm, ratios_hbm, cotangent_hbm, tokens_hbm,
            gain_hbm, weight_hbm,
        ),
        (
            positions_ref, frequency_ref, counts_ref, ratios_ref, cotangent_ref, tokens_ref,
            gain_ref, weight_ref,
        ),
        semaphores,
    )
    rows, width = tokens_ref.shape
    core = lax.axis_index("core")
    domain = lax.axis_index("outer") * 2 + core
    member = lax.axis_index("fsdp")

    for copy in copies[:5]:
        copy.wait()
    lines = positions_ref[...].astype(jnp.float32)
    lanes = lax.broadcasted_iota(jnp.int32, (lines.shape[1], HD), 1)
    left = lanes < HD // 2
    first, second = to_column(lines[0:1, :]), to_column(lines[1:2, :])
    sines, cosines = sine_cosine(jnp.where(left, first, second) * frequency_ref[...])
    turned_sines, turned_cosines = pltpu.roll(sines, HD // 2, 1), pltpu.roll(cosines, HD // 2, 1)
    cosines = jnp.concatenate(
        [jnp.where(left, cosines, turned_cosines), jnp.where(left, turned_cosines, cosines)]
    )
    sines = jnp.concatenate(
        [jnp.where(left, -sines, turned_sines), jnp.where(left, -turned_sines, sines)]
    )
    cosines_ref[...] = cosines
    sines_ref[...] = sines

    counts = counts_ref[...].astype(jnp.float32)
    ratios = ratios_ref[...].astype(jnp.float32)
    at_domain = lax.broadcasted_iota(jnp.int32, counts.shape, 0) == domain
    at_member = lax.broadcasted_iota(jnp.int32, counts.shape, 1) == member
    ratio_at = lax.broadcasted_iota(jnp.int32, ratios.shape, 1) == domain
    live_total = full_sum(counts) * float(BLOCK)
    own_rows = full_sum(jnp.where(at_domain, counts, 0.0)) * float(BLOCK)
    own_live = full_sum(jnp.where(at_domain & at_member, counts, 0.0)) * float(BLOCK)
    own_ratio = full_sum(jnp.where(ratio_at, ratios, 0.0))
    factor = own_ratio / full_sum(ratios) * live_total / own_rows
    row_ids = lax.broadcasted_iota(jnp.int32, (rows, 1), 0).astype(jnp.float32)
    row_factor = jnp.where(row_ids < own_live, factor, 0.0)

    weighted = cotangent_ref[...].astype(jnp.float32) * row_factor
    key_width = KVH * HD
    turned = []
    for head in range(KVH):
        part = weighted[:, head * HD : (head + 1) * HD]
        turned.append(part * cosines - pltpu.roll(part, HD // 2, 1) * sines)
    keys = jnp.concatenate(turned, axis=1).astype(jnp.bfloat16)
    values = weighted[:, key_width:].astype(jnp.bfloat16)
    keep = jnp.where(core == 0, keys, values)
    give = jnp.where(core == 0, values, keys)
    both = jnp.concatenate([keep, give], axis=1)
    half = keep.shape[1]

    copies[5].wait()
    step = 32
    for start in range(0, rows, step):
        block = tokens_ref[start : start + step, :].astype(jnp.float32)
        mean_square = jnp.sum(block * block, axis=1, keepdims=True) * (1.0 / width)
        normed_ref[start : start + step, :] = (
            block * lax.rsqrt(mean_square + 1e-06)
        ).astype(jnp.bfloat16)

    for start in range(0, width, CHUNK):
        at = slice(start, start + CHUNK)
        result = transposed_dot(normed_ref[:, at], both)
        own_ref[at, :] = result[:, :half]
        given_ref[at, :] = result[:, half:].astype(jnp.bfloat16)

    columns = pl.ds(pl.multiple_of(core * half, half), half)
    copies[6].wait()
    gains = to_column(gain_ref[...].astype(jnp.float32).reshape(1, -1))
    copies[7].wait()
    folded = weight_ref[:, columns].astype(jnp.float32) * gains
    folded_ref[...] = folded.astype(jnp.bfloat16)


def aligned(index, size):
    return pl.ds(pl.multiple_of(index * size, size), size)


def total(kept, taken):
    return kept + taken.astype(jnp.float32)


def pair_kernel(own_ref, taken_ref, *out_refs):
    count, rows, _ = out_refs[0].shape
    y, x = lax.axis_index("outer"), lax.axis_index("fsdp") % 2
    for (away_y, away_x), out_ref in zip(((0, 0), (1, 1), (1, 0), (0, 1)), out_refs):
        to_y, to_x = jnp.bitwise_xor(y, away_y), jnp.bitwise_xor(x, away_x)
        for i in range(count):
            at = aligned(4 * i + 2 * to_x + to_y, rows)
            out_ref[i] = total(own_ref[at, :], taken_ref[at, :]).astype(out_ref.dtype)


def z_kernel(kept_ref, first_ref, second_ref, third_ref, *out_refs):
    z = lax.axis_index("fsdp") // 2
    for shift, out_ref in enumerate(out_refs):
        at = jnp.bitwise_xor(z, shift)
        result = total(kept_ref[at], first_ref[at])
        result = total(total(result, second_ref[at]), third_ref[at])
        out_ref[...] = result.astype(out_ref.dtype)


def last_kernel(own_ref, *refs):
    result = own_ref[...]
    for taken_ref in refs[:-1]:
        result = total(result, taken_ref[...])
    refs[-1][...] = result.astype(jnp.bfloat16)


def finish_kernel(counts_ref, gain_ref, weight_ref, *refs):
    parts, (weight_grad_ref, gain_grad_ref, sum_ref) = refs[:-3], refs[-3:]
    rows, half = parts[0].shape
    y, core = lax.axis_index("outer"), lax.axis_index("core")
    live_total = full_sum(counts_ref[...].astype(jnp.float32)) * float(BLOCK)
    scale = 1.0 / jnp.sqrt(live_total)
    gains = to_column(gain_ref[...].astype(jnp.float32).reshape(1, -1)) * scale
    for shift, part_ref in enumerate(parts):
        at_y = 0 if len(parts) == 2 else jnp.bitwise_xor(y, shift // 2)
        at = jnp.bitwise_xor(core, shift % 2)
        sum_ref[aligned(at_y, rows), aligned(at, half)] = part_ref[...].astype(jnp.float32)
    result = sum_ref[...]
    weight_grad_ref[...] = result * gains
    dots = jnp.sum(result * weight_ref[...].astype(jnp.float32), axis=1, keepdims=True)
    gain_grad_ref[...] = to_line(dots * scale).reshape(-1)


def forward_kernel(normed_ref, own_ref, other_ref, cosines_ref, sines_ref, out_ref):
    core = lax.axis_index("core")
    normed = normed_ref[...]
    own = jnp.dot(normed, own_ref[...], preferred_element_type=jnp.float32)
    other = jnp.dot(normed, other_ref[...], preferred_element_type=jnp.float32)
    keys = jnp.where(core == 0, own, other)
    values = jnp.where(core == 0, other, own)
    cosines, sines = cosines_ref[...], sines_ref[...]
    for head in range(KVH):
        part = keys[:, head * HD : (head + 1) * HD]
        out_ref[:, head * HD : (head + 1) * HD] = (
            part * cosines + pltpu.roll(part, HD // 2, 1) * sines
        ).astype(jnp.bfloat16)
    out_ref[:, KVH * HD :] = values.astype(jnp.bfloat16)


def exchange(value, axes, count, shift):
    return lax.ppermute(value, axes, [(i, i ^ shift) for i in range(count)])


def sum_on_cube(own, taken, shard):
    width, half = own.shape
    f32, bf16 = jnp.float32, jnp.bfloat16
    shape = jax.ShapeDtypeStruct
    rows = shard // 2
    kept, *given = call(
        pair_kernel,
        (shape((4, rows, half), f32),) + (shape((4, rows, half), bf16),) * 3,
        (own, taken),
    )
    pair_done = kept
    taken = [
        exchange(given[0], ("outer", "fsdp"), 16, 9),
        exchange(given[1], "outer", 2, 1),
        exchange(given[2], "fsdp", 8, 1),
    ]
    first_xy, second_xy, third_xy = taken
    kept, *given = call(
        z_kernel,
        (shape((rows, half), f32),) + (shape((rows, half), bf16),) * 3,
        (kept, *taken),
    )
    taken = [exchange(given[i], "fsdp", 8, 2 * i + 2) for i in range(3)]
    mine = call(last_kernel, shape((rows, half), bf16), (kept, *taken))
    return mine, (pair_done, pair_done, kept, mine)


def gather_on_cube(folded, steps):
    shard, half = folded.shape
    shape = jax.ShapeDtypeStruct

    def over(part, shift):
        return exchange(part, "fsdp", 8, shift)

    def stack(*parts, after):
        out = shape((len(parts), shard, half), folded.dtype)
        return call(stack_kernel, out, parts, after=after)

    near, far = over(folded, 2), over(folded, 4)
    both = over(stack(far, after=steps[0])[0], 2)
    low = stack(folded, near, after=steps[1])
    high = stack(far, both, after=steps[2])
    shifts = (0, 2, 4, 6, 1, 3, 5, 7)
    return call(
        functools.partial(order_kernel, shifts),
        shape((8 * shard, half), folded.dtype),
        (low, high, over(low, 1), over(high, 1)),
        after=steps[3],
    )


def body(outer, members, tokens, gain, kv_weight, positions, cotangent, counts, ratios):
    domains = 2 * outer
    rows, width = tokens.shape
    shard, columns = kv_weight.shape
    half = columns // 2
    f32, bf16 = jnp.float32, jnp.bfloat16
    shape = jax.ShapeDtypeStruct
    on_cube = outer == 2 and members == 8 and shard % 32 == 0

    exponents = np.arange(HD, dtype=np.float64) % (HD // 2) * (2.0 / HD)
    frequency = jnp.asarray(np.power(1000000.0, -exponents).astype(np.float32))
    normed, cosines, sines, own, given, folded = call(
        backward_kernel,
        (
            shape((rows, width), bf16),
            shape((rows, HD), f32),
            shape((rows, HD), f32),
            shape((width, half), f32),
            shape((width, half), bf16),
            shape((shard, half), bf16),
        ),
        (
            positions.reshape(rows // 128, 128),
            frequency.reshape(1, HD),
            counts,
            ratios.reshape(1, domains),
            cotangent,
            tokens,
            gain,
            kv_weight,
        ),
        fetched=8,
    )
    taken = exchange(given, "core", 2, 1)
    if on_cube:
        mine, steps = sum_on_cube(own, taken, shard)
        own_half = gather_on_cube(folded, steps)
        sums = [mine] + [exchange(mine, ("outer", "core"), 4, i) for i in (1, 2, 3)]
    else:
        pair = own + taken.astype(f32)
        pair = lax.psum_scatter(pair, "fsdp", scatter_dimension=0, tiled=True)
        mine = lax.psum(pair, "outer")
        own_half = lax.all_gather(folded, "fsdp", axis=0, tiled=True)
        sums = [mine, exchange(mine, "core", 2, 1)]
    other_half = exchange(own_half, "core", 2, 1)
    keys_out = call(
        forward_kernel,
        shape((rows, columns), bf16),
        (normed, own_half, other_half, cosines, sines),
        after=mine,
    )
    weight_grad, gain_grad = call(
        finish_kernel,
        (shape((shard, columns), f32), shape((shard,), f32)),
        (counts, gain, kv_weight, *sums),
        scratch=[pltpu.VMEM((shard, columns), f32)],
        after=keys_out,
        in_hbm=True,
    )
    return (keys_out, weight_grad, gain_grad)


def solution(mesh):
    domains, members = mesh.shape["dom"], mesh.shape["fsdp"]
    outer = domains // 2
    split = Mesh(mesh.devices.reshape(outer, 2, members), EVERY)
    return jax.shard_map(
        functools.partial(body, outer, members),
        mesh=split,
        in_specs=(
            P(EVERY, None),
            P("fsdp"),
            P("fsdp", None),
            P(EVERY),
            P(EVERY, None),
            P(),
            P(),
        ),
        out_specs=(P(EVERY, None), P("fsdp", None), P("fsdp")),
        check_vma=False,
    )
```

```python
import functools

import jax
import jax.numpy as jnp
import numpy as np
from jax import lax
from jax.experimental import pallas as pl
from jax.experimental.pallas import tpu as pltpu
from jax.sharding import Mesh
from jax.sharding import PartitionSpec as P

KVH = 2
HD = 128
BLOCK = 128
CHUNK = 384
EVERY = ("outer", "core", "fsdp")
VMEM_BYTES = 32 * 1024 * 1024


def to_column(line):
    n = line.shape[1]
    rows = lax.broadcasted_iota(jnp.int32, (n, n), 0)
    lanes = lax.broadcasted_iota(jnp.int32, (n, n), 1)
    spread = jnp.broadcast_to(line, (n, n))
    return jnp.sum(jnp.where(rows == lanes, spread, 0.0), axis=1, keepdims=True)


def to_line(column):
    n = column.shape[0]
    rows = lax.broadcasted_iota(jnp.int32, (n, n), 0)
    lanes = lax.broadcasted_iota(jnp.int32, (n, n), 1)
    spread = jnp.broadcast_to(column, (n, n))
    return jnp.sum(jnp.where(rows == lanes, spread, 0.0), axis=0, keepdims=True)


def sine_cosine(angles):
    turns = jnp.floor(angles * (2.0 / np.pi) + 0.5)
    rest = angles - turns * 1.5703125
    rest = rest - turns * 4.837512969970703125e-4
    rest = rest - turns * 7.54978995489188216e-8
    square = rest * rest
    sine = (-1.9515295891e-4 * square + 8.3321608736e-3) * square - 1.6666654611e-1
    sine = sine * square * rest + rest
    cosine = (2.443315711809948e-5 * square - 1.388731625493765e-3) * square
    cosine = (cosine + 4.166664568298827e-2) * square * square - 0.5 * square + 1.0
    quarter = turns.astype(jnp.int32) & 3
    odd = (quarter & 1) == 1
    sines, cosines = jnp.where(odd, cosine, sine), jnp.where(odd, sine, cosine)
    sines = jnp.where(quarter >= 2, -sines, sines)
    cosines = jnp.where(((quarter + 1) & 2) == 2, -cosines, cosines)
    return sines, cosines


def transposed_dot(left, right):
    return lax.dot_general(
        left, right, (((0,), (0,)), ((), ())), preferred_element_type=jnp.float32
    )


def full_sum(values):
    return jnp.sum(jnp.sum(values, axis=1, keepdims=True), axis=0, keepdims=True)


def fetch(sources, buffers, semaphores):
    copies = []
    for i, (source, buffer) in enumerate(zip(sources, buffers)):
        copy = pltpu.make_async_copy(source, buffer, semaphores.at[i])
        copy.start()
        copies.append(copy)
    return copies


def call(kernel, out_shape, args, after=None, in_hbm=False, fetched=0, scratch=(), cost=1000000):
    count = len(args)
    args = [
        pltpu.with_memory_space_constraint(arg, pltpu.HBM) if i < fetched else arg
        for i, arg in enumerate(args)
    ]
    spaces = [pl.ANY] * fetched + [pltpu.VMEM] * (count - fetched)
    run = kernel
    if after is not None:
        if in_hbm:
            after = pltpu.with_memory_space_constraint(after, pltpu.HBM)
        args, spaces = args + [after], spaces + [pl.ANY]

        def run(*refs):
            kernel(*refs[:count], *refs[count + 1 :])

    scratch = list(scratch) + [pltpu.VMEM(arg.shape, arg.dtype) for arg in args[:fetched]]
    if fetched:
        scratch.append(pltpu.SemaphoreType.DMA((fetched,)))
    return pl.pallas_call(
        run,
        out_shape=out_shape,
        in_specs=[pl.BlockSpec(memory_space=space) for space in spaces],
        scratch_shapes=scratch,
        out_specs=jax.tree.map(lambda _: pl.BlockSpec(memory_space=pltpu.VMEM), out_shape),
        compiler_params=pltpu.CompilerParams(vmem_limit_bytes=VMEM_BYTES),
        cost_estimate=pl.CostEstimate(flops=0, bytes_accessed=cost, transcendentals=0),
    )(*args)


def stack_kernel(*refs):
    for i, part_ref in enumerate(refs[:-1]):
        refs[-1][i] = part_ref[...]


def order_kernel(shifts, *refs):
    out_ref = refs[-1]
    rows = refs[0].shape[1]
    member = lax.axis_index("fsdp")
    parts = [part_ref.at[i] for part_ref in refs[:-1] for i in range(part_ref.shape[0])]
    for shift, part_ref in zip(shifts, parts):
        out_ref[aligned(jnp.bitwise_xor(member, shift), rows), :] = part_ref[...]


def backward_kernel(
    positions_hbm, frequency_hbm, counts_hbm, ratios_hbm, cotangent_hbm, tokens_hbm,
    gain_hbm, weight_hbm,
    normed_ref, cosines_ref, sines_ref, both_ref, given_ref, folded_ref,
    positions_ref, frequency_ref, counts_ref, ratios_ref, cotangent_ref, tokens_ref,
    gain_ref, weight_ref,
    semaphores,
):
    copies = fetch(
        (
            positions_hbm, frequency_hbm, counts_hbm, ratios_hbm, cotangent_hbm, tokens_hbm,
            gain_hbm, weight_hbm,
        ),
        (
            positions_ref, frequency_ref, counts_ref, ratios_ref, cotangent_ref, tokens_ref,
            gain_ref, weight_ref,
        ),
        semaphores,
    )
    rows, width = tokens_ref.shape
    core = lax.axis_index("core")
    domain = lax.axis_index("outer") * 2 + core
    member = lax.axis_index("fsdp")

    for copy in copies[:5]:
        copy.wait()
    lines = positions_ref[...].astype(jnp.float32)
    lanes = lax.broadcasted_iota(jnp.int32, (lines.shape[1], HD), 1)
    left = lanes < HD // 2
    first, second = to_column(lines[0:1, :]), to_column(lines[1:2, :])
    sines, cosines = sine_cosine(jnp.where(left, first, second) * frequency_ref[...])
    turned_sines, turned_cosines = pltpu.roll(sines, HD // 2, 1), pltpu.roll(cosines, HD // 2, 1)
    cosines = jnp.concatenate(
        [jnp.where(left, cosines, turned_cosines), jnp.where(left, turned_cosines, cosines)]
    )
    sines = jnp.concatenate(
        [jnp.where(left, -sines, turned_sines), jnp.where(left, -turned_sines, sines)]
    )
    cosines_ref[...] = cosines
    sines_ref[...] = sines

    counts = counts_ref[...].astype(jnp.float32)
    ratios = ratios_ref[...].astype(jnp.float32)
    at_domain = lax.broadcasted_iota(jnp.int32, counts.shape, 0) == domain
    at_member = lax.broadcasted_iota(jnp.int32, counts.shape, 1) == member
    ratio_at = lax.broadcasted_iota(jnp.int32, ratios.shape, 1) == domain
    live_total = full_sum(counts) * float(BLOCK)
    own_rows = full_sum(jnp.where(at_domain, counts, 0.0)) * float(BLOCK)
    own_live = full_sum(jnp.where(at_domain & at_member, counts, 0.0)) * float(BLOCK)
    own_ratio = full_sum(jnp.where(ratio_at, ratios, 0.0))
    factor = own_ratio / full_sum(ratios) * live_total / own_rows
    row_ids = lax.broadcasted_iota(jnp.int32, (rows, 1), 0).astype(jnp.float32)
    row_factor = jnp.where(row_ids < own_live, factor, 0.0)

    weighted = cotangent_ref[...].astype(jnp.float32) * row_factor
    key_width = KVH * HD
    turned = []
    for head in range(KVH):
        part = weighted[:, head * HD : (head + 1) * HD]
        turned.append(part * cosines - pltpu.roll(part, HD // 2, 1) * sines)
    keys = jnp.concatenate(turned, axis=1).astype(jnp.bfloat16)
    values = weighted[:, key_width:].astype(jnp.bfloat16)
    keep = jnp.where(core == 0, keys, values)
    give = jnp.where(core == 0, values, keys)
    half = keep.shape[1]
    both_ref[:, :half] = keep
    both_ref[:, half:] = give

    copies[5].wait()
    step = 32
    for start in range(0, rows, step):
        block = tokens_ref[start : start + step, :].astype(jnp.float32)
        mean_square = jnp.sum(block * block, axis=1, keepdims=True) * (1.0 / width)
        normed_ref[start : start + step, :] = (
            block * lax.rsqrt(mean_square + 1e-06)
        ).astype(jnp.bfloat16)

    for start in range(0, given_ref.shape[0], CHUNK):
        at = slice(start, start + CHUNK)
        given_ref[at, :] = transposed_dot(normed_ref[:, at], give).astype(jnp.bfloat16)

    columns = pl.ds(pl.multiple_of(core * half, half), half)
    copies[6].wait()
    gains = to_column(gain_ref[...].astype(jnp.float32).reshape(1, -1))
    copies[7].wait()
    folded = weight_ref[:, columns].astype(jnp.float32) * gains
    folded_ref[...] = folded.astype(jnp.bfloat16)


def rest_kernel(normed_ref, both_ref, own_ref, given_ref):
    width, half = own_ref.shape
    done = width - given_ref.shape[0]
    keep, both = both_ref[:, :half], both_ref[...]
    for start in range(0, width, CHUNK):
        at = slice(start, start + CHUNK)
        if start < done:
            own_ref[at, :] = transposed_dot(normed_ref[:, at], keep)
            continue
        result = transposed_dot(normed_ref[:, at], both)
        own_ref[at, :] = result[:, :half]
        given_ref[start - done : start - done + CHUNK, :] = result[:, half:].astype(jnp.bfloat16)


def aligned(index, size):
    return pl.ds(pl.multiple_of(index * size, size), size)


def total(kept, taken):
    return kept + taken.astype(jnp.float32)


def pair_kernel(own_ref, first_ref, second_ref, *out_refs):
    count, rows, _ = out_refs[0].shape
    first_count = first_ref.shape[0] // (4 * rows)
    y, x = lax.axis_index("outer"), lax.axis_index("fsdp") % 2
    for (away_y, away_x), out_ref in zip(((0, 0), (1, 1), (1, 0), (0, 1)), out_refs):
        to_y, to_x = jnp.bitwise_xor(y, away_y), jnp.bitwise_xor(x, away_x)
        for i in range(count):
            at = aligned(4 * i + 2 * to_x + to_y, rows)
            in_first = i < first_count
            taken_ref = first_ref if in_first else second_ref
            taken_at = 4 * (i if in_first else i - first_count) + 2 * to_x + to_y
            taken_at = aligned(taken_at, rows)
            out_ref[i] = total(own_ref[at, :], taken_ref[taken_at, :]).astype(out_ref.dtype)


def z_kernel(kept_ref, first_ref, second_ref, third_ref, *out_refs):
    z = lax.axis_index("fsdp") // 2
    for shift, out_ref in enumerate(out_refs):
        at = jnp.bitwise_xor(z, shift)
        result = total(kept_ref[at], first_ref[at])
        result = total(total(result, second_ref[at]), third_ref[at])
        out_ref[...] = result.astype(out_ref.dtype)


def last_kernel(own_ref, *refs):
    result = own_ref[...]
    for taken_ref in refs[:-1]:
        result = total(result, taken_ref[...])
    refs[-1][...] = result.astype(jnp.bfloat16)


def finish_kernel(counts_ref, gain_ref, weight_ref, *refs):
    parts, (weight_grad_ref, gain_grad_ref, sum_ref) = refs[:-3], refs[-3:]
    rows, half = parts[0].shape
    y, core = lax.axis_index("outer"), lax.axis_index("core")
    live_total = full_sum(counts_ref[...].astype(jnp.float32)) * float(BLOCK)
    scale = 1.0 / jnp.sqrt(live_total)
    gains = to_column(gain_ref[...].astype(jnp.float32).reshape(1, -1)) * scale
    shifts = (0, 1) if len(parts) == 2 else (0, 3, 2, 1)
    for shift, part_ref in zip(shifts, parts):
        at_y = 0 if len(parts) == 2 else jnp.bitwise_xor(y, shift // 2)
        at = jnp.bitwise_xor(core, shift % 2)
        sum_ref[aligned(at_y, rows), aligned(at, half)] = part_ref[...].astype(jnp.float32)
    result = sum_ref[...]
    weight_grad_ref[...] = result * gains
    dots = jnp.sum(result * weight_ref[...].astype(jnp.float32), axis=1, keepdims=True)
    gain_grad_ref[...] = to_line(dots * scale).reshape(-1)


def forward_kernel(normed_ref, own_ref, other_ref, cosines_ref, sines_ref, out_ref):
    core = lax.axis_index("core")
    normed = normed_ref[...]
    own = jnp.dot(normed, own_ref[...], preferred_element_type=jnp.float32)
    other = jnp.dot(normed, other_ref[...], preferred_element_type=jnp.float32)
    keys = jnp.where(core == 0, own, other)
    values = jnp.where(core == 0, other, own)
    cosines, sines = cosines_ref[...], sines_ref[...]
    for head in range(KVH):
        part = keys[:, head * HD : (head + 1) * HD]
        out_ref[:, head * HD : (head + 1) * HD] = (
            part * cosines + pltpu.roll(part, HD // 2, 1) * sines
        ).astype(jnp.bfloat16)
    out_ref[:, KVH * HD :] = values.astype(jnp.bfloat16)


def exchange(value, axes, count, shift):
    return lax.ppermute(value, axes, [(i, i ^ shift) for i in range(count)])


def sum_on_cube(own, first, second, shard):
    width, half = own.shape
    f32, bf16 = jnp.float32, jnp.bfloat16
    shape = jax.ShapeDtypeStruct
    rows = shard // 2
    kept, *given = call(
        pair_kernel,
        (shape((4, rows, half), f32),) + (shape((4, rows, half), bf16),) * 3,
        (own, first, second),
    )
    pair_done = kept
    taken = [
        exchange(given[0], ("outer", "fsdp"), 16, 9),
        exchange(given[1], "outer", 2, 1),
        exchange(given[2], "fsdp", 8, 1),
    ]
    first_xy, second_xy, third_xy = taken
    kept, *given = call(
        z_kernel,
        (shape((rows, half), f32),) + (shape((rows, half), bf16),) * 3,
        (kept, *taken),
    )
    taken = [exchange(given[i], "fsdp", 8, 2 * i + 2) for i in range(3)]
    mine = call(last_kernel, shape((rows, half), bf16), (kept, *taken))
    return mine, (pair_done, pair_done, kept, mine)


def gather_on_cube(folded, steps):
    shard, half = folded.shape
    shape = jax.ShapeDtypeStruct

    def over(part, shift):
        return exchange(part, "fsdp", 8, shift)

    def stack(*parts, after):
        out = shape((len(parts), shard, half), folded.dtype)
        return call(stack_kernel, out, parts, after=after)

    near, far = over(folded, 2), over(folded, 4)
    both = over(stack(far, after=steps[0])[0], 2)
    low = stack(folded, near, after=steps[1])
    high = stack(far, both, after=steps[2])
    shifts = (0, 2, 4, 6, 1, 3, 5, 7)
    return call(
        functools.partial(order_kernel, shifts),
        shape((8 * shard, half), folded.dtype),
        (low, high, over(low, 1), over(high, 1)),
        after=steps[3],
    )


def body(outer, members, tokens, gain, kv_weight, positions, cotangent, counts, ratios):
    domains = 2 * outer
    rows, width = tokens.shape
    shard, columns = kv_weight.shape
    half = columns // 2
    f32, bf16 = jnp.float32, jnp.bfloat16
    shape = jax.ShapeDtypeStruct
    on_cube = outer == 2 and members == 8 and shard % 32 == 0

    exponents = np.arange(HD, dtype=np.float64) % (HD // 2) * (2.0 / HD)
    frequency = jnp.asarray(np.power(1000000.0, -exponents).astype(np.float32))
    normed, cosines, sines, both, given, folded = call(
        backward_kernel,
        (
            shape((rows, width), bf16),
            shape((rows, HD), f32),
            shape((rows, HD), f32),
            shape((rows, columns), bf16),
            shape((width - width // 4, half), bf16),
            shape((shard, half), bf16),
        ),
        (
            positions.reshape(rows // 128, 128),
            frequency.reshape(1, HD),
            counts,
            ratios.reshape(1, domains),
            cotangent,
            tokens,
            gain,
            kv_weight,
        ),
        fetched=8,
    )
    first = exchange(given, "core", 2, 1)
    own, given = call(
        rest_kernel, (shape((width, half), f32), shape((width // 4, half), bf16)), (normed, both)
    )
    second = exchange(given, "core", 2, 1)
    if on_cube:
        mine, steps = sum_on_cube(own, first, second, shard)
        own_half = gather_on_cube(folded, steps)
        sums = [mine] + [exchange(mine, ("outer", "core"), 4, i) for i in (3, 2, 1)]
    else:
        pair = own + jnp.concatenate([first, second]).astype(f32)
        pair = lax.psum_scatter(pair, "fsdp", scatter_dimension=0, tiled=True)
        mine = lax.psum(pair, "outer")
        own_half = lax.all_gather(folded, "fsdp", axis=0, tiled=True)
        sums = [mine, exchange(mine, "core", 2, 1)]
    other_half = exchange(own_half, "core", 2, 1)
    keys_out = call(
        forward_kernel,
        shape((rows, columns), bf16),
        (normed, own_half, other_half, cosines, sines),
        after=mine,
    )
    weight_grad, gain_grad = call(
        finish_kernel,
        (shape((shard, columns), f32), shape((shard,), f32)),
        (counts, gain, kv_weight, *sums),
        scratch=[pltpu.VMEM((shard, columns), f32)],
        after=keys_out,
        in_hbm=True,
    )
    return (keys_out, weight_grad, gain_grad)


def solution(mesh):
    domains, members = mesh.shape["dom"], mesh.shape["fsdp"]
    outer = domains // 2
    split = Mesh(mesh.devices.reshape(outer, 2, members), EVERY)
    return jax.shard_map(
        functools.partial(body, outer, members),
        mesh=split,
        in_specs=(
            P(EVERY, None),
            P("fsdp"),
            P("fsdp", None),
            P(EVERY),
            P(EVERY, None),
            P(),
            P(),
        ),
        out_specs=(P(EVERY, None), P("fsdp", None), P("fsdp")),
        check_vma=False,
    )
```

```python
import functools

import jax
import jax.numpy as jnp
import numpy as np
from jax import lax
from jax.experimental import pallas as pl
from jax.experimental.pallas import tpu as pltpu
from jax.sharding import Mesh
from jax.sharding import PartitionSpec as P

KVH = 2
HD = 128
BLOCK = 128
CHUNK = 384
EVERY = ("outer", "core", "fsdp")
VMEM_BYTES = 32 * 1024 * 1024


def to_column(line):
    n = line.shape[1]
    rows = lax.broadcasted_iota(jnp.int32, (n, n), 0)
    lanes = lax.broadcasted_iota(jnp.int32, (n, n), 1)
    spread = jnp.broadcast_to(line, (n, n))
    return jnp.sum(jnp.where(rows == lanes, spread, 0.0), axis=1, keepdims=True)


def to_line(column):
    n = column.shape[0]
    rows = lax.broadcasted_iota(jnp.int32, (n, n), 0)
    lanes = lax.broadcasted_iota(jnp.int32, (n, n), 1)
    spread = jnp.broadcast_to(column, (n, n))
    return jnp.sum(jnp.where(rows == lanes, spread, 0.0), axis=0, keepdims=True)


def sine_cosine(angles):
    turns = jnp.floor(angles * (2.0 / np.pi) + 0.5)
    rest = angles - turns * 1.5703125
    rest = rest - turns * 4.837512969970703125e-4
    rest = rest - turns * 7.54978995489188216e-8
    square = rest * rest
    sine = (-1.9515295891e-4 * square + 8.3321608736e-3) * square - 1.6666654611e-1
    sine = sine * square * rest + rest
    cosine = (2.443315711809948e-5 * square - 1.388731625493765e-3) * square
    cosine = (cosine + 4.166664568298827e-2) * square * square - 0.5 * square + 1.0
    quarter = turns.astype(jnp.int32) & 3
    odd = (quarter & 1) == 1
    sines, cosines = jnp.where(odd, cosine, sine), jnp.where(odd, sine, cosine)
    sines = jnp.where(quarter >= 2, -sines, sines)
    cosines = jnp.where(((quarter + 1) & 2) == 2, -cosines, cosines)
    return sines, cosines


def transposed_dot(left, right):
    return lax.dot_general(
        left, right, (((0,), (0,)), ((), ())), preferred_element_type=jnp.float32
    )


def full_sum(values):
    return jnp.sum(jnp.sum(values, axis=1, keepdims=True), axis=0, keepdims=True)


def fetch(sources, buffers, semaphores):
    copies = []
    for i, (source, buffer) in enumerate(zip(sources, buffers)):
        copy = pltpu.make_async_copy(source, buffer, semaphores.at[i])
        copy.start()
        copies.append(copy)
    return copies


def call(kernel, out_shape, args, after=None, in_hbm=False, fetched=0, scratch=(), cost=1000000):
    count = len(args)
    args = [
        pltpu.with_memory_space_constraint(arg, pltpu.HBM) if i < fetched else arg
        for i, arg in enumerate(args)
    ]
    spaces = [pl.ANY] * fetched + [pltpu.VMEM] * (count - fetched)
    run = kernel
    if after is not None:
        if in_hbm:
            after = pltpu.with_memory_space_constraint(after, pltpu.HBM)
        args, spaces = args + [after], spaces + [pl.ANY]

        def run(*refs):
            kernel(*refs[:count], *refs[count + 1 :])

    scratch = list(scratch) + [pltpu.VMEM(arg.shape, arg.dtype) for arg in args[:fetched]]
    if fetched:
        scratch.append(pltpu.SemaphoreType.DMA((fetched,)))
    return pl.pallas_call(
        run,
        out_shape=out_shape,
        in_specs=[pl.BlockSpec(memory_space=space) for space in spaces],
        scratch_shapes=scratch,
        out_specs=jax.tree.map(lambda _: pl.BlockSpec(memory_space=pltpu.VMEM), out_shape),
        compiler_params=pltpu.CompilerParams(vmem_limit_bytes=VMEM_BYTES),
        cost_estimate=pl.CostEstimate(flops=0, bytes_accessed=cost, transcendentals=0),
    )(*args)


def stack_kernel(*refs):
    for i, part_ref in enumerate(refs[:-1]):
        refs[-1][i] = part_ref[...]


def bundle_kernel(shifts, mine_ref, *refs):
    out_ref = refs[-1]
    rows = refs[0].shape[1]
    member = lax.axis_index("fsdp")
    parts = [part_ref.at[i] for part_ref in refs[:-1] for i in range(part_ref.shape[0])]
    for shift, part_ref in zip(shifts, parts):
        out_ref[aligned(jnp.bitwise_xor(member, shift), rows), :] = part_ref[...]
    out_ref[len(parts) * rows :, :] = mine_ref[...]


def backward_kernel(
    positions_hbm, frequency_hbm, counts_hbm, ratios_hbm, cotangent_hbm, tokens_hbm,
    gain_hbm, weight_hbm,
    normed_ref, cosines_ref, sines_ref, both_ref, given_ref, folded_ref,
    positions_ref, frequency_ref, counts_ref, ratios_ref, cotangent_ref, tokens_ref,
    gain_ref, weight_ref,
    semaphores,
):
    copies = fetch(
        (
            positions_hbm, frequency_hbm, counts_hbm, ratios_hbm, cotangent_hbm, tokens_hbm,
            gain_hbm, weight_hbm,
        ),
        (
            positions_ref, frequency_ref, counts_ref, ratios_ref, cotangent_ref, tokens_ref,
            gain_ref, weight_ref,
        ),
        semaphores,
    )
    rows, width = tokens_ref.shape
    core = lax.axis_index("core")
    domain = lax.axis_index("outer") * 2 + core
    member = lax.axis_index("fsdp")

    for copy in copies[:5]:
        copy.wait()
    lines = positions_ref[...].astype(jnp.float32)
    lanes = lax.broadcasted_iota(jnp.int32, (lines.shape[1], HD), 1)
    left = lanes < HD // 2
    first, second = to_column(lines[0:1, :]), to_column(lines[1:2, :])
    sines, cosines = sine_cosine(jnp.where(left, first, second) * frequency_ref[...])
    turned_sines, turned_cosines = pltpu.roll(sines, HD // 2, 1), pltpu.roll(cosines, HD // 2, 1)
    cosines = jnp.concatenate(
        [jnp.where(left, cosines, turned_cosines), jnp.where(left, turned_cosines, cosines)]
    )
    sines = jnp.concatenate(
        [jnp.where(left, -sines, turned_sines), jnp.where(left, -turned_sines, sines)]
    )
    cosines_ref[...] = cosines
    sines_ref[...] = sines

    counts = counts_ref[...].astype(jnp.float32)
    ratios = ratios_ref[...].astype(jnp.float32)
    at_domain = lax.broadcasted_iota(jnp.int32, counts.shape, 0) == domain
    at_member = lax.broadcasted_iota(jnp.int32, counts.shape, 1) == member
    ratio_at = lax.broadcasted_iota(jnp.int32, ratios.shape, 1) == domain
    live_total = full_sum(counts) * float(BLOCK)
    own_rows = full_sum(jnp.where(at_domain, counts, 0.0)) * float(BLOCK)
    own_live = full_sum(jnp.where(at_domain & at_member, counts, 0.0)) * float(BLOCK)
    own_ratio = full_sum(jnp.where(ratio_at, ratios, 0.0))
    factor = own_ratio / full_sum(ratios) * live_total / own_rows
    row_ids = lax.broadcasted_iota(jnp.int32, (rows, 1), 0).astype(jnp.float32)
    row_factor = jnp.where(row_ids < own_live, factor, 0.0)

    weighted = cotangent_ref[...].astype(jnp.float32) * row_factor
    key_width = KVH * HD
    turned = []
    for head in range(KVH):
        part = weighted[:, head * HD : (head + 1) * HD]
        turned.append(part * cosines - pltpu.roll(part, HD // 2, 1) * sines)
    keys = jnp.concatenate(turned, axis=1).astype(jnp.bfloat16)
    values = weighted[:, key_width:].astype(jnp.bfloat16)
    keep = jnp.where(core == 0, keys, values)
    give = jnp.where(core == 0, values, keys)
    half = keep.shape[1]
    both_ref[:, :half] = keep
    both_ref[:, half:] = give

    copies[5].wait()
    step = 32
    for start in range(0, rows, step):
        block = tokens_ref[start : start + step, :].astype(jnp.float32)
        mean_square = jnp.sum(block * block, axis=1, keepdims=True) * (1.0 / width)
        normed_ref[start : start + step, :] = (
            block * lax.rsqrt(mean_square + 1e-06)
        ).astype(jnp.bfloat16)

    for start in range(0, given_ref.shape[0], CHUNK):
        at = slice(start, start + CHUNK)
        given_ref[at, :] = transposed_dot(normed_ref[:, at], give).astype(jnp.bfloat16)

    columns = pl.ds(pl.multiple_of(core * half, half), half)
    copies[6].wait()
    gains = to_column(gain_ref[...].astype(jnp.float32).reshape(1, -1))
    copies[7].wait()
    folded = weight_ref[:, columns].astype(jnp.float32) * gains
    folded_ref[...] = folded.astype(jnp.bfloat16)


def rest_kernel(normed_ref, both_ref, own_ref, given_ref):
    width, half = own_ref.shape
    done = width - given_ref.shape[0]
    keep, both = both_ref[:, :half], both_ref[...]
    for start in range(0, width, CHUNK):
        at = slice(start, start + CHUNK)
        if start < done:
            own_ref[at, :] = transposed_dot(normed_ref[:, at], keep)
            continue
        result = transposed_dot(normed_ref[:, at], both)
        own_ref[at, :] = result[:, :half]
        given_ref[start - done : start - done + CHUNK, :] = result[:, half:].astype(jnp.bfloat16)


def aligned(index, size):
    return pl.ds(pl.multiple_of(index * size, size), size)


def total(kept, taken):
    return kept + taken.astype(jnp.float32)


def pair_kernel(own_ref, first_ref, second_ref, *out_refs):
    count, rows, _ = out_refs[0].shape
    first_count = first_ref.shape[0] // (4 * rows)
    y, x = lax.axis_index("outer"), lax.axis_index("fsdp") % 2
    for (away_y, away_x), out_ref in zip(((0, 0), (1, 1), (1, 0), (0, 1)), out_refs):
        to_y, to_x = jnp.bitwise_xor(y, away_y), jnp.bitwise_xor(x, away_x)
        for i in range(count):
            at = aligned(4 * i + 2 * to_x + to_y, rows)
            in_first = i < first_count
            taken_ref = first_ref if in_first else second_ref
            taken_at = 4 * (i if in_first else i - first_count) + 2 * to_x + to_y
            taken_at = aligned(taken_at, rows)
            out_ref[i] = total(own_ref[at, :], taken_ref[taken_at, :]).astype(out_ref.dtype)


def z_kernel(kept_ref, first_ref, second_ref, third_ref, *out_refs):
    z = lax.axis_index("fsdp") // 2
    for shift, out_ref in enumerate(out_refs):
        at = jnp.bitwise_xor(z, shift)
        result = total(kept_ref[at], first_ref[at])
        result = total(total(result, second_ref[at]), third_ref[at])
        out_ref[...] = result.astype(out_ref.dtype)


def last_kernel(own_ref, *refs):
    result = own_ref[...]
    for taken_ref in refs[:-1]:
        result = total(result, taken_ref[...])
    refs[-1][...] = result.astype(jnp.bfloat16)


def finish_kernel(counts_ref, gain_ref, weight_ref, *refs):
    parts, (weight_grad_ref, gain_grad_ref, sum_ref) = refs[:-3], refs[-3:]
    rows, half = parts[0].shape
    y, core = lax.axis_index("outer"), lax.axis_index("core")
    live_total = full_sum(counts_ref[...].astype(jnp.float32)) * float(BLOCK)
    scale = 1.0 / jnp.sqrt(live_total)
    gains = to_column(gain_ref[...].astype(jnp.float32).reshape(1, -1)) * scale
    shifts = (0, 1) if len(parts) == 2 else (0, 1, 2, 3)
    for shift, part_ref in zip(shifts, parts):
        at_y = 0 if len(parts) == 2 else jnp.bitwise_xor(y, shift // 2)
        at = jnp.bitwise_xor(core, shift % 2)
        tail = slice(part_ref.shape[0] - rows, None)
        sum_ref[aligned(at_y, rows), aligned(at, half)] = part_ref[tail, :].astype(jnp.float32)
    result = sum_ref[...]
    weight_grad_ref[...] = result * gains
    dots = jnp.sum(result * weight_ref[...].astype(jnp.float32), axis=1, keepdims=True)
    gain_grad_ref[...] = to_line(dots * scale).reshape(-1)


def forward_kernel(normed_ref, own_ref, other_ref, cosines_ref, sines_ref, out_ref):
    core = lax.axis_index("core")
    normed = normed_ref[...]
    width = normed.shape[1]
    own = jnp.dot(normed, own_ref[:width, :], preferred_element_type=jnp.float32)
    other = jnp.dot(normed, other_ref[:width, :], preferred_element_type=jnp.float32)
    keys = jnp.where(core == 0, own, other)
    values = jnp.where(core == 0, other, own)
    cosines, sines = cosines_ref[...], sines_ref[...]
    for head in range(KVH):
        part = keys[:, head * HD : (head + 1) * HD]
        out_ref[:, head * HD : (head + 1) * HD] = (
            part * cosines + pltpu.roll(part, HD // 2, 1) * sines
        ).astype(jnp.bfloat16)
    out_ref[:, KVH * HD :] = values.astype(jnp.bfloat16)


def exchange(value, axes, count, shift):
    return lax.ppermute(value, axes, [(i, i ^ shift) for i in range(count)])


def sum_on_cube(own, first, second, shard):
    width, half = own.shape
    f32, bf16 = jnp.float32, jnp.bfloat16
    shape = jax.ShapeDtypeStruct
    rows = shard // 2
    kept, *given = call(
        pair_kernel,
        (shape((4, rows, half), f32),) + (shape((4, rows, half), bf16),) * 3,
        (own, first, second),
    )
    pair_done = kept
    taken = [
        exchange(given[0], ("outer", "fsdp"), 16, 9),
        exchange(given[1], "outer", 2, 1),
        exchange(given[2], "fsdp", 8, 1),
    ]
    first_xy, second_xy, third_xy = taken
    kept, *given = call(
        z_kernel,
        (shape((rows, half), f32),) + (shape((rows, half), bf16),) * 3,
        (kept, *taken),
    )
    taken = [exchange(given[i], "fsdp", 8, 2 * i + 2) for i in (1, 2, 0)]
    mine = call(last_kernel, shape((rows, half), bf16), (kept, *taken))
    return mine, (pair_done, pair_done, kept, mine)


def gather_on_cube(folded, steps):
    shard, half = folded.shape
    shape = jax.ShapeDtypeStruct

    def over(part, shift):
        return exchange(part, "fsdp", 8, shift)

    def stack(*parts, after):
        out = shape((len(parts), shard, half), folded.dtype)
        return call(stack_kernel, out, parts, after=after)

    near, far = over(folded, 2), over(folded, 4)
    both = over(stack(far, after=steps[0])[0], 2)
    low = stack(folded, near, after=steps[1])
    high = stack(far, both, after=steps[2])
    shifts = (0, 2, 4, 6, 1, 3, 5, 7)
    mine = steps[3]
    return call(
        functools.partial(bundle_kernel, shifts),
        shape((8 * shard + mine.shape[0], half), folded.dtype),
        (mine, low, high, over(low, 1), over(high, 1)),
    )


def body(outer, members, tokens, gain, kv_weight, positions, cotangent, counts, ratios):
    domains = 2 * outer
    rows, width = tokens.shape
    shard, columns = kv_weight.shape
    half = columns // 2
    f32, bf16 = jnp.float32, jnp.bfloat16
    shape = jax.ShapeDtypeStruct
    on_cube = outer == 2 and members == 8 and shard % 32 == 0

    exponents = np.arange(HD, dtype=np.float64) % (HD // 2) * (2.0 / HD)
    frequency = jnp.asarray(np.power(1000000.0, -exponents).astype(np.float32))
    normed, cosines, sines, both, given, folded = call(
        backward_kernel,
        (
            shape((rows, width), bf16),
            shape((rows, HD), f32),
            shape((rows, HD), f32),
            shape((rows, columns), bf16),
            shape((width - width // 4, half), bf16),
            shape((shard, half), bf16),
        ),
        (
            positions.reshape(rows // 128, 128),
            frequency.reshape(1, HD),
            counts,
            ratios.reshape(1, domains),
            cotangent,
            tokens,
            gain,
            kv_weight,
        ),
        fetched=8,
    )
    first = exchange(given, "core", 2, 1)
    own, given = call(
        rest_kernel, (shape((width, half), f32), shape((width // 4, half), bf16)), (normed, both)
    )
    second = exchange(given, "core", 2, 1)
    if on_cube:
        mine, steps = sum_on_cube(own, first, second, shard)
        own_half = gather_on_cube(folded, steps)
        other_half = exchange(own_half, "core", 2, 1)
        sums = [mine, other_half] + [exchange(mine, ("outer", "core"), 4, i) for i in (2, 3)]
    else:
        pair = own + jnp.concatenate([first, second]).astype(f32)
        pair = lax.psum_scatter(pair, "fsdp", scatter_dimension=0, tiled=True)
        mine = lax.psum(pair, "outer")
        own_half = lax.all_gather(folded, "fsdp", axis=0, tiled=True)
        other_half = exchange(own_half, "core", 2, 1)
        sums = [mine, exchange(mine, "core", 2, 1)]
    keys_out = call(
        forward_kernel,
        shape((rows, columns), bf16),
        (normed, own_half, other_half, cosines, sines),
        after=mine,
    )
    weight_grad, gain_grad = call(
        finish_kernel,
        (shape((shard, columns), f32), shape((shard,), f32)),
        (counts, gain, kv_weight, *sums),
        scratch=[pltpu.VMEM((shard, columns), f32)],
        after=keys_out,
        in_hbm=True,
    )
    return (keys_out, weight_grad, gain_grad)


def solution(mesh):
    domains, members = mesh.shape["dom"], mesh.shape["fsdp"]
    outer = domains // 2
    split = Mesh(mesh.devices.reshape(outer, 2, members), EVERY)
    return jax.shard_map(
        functools.partial(body, outer, members),
        mesh=split,
        in_specs=(
            P(EVERY, None),
            P("fsdp"),
            P("fsdp", None),
            P(EVERY),
            P(EVERY, None),
            P(),
            P(),
        ),
        out_specs=(P(EVERY, None), P("fsdp", None), P("fsdp")),
        check_vma=False,
    )
```

```python
import functools

import jax
import jax.numpy as jnp
import numpy as np
from jax import lax
from jax.experimental import pallas as pl
from jax.experimental.pallas import tpu as pltpu
from jax.sharding import Mesh
from jax.sharding import PartitionSpec as P

KVH = 2
HD = 128
BLOCK = 128
CHUNK = 384
FLOPS = dict(cross=10**10, z=3 * 10**9, last=10**11, far=2 * 10**9, stack=10**10)
EVERY = ("outer", "core", "fsdp")
VMEM_BYTES = 32 * 1024 * 1024


def to_column(line):
    n = line.shape[1]
    rows = lax.broadcasted_iota(jnp.int32, (n, n), 0)
    lanes = lax.broadcasted_iota(jnp.int32, (n, n), 1)
    spread = jnp.broadcast_to(line, (n, n))
    return jnp.sum(jnp.where(rows == lanes, spread, 0.0), axis=1, keepdims=True)


def to_line(column):
    n = column.shape[0]
    rows = lax.broadcasted_iota(jnp.int32, (n, n), 0)
    lanes = lax.broadcasted_iota(jnp.int32, (n, n), 1)
    spread = jnp.broadcast_to(column, (n, n))
    return jnp.sum(jnp.where(rows == lanes, spread, 0.0), axis=0, keepdims=True)


def sine_cosine(angles):
    turns = jnp.floor(angles * (2.0 / np.pi) + 0.5)
    rest = angles - turns * 1.5703125
    rest = rest - turns * 4.837512969970703125e-4
    rest = rest - turns * 7.54978995489188216e-8
    square = rest * rest
    sine = (-1.9515295891e-4 * square + 8.3321608736e-3) * square - 1.6666654611e-1
    sine = sine * square * rest + rest
    cosine = (2.443315711809948e-5 * square - 1.388731625493765e-3) * square
    cosine = (cosine + 4.166664568298827e-2) * square * square - 0.5 * square + 1.0
    quarter = turns.astype(jnp.int32) & 3
    odd = (quarter & 1) == 1
    sines, cosines = jnp.where(odd, cosine, sine), jnp.where(odd, sine, cosine)
    sines = jnp.where(quarter >= 2, -sines, sines)
    cosines = jnp.where(((quarter + 1) & 2) == 2, -cosines, cosines)
    return sines, cosines


def transposed_dot(left, right):
    return lax.dot_general(
        left, right, (((0,), (0,)), ((), ())), preferred_element_type=jnp.float32
    )


def full_sum(values):
    return jnp.sum(jnp.sum(values, axis=1, keepdims=True), axis=0, keepdims=True)


def fetch(sources, buffers, semaphores):
    copies = []
    for i, (source, buffer) in enumerate(zip(sources, buffers)):
        copy = pltpu.make_async_copy(source, buffer, semaphores.at[i])
        copy.start()
        copies.append(copy)
    return copies


def call(kernel, out_shape, args, after=None, in_hbm=False, fetched=0, scratch=(), flops=0):
    count = len(args)
    args = [
        pltpu.with_memory_space_constraint(arg, pltpu.HBM) if i < fetched else arg
        for i, arg in enumerate(args)
    ]
    spaces = [pl.ANY] * fetched + [pltpu.VMEM] * (count - fetched)
    run = kernel
    if after is not None:
        if in_hbm:
            after = pltpu.with_memory_space_constraint(after, pltpu.HBM)
        args, spaces = args + [after], spaces + [pl.ANY]

        def run(*refs):
            kernel(*refs[:count], *refs[count + 1 :])

    scratch = list(scratch) + [pltpu.VMEM(arg.shape, arg.dtype) for arg in args[:fetched]]
    if fetched:
        scratch.append(pltpu.SemaphoreType.DMA((fetched,)))
    return pl.pallas_call(
        run,
        out_shape=out_shape,
        in_specs=[pl.BlockSpec(memory_space=space) for space in spaces],
        scratch_shapes=scratch,
        out_specs=jax.tree.map(lambda _: pl.BlockSpec(memory_space=pltpu.VMEM), out_shape),
        compiler_params=pltpu.CompilerParams(vmem_limit_bytes=VMEM_BYTES),
        cost_estimate=pl.CostEstimate(
            flops=flops, bytes_accessed=1000000, transcendentals=0
        ),
    )(*args)


def stack_kernel(*refs):
    for i, part_ref in enumerate(refs[:-1]):
        refs[-1][i] = part_ref[...]


def order_kernel(shifts, *refs):
    out_ref = refs[-1]
    rows, half = refs[0].shape[-2:]
    member = lax.axis_index("fsdp")
    parts = []
    for part_ref in refs[:-1]:
        count = part_ref.shape[0] if part_ref.ndim == 3 else 0
        parts += [part_ref.at[i] for i in range(count)] or [part_ref]
    for shift, part_ref in zip(shifts, parts):
        out_ref[aligned(jnp.bitwise_xor(member, shift), rows), :] = part_ref[...]


def backward_kernel(
    positions_hbm, frequency_hbm, counts_hbm, ratios_hbm, cotangent_hbm, tokens_hbm,
    gain_hbm, weight_hbm,
    normed_ref, cosines_ref, sines_ref, both_ref, given_ref, folded_ref,
    positions_ref, frequency_ref, counts_ref, ratios_ref, cotangent_ref, tokens_ref,
    gain_ref, weight_ref,
    semaphores,
):
    copies = fetch(
        (
            positions_hbm, frequency_hbm, counts_hbm, ratios_hbm, cotangent_hbm, tokens_hbm,
            gain_hbm, weight_hbm,
        ),
        (
            positions_ref, frequency_ref, counts_ref, ratios_ref, cotangent_ref, tokens_ref,
            gain_ref, weight_ref,
        ),
        semaphores,
    )
    rows, width = tokens_ref.shape
    core = lax.axis_index("core")
    domain = lax.axis_index("outer") * 2 + core
    member = lax.axis_index("fsdp")

    for copy in copies[:5]:
        copy.wait()
    lines = positions_ref[...].astype(jnp.float32)
    lanes = lax.broadcasted_iota(jnp.int32, (lines.shape[1], HD), 1)
    left = lanes < HD // 2
    first, second = to_column(lines[0:1, :]), to_column(lines[1:2, :])
    sines, cosines = sine_cosine(jnp.where(left, first, second) * frequency_ref[...])
    turned_sines, turned_cosines = pltpu.roll(sines, HD // 2, 1), pltpu.roll(cosines, HD // 2, 1)
    cosines = jnp.concatenate(
        [jnp.where(left, cosines, turned_cosines), jnp.where(left, turned_cosines, cosines)]
    )
    sines = jnp.concatenate(
        [jnp.where(left, -sines, turned_sines), jnp.where(left, -turned_sines, sines)]
    )
    cosines_ref[...] = cosines
    sines_ref[...] = sines

    counts = counts_ref[...].astype(jnp.float32)
    ratios = ratios_ref[...].astype(jnp.float32)
    at_domain = lax.broadcasted_iota(jnp.int32, counts.shape, 0) == domain
    at_member = lax.broadcasted_iota(jnp.int32, counts.shape, 1) == member
    ratio_at = lax.broadcasted_iota(jnp.int32, ratios.shape, 1) == domain
    live_total = full_sum(counts) * float(BLOCK)
    own_rows = full_sum(jnp.where(at_domain, counts, 0.0)) * float(BLOCK)
    own_live = full_sum(jnp.where(at_domain & at_member, counts, 0.0)) * float(BLOCK)
    own_ratio = full_sum(jnp.where(ratio_at, ratios, 0.0))
    factor = own_ratio / full_sum(ratios) * live_total / own_rows
    row_ids = lax.broadcasted_iota(jnp.int32, (rows, 1), 0).astype(jnp.float32)
    row_factor = jnp.where(row_ids < own_live, factor, 0.0)

    weighted = cotangent_ref[...].astype(jnp.float32) * row_factor
    key_width = KVH * HD
    turned = []
    for head in range(KVH):
        part = weighted[:, head * HD : (head + 1) * HD]
        turned.append(part * cosines - pltpu.roll(part, HD // 2, 1) * sines)
    keys = jnp.concatenate(turned, axis=1).astype(jnp.bfloat16)
    values = weighted[:, key_width:].astype(jnp.bfloat16)
    keep = jnp.where(core == 0, keys, values)
    give = jnp.where(core == 0, values, keys)
    half = keep.shape[1]
    both_ref[:, :half] = keep
    both_ref[:, half:] = give

    copies[5].wait()
    step = 32
    for start in range(0, rows, step):
        block = tokens_ref[start : start + step, :].astype(jnp.float32)
        mean_square = jnp.sum(block * block, axis=1, keepdims=True) * (1.0 / width)
        normed_ref[start : start + step, :] = (
            block * lax.rsqrt(mean_square + 1e-06)
        ).astype(jnp.bfloat16)

    for start in range(0, given_ref.shape[0], CHUNK):
        at = slice(start, start + CHUNK)
        given_ref[at, :] = transposed_dot(normed_ref[:, at], give).astype(jnp.bfloat16)

    columns = pl.ds(pl.multiple_of(core * half, half), half)
    copies[6].wait()
    gains = to_column(gain_ref[...].astype(jnp.float32).reshape(1, -1))
    copies[7].wait()
    folded = weight_ref[:, columns].astype(jnp.float32) * gains
    folded_ref[...] = folded.astype(jnp.bfloat16)


def rest_kernel(normed_ref, both_ref, own_ref, given_ref):
    width, half = own_ref.shape
    done = width - given_ref.shape[0]
    keep, both = both_ref[:, :half], both_ref[...]
    for start in range(0, width, CHUNK):
        at = slice(start, start + CHUNK)
        if start < done:
            own_ref[at, :] = transposed_dot(normed_ref[:, at], keep)
            continue
        result = transposed_dot(normed_ref[:, at], both)
        own_ref[at, :] = result[:, :half]
        given_ref[start - done : start - done + CHUNK, :] = result[:, half:].astype(jnp.bfloat16)


def aligned(index, size):
    return pl.ds(pl.multiple_of(index * size, size), size)


def total(kept, taken):
    return kept + taken.astype(jnp.float32)


def pair_kernel(
    own_ref, first_ref, second_ref, kept_y_ref, given_y_ref, kept_x_ref, given_x_ref
):
    members, rows, columns = kept_y_ref.shape
    left, right = slice(0, columns), slice(columns, 2 * columns)
    y, x = lax.axis_index("outer"), lax.axis_index("fsdp") % 2

    def pair(i, offset, size, side):
        done = first_ref.shape[0] // size
        taken_ref, shift = (first_ref, 0) if 2 * i < done else (second_ref, done)
        at, taken_at = aligned(2 * i + offset, size), aligned(2 * i - shift + offset, size)
        return total(own_ref[at, side], taken_ref[taken_at, side])

    for i in range(members):
        kept_y_ref[i] = pair(i, y, rows, left)
        given_y_ref[i] = pair(i, 1 - y, rows, left).astype(jnp.bfloat16)
    for i in range(members // 2):
        kept_x_ref[i] = pair(i, x, 2 * rows, right)
        given_x_ref[i] = pair(i, 1 - x, 2 * rows, right).astype(jnp.bfloat16)


def cross_kernel(
    kept_y_ref, taken_y_ref, kept_x_ref, taken_x_ref,
    next_x_ref, given_x_ref, next_y_ref, given_y_ref,
):
    count, rows, _ = next_x_ref.shape
    y, x = lax.axis_index("outer"), lax.axis_index("fsdp") % 2
    for i in range(count):
        at = 2 * i + x
        next_x_ref[i] = total(kept_y_ref[at], taken_y_ref[at])
        at = 2 * i + 1 - x
        given_x_ref[i] = total(kept_y_ref[at], taken_y_ref[at]).astype(jnp.bfloat16)
        at = aligned(y, rows)
        next_y_ref[i] = total(kept_x_ref[i, at, :], taken_x_ref[i, at, :])
        at = aligned(1 - y, rows)
        given_y_ref[i] = total(kept_x_ref[i, at, :], taken_x_ref[i, at, :]).astype(jnp.bfloat16)


def z_kernel(kept_x_ref, taken_x_ref, kept_y_ref, taken_y_ref, *out_refs):
    columns = kept_x_ref.shape[2]
    left, right = slice(0, columns), slice(columns, 2 * columns)
    z = lax.axis_index("fsdp") // 2
    for shift, out_ref in enumerate(out_refs):
        at = jnp.bitwise_xor(z, shift)
        out_ref[:, left] = total(kept_x_ref[at], taken_x_ref[at]).astype(out_ref.dtype)
        out_ref[:, right] = total(kept_y_ref[at], taken_y_ref[at]).astype(out_ref.dtype)


def last_kernel(own_ref, *refs):
    result = own_ref[...]
    for taken_ref in refs[:-1]:
        result = total(result, taken_ref[...])
    refs[-1][...] = result.astype(jnp.bfloat16)


def finish_kernel(counts_ref, gain_ref, weight_ref, *refs):
    parts, (weight_grad_ref, gain_grad_ref, sum_ref) = refs[:-3], refs[-3:]
    rows, half = parts[0].shape
    y, core = lax.axis_index("outer"), lax.axis_index("core")
    live_total = full_sum(counts_ref[...].astype(jnp.float32)) * float(BLOCK)
    scale = 1.0 / jnp.sqrt(live_total)
    gains = to_column(gain_ref[...].astype(jnp.float32).reshape(1, -1)) * scale
    shifts = (0, 1) if len(parts) == 2 else (0, 1, 2, 3)
    for shift, part_ref in zip(shifts, parts):
        at_y = 0 if len(parts) == 2 else jnp.bitwise_xor(y, shift // 2)
        at = jnp.bitwise_xor(core, shift % 2)
        sum_ref[aligned(at_y, rows), aligned(at, half)] = part_ref[...].astype(jnp.float32)
    result = sum_ref[...]
    weight_grad_ref[...] = result * gains
    dots = jnp.sum(result * weight_ref[...].astype(jnp.float32), axis=1, keepdims=True)
    gain_grad_ref[...] = to_line(dots * scale).reshape(-1)


def forward_kernel(normed_ref, own_ref, other_ref, cosines_ref, sines_ref, out_ref):
    core = lax.axis_index("core")
    normed = normed_ref[...]
    own = jnp.dot(normed, own_ref[...], preferred_element_type=jnp.float32)
    other = jnp.dot(normed, other_ref[...], preferred_element_type=jnp.float32)
    keys = jnp.where(core == 0, own, other)
    values = jnp.where(core == 0, other, own)
    cosines, sines = cosines_ref[...], sines_ref[...]
    for head in range(KVH):
        part = keys[:, head * HD : (head + 1) * HD]
        out_ref[:, head * HD : (head + 1) * HD] = (
            part * cosines + pltpu.roll(part, HD // 2, 1) * sines
        ).astype(jnp.bfloat16)
    out_ref[:, KVH * HD :] = values.astype(jnp.bfloat16)


def exchange(value, axes, count, shift):
    return lax.ppermute(value, axes, [(i, i ^ shift) for i in range(count)])


def sum_on_cube(own, first, second, shard):
    width, half = own.shape
    f32, bf16 = jnp.float32, jnp.bfloat16
    shape = jax.ShapeDtypeStruct
    rows, columns = shard // 2, half // 2

    def both(*dims):
        return (shape(dims, f32), shape(dims, bf16))

    kept_y, given_y, kept_x, given_x = call(
        pair_kernel, both(8, rows, columns) + both(4, shard, columns), (own, first, second)
    )
    pair_done = kept_y
    taken_y = exchange(given_y, "outer", 2, 1)
    taken_x = exchange(given_x, "fsdp", 8, 1)
    kept_x, given_x, kept_y, given_y = call(
        cross_kernel,
        both(4, rows, columns) + both(4, rows, columns),
        (kept_y, taken_y, kept_x, taken_x),
        flops=FLOPS["cross"],
    )
    taken_x = exchange(given_x, "fsdp", 8, 1)
    taken_y = exchange(given_y, "outer", 2, 1)
    kept, *given = call(
        z_kernel,
        (shape((rows, half), f32),) + (shape((rows, half), bf16),) * 3,
        (kept_x, taken_x, kept_y, taken_y),
        flops=FLOPS["z"],
    )
    taken = [exchange(given[i], "fsdp", 8, 2 * i + 2) for i in (1, 2, 0)]
    mine = call(
        last_kernel, shape((rows, half), bf16), (kept, *taken), flops=FLOPS["last"]
    )
    return mine, (pair_done, pair_done, kept)


def gather_on_cube(folded, steps):
    shard, half = folded.shape
    shape = jax.ShapeDtypeStruct

    def over(part, shift):
        return exchange(part, "fsdp", 8, shift)

    def stack(*parts, after, flops=0):
        out = shape((len(parts), shard, half), folded.dtype)
        return call(stack_kernel, out, parts, after=after, flops=flops)

    near, far = over(folded, 2), over(folded, 4)
    both = over(stack(far, after=steps[0], flops=FLOPS["far"])[0], 2)
    parts = stack(near, far, both, after=steps[1], flops=FLOPS["stack"])
    shifts = (2, 4, 6, 3, 5, 7, 0, 1)
    return call(
        functools.partial(order_kernel, shifts),
        shape((8 * shard, half), folded.dtype),
        (parts, over(parts, 1), folded, over(folded, 1)),
        after=steps[2],
    )


def body(outer, members, tokens, gain, kv_weight, positions, cotangent, counts, ratios):
    domains = 2 * outer
    rows, width = tokens.shape
    shard, columns = kv_weight.shape
    half = columns // 2
    f32, bf16 = jnp.float32, jnp.bfloat16
    shape = jax.ShapeDtypeStruct
    on_cube = outer == 2 and members == 8 and shard % 32 == 0

    exponents = np.arange(HD, dtype=np.float64) % (HD // 2) * (2.0 / HD)
    frequency = jnp.asarray(np.power(1000000.0, -exponents).astype(np.float32))
    normed, cosines, sines, both, given, folded = call(
        backward_kernel,
        (
            shape((rows, width), bf16),
            shape((rows, HD), f32),
            shape((rows, HD), f32),
            shape((rows, columns), bf16),
            shape((width - width // 4, half), bf16),
            shape((shard, half), bf16),
        ),
        (
            positions.reshape(rows // 128, 128),
            frequency.reshape(1, HD),
            counts,
            ratios.reshape(1, domains),
            cotangent,
            tokens,
            gain,
            kv_weight,
        ),
        fetched=8,
    )
    first = exchange(given, "core", 2, 1)
    own, given = call(
        rest_kernel, (shape((width, half), f32), shape((width // 4, half), bf16)), (normed, both)
    )
    second = exchange(given, "core", 2, 1)
    if on_cube:
        mine, steps = sum_on_cube(own, first, second, shard)
        own_half = gather_on_cube(folded, steps)
        other_half = exchange(own_half, "core", 2, 1)
        sums = [mine] + [exchange(mine, ("outer", "core"), 4, i) for i in (1, 2, 3)]
    else:
        pair = own + jnp.concatenate([first, second]).astype(f32)
        pair = lax.psum_scatter(pair, "fsdp", scatter_dimension=0, tiled=True)
        mine = lax.psum(pair, "outer")
        own_half = lax.all_gather(folded, "fsdp", axis=0, tiled=True)
        other_half = exchange(own_half, "core", 2, 1)
        sums = [mine, exchange(mine, "core", 2, 1)]
    keys_out = call(
        forward_kernel,
        shape((rows, columns), bf16),
        (normed, own_half, other_half, cosines, sines),
        after=mine,
    )
    weight_grad, gain_grad = call(
        finish_kernel,
        (shape((shard, columns), f32), shape((shard,), f32)),
        (counts, gain, kv_weight, *sums),
        scratch=[pltpu.VMEM((shard, columns), f32)],
        after=keys_out,
        in_hbm=True,
    )
    return (keys_out, weight_grad, gain_grad)


def solution(mesh):
    domains, members = mesh.shape["dom"], mesh.shape["fsdp"]
    outer = domains // 2
    split = Mesh(mesh.devices.reshape(outer, 2, members), EVERY)
    return jax.shard_map(
        functools.partial(body, outer, members),
        mesh=split,
        in_specs=(
            P(EVERY, None),
            P("fsdp"),
            P("fsdp", None),
            P(EVERY),
            P(EVERY, None),
            P(),
            P(),
        ),
        out_specs=(P(EVERY, None), P("fsdp", None), P("fsdp")),
        check_vma=False,
    )
```

```python
import functools

import jax
import jax.numpy as jnp
import numpy as np
from jax import lax
from jax.experimental import pallas as pl
from jax.experimental.pallas import tpu as pltpu
from jax.sharding import Mesh
from jax.sharding import PartitionSpec as P

KVH = 2
HD = 128
BLOCK = 128
CHUNK = 384
Z_FLOPS = 2 * 10**9
EVERY = ("outer", "core", "fsdp")
VMEM_BYTES = 32 * 1024 * 1024


def to_column(line):
    n = line.shape[1]
    rows = lax.broadcasted_iota(jnp.int32, (n, n), 0)
    lanes = lax.broadcasted_iota(jnp.int32, (n, n), 1)
    spread = jnp.broadcast_to(line, (n, n))
    return jnp.sum(jnp.where(rows == lanes, spread, 0.0), axis=1, keepdims=True)


def to_line(column):
    n = column.shape[0]
    rows = lax.broadcasted_iota(jnp.int32, (n, n), 0)
    lanes = lax.broadcasted_iota(jnp.int32, (n, n), 1)
    spread = jnp.broadcast_to(column, (n, n))
    return jnp.sum(jnp.where(rows == lanes, spread, 0.0), axis=0, keepdims=True)


def sine_cosine(angles):
    turns = jnp.floor(angles * (2.0 / np.pi) + 0.5)
    rest = angles - turns * 1.5703125
    rest = rest - turns * 4.837512969970703125e-4
    rest = rest - turns * 7.54978995489188216e-8
    square = rest * rest
    sine = (-1.9515295891e-4 * square + 8.3321608736e-3) * square - 1.6666654611e-1
    sine = sine * square * rest + rest
    cosine = (2.443315711809948e-5 * square - 1.388731625493765e-3) * square
    cosine = (cosine + 4.166664568298827e-2) * square * square - 0.5 * square + 1.0
    quarter = turns.astype(jnp.int32) & 3
    odd = (quarter & 1) == 1
    sines, cosines = jnp.where(odd, cosine, sine), jnp.where(odd, sine, cosine)
    sines = jnp.where(quarter >= 2, -sines, sines)
    cosines = jnp.where(((quarter + 1) & 2) == 2, -cosines, cosines)
    return sines, cosines


def transposed_dot(left, right):
    return lax.dot_general(
        left, right, (((0,), (0,)), ((), ())), preferred_element_type=jnp.float32
    )


def full_sum(values):
    return jnp.sum(jnp.sum(values, axis=1, keepdims=True), axis=0, keepdims=True)


def fetch(sources, buffers, semaphores):
    copies = []
    for i, (source, buffer) in enumerate(zip(sources, buffers)):
        copy = pltpu.make_async_copy(source, buffer, semaphores.at[i])
        copy.start()
        copies.append(copy)
    return copies


def call(kernel, out_shape, args, after=None, in_hbm=False, fetched=0, scratch=(), flops=0):
    count = len(args)
    args = [
        pltpu.with_memory_space_constraint(arg, pltpu.HBM) if i < fetched else arg
        for i, arg in enumerate(args)
    ]
    spaces = [pl.ANY] * fetched + [pltpu.VMEM] * (count - fetched)
    run = kernel
    if after is not None:
        if in_hbm:
            after = pltpu.with_memory_space_constraint(after, pltpu.HBM)
        args, spaces = args + [after], spaces + [pl.ANY]

        def run(*refs):
            kernel(*refs[:count], *refs[count + 1 :])

    scratch = list(scratch) + [pltpu.VMEM(arg.shape, arg.dtype) for arg in args[:fetched]]
    if fetched:
        scratch.append(pltpu.SemaphoreType.DMA((fetched,)))
    return pl.pallas_call(
        run,
        out_shape=out_shape,
        in_specs=[pl.BlockSpec(memory_space=space) for space in spaces],
        scratch_shapes=scratch,
        out_specs=jax.tree.map(lambda _: pl.BlockSpec(memory_space=pltpu.VMEM), out_shape),
        compiler_params=pltpu.CompilerParams(vmem_limit_bytes=VMEM_BYTES),
        cost_estimate=pl.CostEstimate(
            flops=flops, bytes_accessed=1000000, transcendentals=0
        ),
    )(*args)


def stack_kernel(*refs):
    for i, part_ref in enumerate(refs[:-1]):
        refs[-1][i] = part_ref[...]


def bundle_kernel(shifts, mine_ref, *refs):
    out_ref = refs[-1]
    rows = refs[0].shape[1]
    member = lax.axis_index("fsdp")
    parts = [part_ref.at[i] for part_ref in refs[:-1] for i in range(part_ref.shape[0])]
    for shift, part_ref in zip(shifts, parts):
        out_ref[aligned(jnp.bitwise_xor(member, shift), rows), :] = part_ref[...]
    out_ref[len(parts) * rows :, :] = mine_ref[...]


def backward_kernel(
    positions_hbm, frequency_hbm, counts_hbm, ratios_hbm, cotangent_hbm, tokens_hbm,
    gain_hbm, weight_hbm,
    normed_ref, cosines_ref, sines_ref, both_ref, given_ref, folded_ref,
    positions_ref, frequency_ref, counts_ref, ratios_ref, cotangent_ref, tokens_ref,
    gain_ref, weight_ref,
    semaphores,
):
    copies = fetch(
        (
            positions_hbm, frequency_hbm, counts_hbm, ratios_hbm, cotangent_hbm, tokens_hbm,
            gain_hbm, weight_hbm,
        ),
        (
            positions_ref, frequency_ref, counts_ref, ratios_ref, cotangent_ref, tokens_ref,
            gain_ref, weight_ref,
        ),
        semaphores,
    )
    rows, width = tokens_ref.shape
    core = lax.axis_index("core")
    domain = lax.axis_index("outer") * 2 + core
    member = lax.axis_index("fsdp")

    for copy in copies[:5]:
        copy.wait()
    lines = positions_ref[...].astype(jnp.float32)
    lanes = lax.broadcasted_iota(jnp.int32, (lines.shape[1], HD), 1)
    left = lanes < HD // 2
    first, second = to_column(lines[0:1, :]), to_column(lines[1:2, :])
    sines, cosines = sine_cosine(jnp.where(left, first, second) * frequency_ref[...])
    turned_sines, turned_cosines = pltpu.roll(sines, HD // 2, 1), pltpu.roll(cosines, HD // 2, 1)
    cosines = jnp.concatenate(
        [jnp.where(left, cosines, turned_cosines), jnp.where(left, turned_cosines, cosines)]
    )
    sines = jnp.concatenate(
        [jnp.where(left, -sines, turned_sines), jnp.where(left, -turned_sines, sines)]
    )
    cosines_ref[...] = cosines
    sines_ref[...] = sines

    counts = counts_ref[...].astype(jnp.float32)
    ratios = ratios_ref[...].astype(jnp.float32)
    at_domain = lax.broadcasted_iota(jnp.int32, counts.shape, 0) == domain
    at_member = lax.broadcasted_iota(jnp.int32, counts.shape, 1) == member
    ratio_at = lax.broadcasted_iota(jnp.int32, ratios.shape, 1) == domain
    live_total = full_sum(counts) * float(BLOCK)
    own_rows = full_sum(jnp.where(at_domain, counts, 0.0)) * float(BLOCK)
    own_live = full_sum(jnp.where(at_domain & at_member, counts, 0.0)) * float(BLOCK)
    own_ratio = full_sum(jnp.where(ratio_at, ratios, 0.0))
    factor = own_ratio / full_sum(ratios) * live_total / own_rows
    row_ids = lax.broadcasted_iota(jnp.int32, (rows, 1), 0).astype(jnp.float32)
    row_factor = jnp.where(row_ids < own_live, factor, 0.0)

    weighted = cotangent_ref[...].astype(jnp.float32) * row_factor
    key_width = KVH * HD
    turned = []
    for head in range(KVH):
        part = weighted[:, head * HD : (head + 1) * HD]
        turned.append(part * cosines - pltpu.roll(part, HD // 2, 1) * sines)
    keys = jnp.concatenate(turned, axis=1).astype(jnp.bfloat16)
    values = weighted[:, key_width:].astype(jnp.bfloat16)
    keep = jnp.where(core == 0, keys, values)
    give = jnp.where(core == 0, values, keys)
    half = keep.shape[1]
    both_ref[:, :half] = keep
    both_ref[:, half:] = give

    copies[5].wait()
    step = 32
    for start in range(0, rows, step):
        block = tokens_ref[start : start + step, :].astype(jnp.float32)
        mean_square = jnp.sum(block * block, axis=1, keepdims=True) * (1.0 / width)
        normed_ref[start : start + step, :] = (
            block * lax.rsqrt(mean_square + 1e-06)
        ).astype(jnp.bfloat16)

    for start in range(0, given_ref.shape[0], CHUNK):
        at = slice(start, start + CHUNK)
        given_ref[at, :] = transposed_dot(normed_ref[:, at], give).astype(jnp.bfloat16)

    columns = pl.ds(pl.multiple_of(core * half, half), half)
    copies[6].wait()
    gains = to_column(gain_ref[...].astype(jnp.float32).reshape(1, -1))
    copies[7].wait()
    folded = weight_ref[:, columns].astype(jnp.float32) * gains
    folded_ref[...] = folded.astype(jnp.bfloat16)


def rest_kernel(normed_ref, both_ref, own_ref, given_ref):
    width, half = own_ref.shape
    done = width - given_ref.shape[0]
    keep, both = both_ref[:, :half], both_ref[...]
    for start in range(0, width, CHUNK):
        at = slice(start, start + CHUNK)
        if start < done:
            own_ref[at, :] = transposed_dot(normed_ref[:, at], keep)
            continue
        result = transposed_dot(normed_ref[:, at], both)
        own_ref[at, :] = result[:, :half]
        given_ref[start - done : start - done + CHUNK, :] = result[:, half:].astype(jnp.bfloat16)


def aligned(index, size):
    return pl.ds(pl.multiple_of(index * size, size), size)


def total(kept, taken):
    return kept + taken.astype(jnp.float32)


def pair_kernel(own_ref, first_ref, second_ref, *out_refs):
    count, rows, _ = out_refs[0].shape
    first_count = first_ref.shape[0] // (4 * rows)
    y, x = lax.axis_index("outer"), lax.axis_index("fsdp") % 2
    for (away_y, away_x), out_ref in zip(((0, 0), (1, 1), (1, 0), (0, 1)), out_refs):
        to_y, to_x = jnp.bitwise_xor(y, away_y), jnp.bitwise_xor(x, away_x)
        for i in range(count):
            at = aligned(4 * i + 2 * to_x + to_y, rows)
            in_first = i < first_count
            taken_ref = first_ref if in_first else second_ref
            taken_at = 4 * (i if in_first else i - first_count) + 2 * to_x + to_y
            taken_at = aligned(taken_at, rows)
            out_ref[i] = total(own_ref[at, :], taken_ref[taken_at, :]).astype(out_ref.dtype)


def z_kernel(kept_ref, first_ref, second_ref, third_ref, *out_refs):
    z = lax.axis_index("fsdp") // 2
    for shift, out_ref in enumerate(out_refs):
        at = jnp.bitwise_xor(z, shift)
        result = total(kept_ref[at], first_ref[at])
        result = total(total(result, second_ref[at]), third_ref[at])
        out_ref[...] = result.astype(out_ref.dtype)


def last_kernel(own_ref, *refs):
    result = own_ref[...]
    for taken_ref in refs[:-1]:
        result = total(result, taken_ref[...])
    refs[-1][...] = result.astype(jnp.bfloat16)


def finish_kernel(counts_ref, gain_ref, weight_ref, *refs):
    parts, (weight_grad_ref, gain_grad_ref, sum_ref) = refs[:-3], refs[-3:]
    rows, half = parts[0].shape
    y, core = lax.axis_index("outer"), lax.axis_index("core")
    live_total = full_sum(counts_ref[...].astype(jnp.float32)) * float(BLOCK)
    scale = 1.0 / jnp.sqrt(live_total)
    gains = to_column(gain_ref[...].astype(jnp.float32).reshape(1, -1)) * scale
    shifts = (0, 1) if len(parts) == 2 else (0, 1, 2, 3)
    for shift, part_ref in zip(shifts, parts):
        at_y = 0 if len(parts) == 2 else jnp.bitwise_xor(y, shift // 2)
        at = jnp.bitwise_xor(core, shift % 2)
        tail = slice(part_ref.shape[0] - rows, None)
        sum_ref[aligned(at_y, rows), aligned(at, half)] = part_ref[tail, :].astype(jnp.float32)
    result = sum_ref[...]
    weight_grad_ref[...] = result * gains
    dots = jnp.sum(result * weight_ref[...].astype(jnp.float32), axis=1, keepdims=True)
    gain_grad_ref[...] = to_line(dots * scale).reshape(-1)


def forward_kernel(normed_ref, own_ref, other_ref, cosines_ref, sines_ref, out_ref):
    core = lax.axis_index("core")
    normed = normed_ref[...]
    width = normed.shape[1]
    own = jnp.dot(normed, own_ref[:width, :], preferred_element_type=jnp.float32)
    other = jnp.dot(normed, other_ref[:width, :], preferred_element_type=jnp.float32)
    keys = jnp.where(core == 0, own, other)
    values = jnp.where(core == 0, other, own)
    cosines, sines = cosines_ref[...], sines_ref[...]
    for head in range(KVH):
        part = keys[:, head * HD : (head + 1) * HD]
        out_ref[:, head * HD : (head + 1) * HD] = (
            part * cosines + pltpu.roll(part, HD // 2, 1) * sines
        ).astype(jnp.bfloat16)
    out_ref[:, KVH * HD :] = values.astype(jnp.bfloat16)


def exchange(value, axes, count, shift):
    return lax.ppermute(value, axes, [(i, i ^ shift) for i in range(count)])


def sum_on_cube(own, first, second, shard):
    width, half = own.shape
    f32, bf16 = jnp.float32, jnp.bfloat16
    shape = jax.ShapeDtypeStruct
    rows = shard // 2
    kept, *given = call(
        pair_kernel,
        (shape((4, rows, half), f32),) + (shape((4, rows, half), bf16),) * 3,
        (own, first, second),
    )
    pair_done = kept
    taken = [
        exchange(given[0], ("outer", "fsdp"), 16, 9),
        exchange(given[1], "outer", 2, 1),
        exchange(given[2], "fsdp", 8, 1),
    ]
    first_xy, second_xy, third_xy = taken
    kept, *given = call(
        z_kernel,
        (shape((rows, half), f32),) + (shape((rows, half), bf16),) * 3,
        (kept, *taken),
        flops=Z_FLOPS,
    )
    taken = [exchange(given[i], "fsdp", 8, 2 * i + 2) for i in (1, 2, 0)]
    mine = call(
        last_kernel, shape((rows, half), bf16), (kept, *taken)
    )
    return mine, (None, pair_done, pair_done, mine)


def gather_on_cube(folded, steps):
    shard, half = folded.shape
    shape = jax.ShapeDtypeStruct

    def over(part, shift):
        return exchange(part, "fsdp", 8, shift)

    def stack(*parts, after, flops=0):
        out = shape((len(parts), shard, half), folded.dtype)
        return call(stack_kernel, out, parts, after=after, flops=flops)

    near, far = over(folded, 2), over(folded, 4)
    both = over(stack(far, after=steps[0])[0], 2)
    low = stack(folded, near, after=steps[1])
    high = stack(far, both, after=steps[2])
    shifts = (0, 2, 4, 6, 1, 3, 5, 7)
    mine = steps[3]
    return call(
        functools.partial(bundle_kernel, shifts),
        shape((8 * shard + mine.shape[0], half), folded.dtype),
        (mine, low, high, over(low, 1), over(high, 1)),
    )


def body(outer, members, tokens, gain, kv_weight, positions, cotangent, counts, ratios):
    domains = 2 * outer
    rows, width = tokens.shape
    shard, columns = kv_weight.shape
    half = columns // 2
    f32, bf16 = jnp.float32, jnp.bfloat16
    shape = jax.ShapeDtypeStruct
    on_cube = outer == 2 and members == 8 and shard % 32 == 0

    exponents = np.arange(HD, dtype=np.float64) % (HD // 2) * (2.0 / HD)
    frequency = jnp.asarray(np.power(1000000.0, -exponents).astype(np.float32))
    normed, cosines, sines, both, given, folded = call(
        backward_kernel,
        (
            shape((rows, width), bf16),
            shape((rows, HD), f32),
            shape((rows, HD), f32),
            shape((rows, columns), bf16),
            shape((width - width // 4, half), bf16),
            shape((shard, half), bf16),
        ),
        (
            positions.reshape(rows // 128, 128),
            frequency.reshape(1, HD),
            counts,
            ratios.reshape(1, domains),
            cotangent,
            tokens,
            gain,
            kv_weight,
        ),
        fetched=8,
    )
    first = exchange(given, "core", 2, 1)
    own, given = call(
        rest_kernel, (shape((width, half), f32), shape((width // 4, half), bf16)), (normed, both)
    )
    second = exchange(given, "core", 2, 1)
    if on_cube:
        mine, steps = sum_on_cube(own, first, second, shard)
        own_half = gather_on_cube(folded, steps)
        other_half = exchange(own_half, "core", 2, 1)
        sums = [mine, other_half] + [exchange(mine, ("outer", "core"), 4, i) for i in (2, 3)]
    else:
        pair = own + jnp.concatenate([first, second]).astype(f32)
        pair = lax.psum_scatter(pair, "fsdp", scatter_dimension=0, tiled=True)
        mine = lax.psum(pair, "outer")
        own_half = lax.all_gather(folded, "fsdp", axis=0, tiled=True)
        other_half = exchange(own_half, "core", 2, 1)
        sums = [mine, exchange(mine, "core", 2, 1)]
    keys_out = call(
        forward_kernel,
        shape((rows, columns), bf16),
        (normed, own_half, other_half, cosines, sines),
        after=mine,
    )
    weight_grad, gain_grad = call(
        finish_kernel,
        (shape((shard, columns), f32), shape((shard,), f32)),
        (counts, gain, kv_weight, *sums),
        scratch=[pltpu.VMEM((shard, columns), f32)],
        after=keys_out,
        in_hbm=True,
    )
    return (keys_out, weight_grad, gain_grad)


def solution(mesh):
    domains, members = mesh.shape["dom"], mesh.shape["fsdp"]
    outer = domains // 2
    split = Mesh(mesh.devices.reshape(outer, 2, members), EVERY)
    return jax.shard_map(
        functools.partial(body, outer, members),
        mesh=split,
        in_specs=(
            P(EVERY, None),
            P("fsdp"),
            P("fsdp", None),
            P(EVERY),
            P(EVERY, None),
            P(),
            P(),
        ),
        out_specs=(P(EVERY, None), P("fsdp", None), P("fsdp")),
        check_vma=False,
    )
```

```python
import functools

import jax
import jax.numpy as jnp
import numpy as np
from jax import lax
from jax.experimental import pallas as pl
from jax.experimental.pallas import tpu as pltpu
from jax.sharding import Mesh
from jax.sharding import PartitionSpec as P

KVH = 2
HD = 128
BLOCK = 128
CHUNK = 384
EVERY = ("outer", "core", "fsdp")
VMEM_BYTES = 32 * 1024 * 1024


def to_column(line):
    n = line.shape[1]
    rows = lax.broadcasted_iota(jnp.int32, (n, n), 0)
    lanes = lax.broadcasted_iota(jnp.int32, (n, n), 1)
    spread = jnp.broadcast_to(line, (n, n))
    return jnp.sum(jnp.where(rows == lanes, spread, 0.0), axis=1, keepdims=True)


def to_line(column):
    n = column.shape[0]
    rows = lax.broadcasted_iota(jnp.int32, (n, n), 0)
    lanes = lax.broadcasted_iota(jnp.int32, (n, n), 1)
    spread = jnp.broadcast_to(column, (n, n))
    return jnp.sum(jnp.where(rows == lanes, spread, 0.0), axis=0, keepdims=True)


def sine_cosine(angles):
    turns = jnp.floor(angles * (2.0 / np.pi) + 0.5)
    rest = angles - turns * 1.5703125
    rest = rest - turns * 4.837512969970703125e-4
    rest = rest - turns * 7.54978995489188216e-8
    square = rest * rest
    sine = (-1.9515295891e-4 * square + 8.3321608736e-3) * square - 1.6666654611e-1
    sine = sine * square * rest + rest
    cosine = (2.443315711809948e-5 * square - 1.388731625493765e-3) * square
    cosine = (cosine + 4.166664568298827e-2) * square * square - 0.5 * square + 1.0
    quarter = turns.astype(jnp.int32) & 3
    odd = (quarter & 1) == 1
    sines, cosines = jnp.where(odd, cosine, sine), jnp.where(odd, sine, cosine)
    sines = jnp.where(quarter >= 2, -sines, sines)
    cosines = jnp.where(((quarter + 1) & 2) == 2, -cosines, cosines)
    return sines, cosines


def transposed_dot(left, right):
    return lax.dot_general(
        left, right, (((0,), (0,)), ((), ())), preferred_element_type=jnp.float32
    )


def full_sum(values):
    return jnp.sum(jnp.sum(values, axis=1, keepdims=True), axis=0, keepdims=True)


def fetch(sources, buffers, semaphores):
    copies = []
    for i, (source, buffer) in enumerate(zip(sources, buffers)):
        copy = pltpu.make_async_copy(source, buffer, semaphores.at[i])
        copy.start()
        copies.append(copy)
    return copies


def call(kernel, out_shape, args, after=None, in_hbm=False, fetched=0, scratch=(), flops=0):
    count = len(args)
    args = [
        pltpu.with_memory_space_constraint(arg, pltpu.HBM) if i < fetched else arg
        for i, arg in enumerate(args)
    ]
    spaces = [pl.ANY] * fetched + [pltpu.VMEM] * (count - fetched)
    run = kernel
    if after is not None:
        if in_hbm:
            after = pltpu.with_memory_space_constraint(after, pltpu.HBM)
        args, spaces = args + [after], spaces + [pl.ANY]

        def run(*refs):
            kernel(*refs[:count], *refs[count + 1 :])

    scratch = list(scratch) + [pltpu.VMEM(arg.shape, arg.dtype) for arg in args[:fetched]]
    if fetched:
        scratch.append(pltpu.SemaphoreType.DMA((fetched,)))
    return pl.pallas_call(
        run,
        out_shape=out_shape,
        in_specs=[pl.BlockSpec(memory_space=space) for space in spaces],
        scratch_shapes=scratch,
        out_specs=jax.tree.map(lambda _: pl.BlockSpec(memory_space=pltpu.VMEM), out_shape),
        compiler_params=pltpu.CompilerParams(vmem_limit_bytes=VMEM_BYTES),
        cost_estimate=pl.CostEstimate(
            flops=flops, bytes_accessed=1000000, transcendentals=0
        ),
    )(*args)


def stack_kernel(*refs):
    for i, part_ref in enumerate(refs[:-1]):
        refs[-1][i] = part_ref[...]


def bundle_kernel(shifts, mine_ref, *refs):
    out_ref = refs[-1]
    rows = refs[0].shape[1]
    member = lax.axis_index("fsdp")
    parts = [part_ref.at[i] for part_ref in refs[:-1] for i in range(part_ref.shape[0])]
    for shift, part_ref in zip(shifts, parts):
        out_ref[aligned(jnp.bitwise_xor(member, shift), rows), :] = part_ref[...]
    out_ref[len(parts) * rows :, :] = mine_ref[...]


def backward_kernel(
    positions_hbm, frequency_hbm, counts_hbm, ratios_hbm, cotangent_hbm, tokens_hbm,
    gain_hbm, weight_hbm,
    normed_ref, cosines_ref, sines_ref, both_ref, given_ref, folded_ref,
    positions_ref, frequency_ref, counts_ref, ratios_ref, cotangent_ref, tokens_ref,
    gain_ref, weight_ref,
    semaphores,
):
    copies = fetch(
        (
            positions_hbm, frequency_hbm, counts_hbm, ratios_hbm, cotangent_hbm, tokens_hbm,
            gain_hbm, weight_hbm,
        ),
        (
            positions_ref, frequency_ref, counts_ref, ratios_ref, cotangent_ref, tokens_ref,
            gain_ref, weight_ref,
        ),
        semaphores,
    )
    rows, width = tokens_ref.shape
    core = lax.axis_index("core")
    domain = lax.axis_index("outer") * 2 + core
    member = lax.axis_index("fsdp")

    for copy in copies[:5]:
        copy.wait()
    lines = positions_ref[...].astype(jnp.float32)
    lanes = lax.broadcasted_iota(jnp.int32, (lines.shape[1], HD), 1)
    left = lanes < HD // 2
    first, second = to_column(lines[0:1, :]), to_column(lines[1:2, :])
    sines, cosines = sine_cosine(jnp.where(left, first, second) * frequency_ref[...])
    turned_sines, turned_cosines = pltpu.roll(sines, HD // 2, 1), pltpu.roll(cosines, HD // 2, 1)
    cosines = jnp.concatenate(
        [jnp.where(left, cosines, turned_cosines), jnp.where(left, turned_cosines, cosines)]
    )
    sines = jnp.concatenate(
        [jnp.where(left, -sines, turned_sines), jnp.where(left, -turned_sines, sines)]
    )
    cosines_ref[...] = cosines
    sines_ref[...] = sines

    counts = counts_ref[...].astype(jnp.float32)
    ratios = ratios_ref[...].astype(jnp.float32)
    at_domain = lax.broadcasted_iota(jnp.int32, counts.shape, 0) == domain
    at_member = lax.broadcasted_iota(jnp.int32, counts.shape, 1) == member
    ratio_at = lax.broadcasted_iota(jnp.int32, ratios.shape, 1) == domain
    live_total = full_sum(counts) * float(BLOCK)
    own_rows = full_sum(jnp.where(at_domain, counts, 0.0)) * float(BLOCK)
    own_live = full_sum(jnp.where(at_domain & at_member, counts, 0.0)) * float(BLOCK)
    own_ratio = full_sum(jnp.where(ratio_at, ratios, 0.0))
    factor = own_ratio / full_sum(ratios) * live_total / own_rows
    row_ids = lax.broadcasted_iota(jnp.int32, (rows, 1), 0).astype(jnp.float32)
    row_factor = jnp.where(row_ids < own_live, factor, 0.0)

    weighted = cotangent_ref[...].astype(jnp.float32) * row_factor
    key_width = KVH * HD
    turned = []
    for head in range(KVH):
        part = weighted[:, head * HD : (head + 1) * HD]
        turned.append(part * cosines - pltpu.roll(part, HD // 2, 1) * sines)
    keys = jnp.concatenate(turned, axis=1).astype(jnp.bfloat16)
    values = weighted[:, key_width:].astype(jnp.bfloat16)
    keep = jnp.where(core == 0, keys, values)
    give = jnp.where(core == 0, values, keys)
    half = keep.shape[1]
    both_ref[:, :half] = keep
    both_ref[:, half:] = give

    copies[5].wait()
    step = 32
    for start in range(0, rows, step):
        block = tokens_ref[start : start + step, :].astype(jnp.float32)
        mean_square = jnp.sum(block * block, axis=1, keepdims=True) * (1.0 / width)
        normed_ref[start : start + step, :] = (
            block * lax.rsqrt(mean_square + 1e-06)
        ).astype(jnp.bfloat16)

    for start in range(0, given_ref.shape[0], CHUNK):
        at = slice(start, start + CHUNK)
        given_ref[at, :] = transposed_dot(normed_ref[:, at], give).astype(jnp.bfloat16)

    columns = pl.ds(pl.multiple_of(core * half, half), half)
    copies[6].wait()
    gains = to_column(gain_ref[...].astype(jnp.float32).reshape(1, -1))
    copies[7].wait()
    folded = weight_ref[:, columns].astype(jnp.float32) * gains
    folded_ref[...] = folded.astype(jnp.bfloat16)


def rest_kernel(normed_ref, both_ref, own_ref, given_ref):
    width, half = own_ref.shape
    done = width - given_ref.shape[0]
    keep, both = both_ref[:, :half], both_ref[...]
    for start in range(0, width, CHUNK):
        at = slice(start, start + CHUNK)
        if start < done:
            own_ref[at, :] = transposed_dot(normed_ref[:, at], keep)
            continue
        result = transposed_dot(normed_ref[:, at], both)
        own_ref[at, :] = result[:, :half]
        given_ref[start - done : start - done + CHUNK, :] = result[:, half:].astype(jnp.bfloat16)


def aligned(index, size):
    return pl.ds(pl.multiple_of(index * size, size), size)


def total(kept, taken):
    return kept + taken.astype(jnp.float32)


def pair_kernel(own_ref, first_ref, second_ref, *out_refs):
    count, rows, _ = out_refs[0].shape
    first_count = first_ref.shape[0] // (4 * rows)
    y, x = lax.axis_index("outer"), lax.axis_index("fsdp") % 2
    for (away_y, away_x), out_ref in zip(((0, 0), (1, 1), (1, 0), (0, 1)), out_refs):
        to_y, to_x = jnp.bitwise_xor(y, away_y), jnp.bitwise_xor(x, away_x)
        for i in range(count):
            at = aligned(4 * i + 2 * to_x + to_y, rows)
            in_first = i < first_count
            taken_ref = first_ref if in_first else second_ref
            taken_at = 4 * (i if in_first else i - first_count) + 2 * to_x + to_y
            taken_at = aligned(taken_at, rows)
            out_ref[i] = total(own_ref[at, :], taken_ref[taken_at, :]).astype(out_ref.dtype)


def z_kernel(kept_ref, first_ref, second_ref, third_ref, *out_refs):
    z = lax.axis_index("fsdp") // 2
    for shift, out_ref in enumerate(out_refs):
        at = jnp.bitwise_xor(z, shift)
        result = total(kept_ref[at], first_ref[at])
        result = total(total(result, second_ref[at]), third_ref[at])
        out_ref[...] = result.astype(out_ref.dtype)


def last_kernel(own_ref, *refs):
    result = own_ref[...]
    for taken_ref in refs[:-1]:
        result = total(result, taken_ref[...])
    refs[-1][...] = result.astype(jnp.bfloat16)


def finish_kernel(counts_ref, gain_ref, weight_ref, *refs):
    parts, (weight_grad_ref, gain_grad_ref, sum_ref) = refs[:-3], refs[-3:]
    rows, half = parts[0].shape
    y, core = lax.axis_index("outer"), lax.axis_index("core")
    live_total = full_sum(counts_ref[...].astype(jnp.float32)) * float(BLOCK)
    scale = 1.0 / jnp.sqrt(live_total)
    gains = to_column(gain_ref[...].astype(jnp.float32).reshape(1, -1)) * scale
    shifts = (0, 1) if len(parts) == 2 else (0, 1, 2, 3)
    for shift, part_ref in zip(shifts, parts):
        at_y = 0 if len(parts) == 2 else jnp.bitwise_xor(y, shift // 2)
        at = jnp.bitwise_xor(core, shift % 2)
        tail = slice(part_ref.shape[0] - rows, None)
        sum_ref[aligned(at_y, rows), aligned(at, half)] = part_ref[tail, :].astype(jnp.float32)
    result = sum_ref[...]
    weight_grad_ref[...] = result * gains
    dots = jnp.sum(result * weight_ref[...].astype(jnp.float32), axis=1, keepdims=True)
    gain_grad_ref[...] = to_line(dots * scale).reshape(-1)


def forward_kernel(normed_ref, own_ref, other_ref, cosines_ref, sines_ref, out_ref):
    core = lax.axis_index("core")
    normed = normed_ref[...]
    width = normed.shape[1]
    own = jnp.dot(normed, own_ref[:width, :], preferred_element_type=jnp.float32)
    other = jnp.dot(normed, other_ref[:width, :], preferred_element_type=jnp.float32)
    keys = jnp.where(core == 0, own, other)
    values = jnp.where(core == 0, other, own)
    cosines, sines = cosines_ref[...], sines_ref[...]
    for head in range(KVH):
        part = keys[:, head * HD : (head + 1) * HD]
        out_ref[:, head * HD : (head + 1) * HD] = (
            part * cosines + pltpu.roll(part, HD // 2, 1) * sines
        ).astype(jnp.bfloat16)
    out_ref[:, KVH * HD :] = values.astype(jnp.bfloat16)


def exchange(value, axes, count, shift):
    return lax.ppermute(value, axes, [(i, i ^ shift) for i in range(count)])


def sum_on_cube(own, first, second, shard):
    width, half = own.shape
    f32, bf16 = jnp.float32, jnp.bfloat16
    shape = jax.ShapeDtypeStruct
    rows = shard // 2
    kept, *given = call(
        pair_kernel,
        (shape((4, rows, half), f32),) + (shape((4, rows, half), bf16),) * 3,
        (own, first, second),
    )
    pair_done = kept
    taken = [
        exchange(given[0], ("outer", "fsdp"), 16, 9),
        exchange(given[1], "outer", 2, 1),
        exchange(given[2], "fsdp", 8, 1),
    ]
    first_xy, second_xy, third_xy = taken
    kept, *given = call(
        z_kernel,
        (shape((rows, half), f32),) + (shape((rows, half), bf16),) * 3,
        (kept, *taken),
    )
    taken = [exchange(given[i], "fsdp", 8, 2 * i + 2) for i in (1, 2, 0)]
    mine = call(last_kernel, shape((rows, half), bf16), (kept, *taken))
    return mine, (pair_done, pair_done, None, mine)


def gather_on_cube(folded, steps):
    shard, half = folded.shape
    shape = jax.ShapeDtypeStruct

    def over(part, shift):
        return exchange(part, "fsdp", 8, shift)

    def stack(*parts, after, flops):
        out = shape((len(parts), shard, half), folded.dtype)
        return call(stack_kernel, out, parts, after=after, flops=flops)

    near, far = over(folded, 2), over(folded, 4)
    both = over(stack(far, after=steps[0], flops=10**10)[0], 2)
    low = stack(folded, near, after=steps[1], flops=2 * 10**9)
    high = stack(far, both, after=steps[2], flops=10**10)
    shifts = (0, 2, 4, 6, 1, 3, 5, 7)
    mine = steps[3]
    return call(
        functools.partial(bundle_kernel, shifts),
        shape((8 * shard + mine.shape[0], half), folded.dtype),
        (mine, low, high, over(low, 1), over(high, 1)),
    )


def body(outer, members, tokens, gain, kv_weight, positions, cotangent, counts, ratios):
    domains = 2 * outer
    rows, width = tokens.shape
    shard, columns = kv_weight.shape
    half = columns // 2
    f32, bf16 = jnp.float32, jnp.bfloat16
    shape = jax.ShapeDtypeStruct
    on_cube = outer == 2 and members == 8 and shard % 32 == 0

    exponents = np.arange(HD, dtype=np.float64) % (HD // 2) * (2.0 / HD)
    frequency = jnp.asarray(np.power(1000000.0, -exponents).astype(np.float32))
    normed, cosines, sines, both, given, folded = call(
        backward_kernel,
        (
            shape((rows, width), bf16),
            shape((rows, HD), f32),
            shape((rows, HD), f32),
            shape((rows, columns), bf16),
            shape((width - width // 4, half), bf16),
            shape((shard, half), bf16),
        ),
        (
            positions.reshape(rows // 128, 128),
            frequency.reshape(1, HD),
            counts,
            ratios.reshape(1, domains),
            cotangent,
            tokens,
            gain,
            kv_weight,
        ),
        fetched=8,
    )
    first = exchange(given, "core", 2, 1)
    own, given = call(
        rest_kernel, (shape((width, half), f32), shape((width // 4, half), bf16)), (normed, both)
    )
    second = exchange(given, "core", 2, 1)
    if on_cube:
        mine, steps = sum_on_cube(own, first, second, shard)
        own_half = gather_on_cube(folded, steps)
        other_half = exchange(own_half, "core", 2, 1)
        sums = [mine, other_half] + [exchange(mine, ("outer", "core"), 4, i) for i in (2, 3)]
    else:
        pair = own + jnp.concatenate([first, second]).astype(f32)
        pair = lax.psum_scatter(pair, "fsdp", scatter_dimension=0, tiled=True)
        mine = lax.psum(pair, "outer")
        own_half = lax.all_gather(folded, "fsdp", axis=0, tiled=True)
        other_half = exchange(own_half, "core", 2, 1)
        sums = [mine, exchange(mine, "core", 2, 1)]
    keys_out = call(
        forward_kernel,
        shape((rows, columns), bf16),
        (normed, own_half, other_half, cosines, sines),
        after=mine,
    )
    weight_grad, gain_grad = call(
        finish_kernel,
        (shape((shard, columns), f32), shape((shard,), f32)),
        (counts, gain, kv_weight, *sums),
        scratch=[pltpu.VMEM((shard, columns), f32)],
        after=keys_out,
        in_hbm=True,
    )
    return (keys_out, weight_grad, gain_grad)


def solution(mesh):
    domains, members = mesh.shape["dom"], mesh.shape["fsdp"]
    outer = domains // 2
    split = Mesh(mesh.devices.reshape(outer, 2, members), EVERY)
    return jax.shard_map(
        functools.partial(body, outer, members),
        mesh=split,
        in_specs=(
            P(EVERY, None),
            P("fsdp"),
            P("fsdp", None),
            P(EVERY),
            P(EVERY, None),
            P(),
            P(),
        ),
        out_specs=(P(EVERY, None), P("fsdp", None), P("fsdp")),
        check_vma=False,
    )
```

```python
import functools

import jax
import jax.numpy as jnp
import numpy as np
from jax import lax
from jax.experimental import pallas as pl
from jax.experimental.pallas import tpu as pltpu
from jax.sharding import Mesh
from jax.sharding import PartitionSpec as P

KVH = 2
HD = 128
BLOCK = 128
CHUNK = 384
EVERY = ("outer", "core", "fsdp")
VMEM_BYTES = 32 * 1024 * 1024


def to_column(line):
    n = line.shape[1]
    rows = lax.broadcasted_iota(jnp.int32, (n, n), 0)
    lanes = lax.broadcasted_iota(jnp.int32, (n, n), 1)
    spread = jnp.broadcast_to(line, (n, n))
    return jnp.sum(jnp.where(rows == lanes, spread, 0.0), axis=1, keepdims=True)


def to_line(column):
    n = column.shape[0]
    rows = lax.broadcasted_iota(jnp.int32, (n, n), 0)
    lanes = lax.broadcasted_iota(jnp.int32, (n, n), 1)
    spread = jnp.broadcast_to(column, (n, n))
    return jnp.sum(jnp.where(rows == lanes, spread, 0.0), axis=0, keepdims=True)


def sine_cosine(angles):
    turns = jnp.floor(angles * (2.0 / np.pi) + 0.5)
    rest = angles - turns * 1.5703125
    rest = rest - turns * 4.837512969970703125e-4
    rest = rest - turns * 7.54978995489188216e-8
    square = rest * rest
    sine = (-1.9515295891e-4 * square + 8.3321608736e-3) * square - 1.6666654611e-1
    sine = sine * square * rest + rest
    cosine = (2.443315711809948e-5 * square - 1.388731625493765e-3) * square
    cosine = (cosine + 4.166664568298827e-2) * square * square - 0.5 * square + 1.0
    quarter = turns.astype(jnp.int32) & 3
    odd = (quarter & 1) == 1
    sines, cosines = jnp.where(odd, cosine, sine), jnp.where(odd, sine, cosine)
    sines = jnp.where(quarter >= 2, -sines, sines)
    cosines = jnp.where(((quarter + 1) & 2) == 2, -cosines, cosines)
    return sines, cosines


def transposed_dot(left, right):
    return lax.dot_general(
        left, right, (((0,), (0,)), ((), ())), preferred_element_type=jnp.float32
    )


def full_sum(values):
    return jnp.sum(jnp.sum(values, axis=1, keepdims=True), axis=0, keepdims=True)


def fetch(sources, buffers, semaphores):
    copies = []
    for i, (source, buffer) in enumerate(zip(sources, buffers)):
        copy = pltpu.make_async_copy(source, buffer, semaphores.at[i])
        copy.start()
        copies.append(copy)
    return copies


def call(kernel, out_shape, args, after=None, in_hbm=False, fetched=0, scratch=(), flops=0):
    count = len(args)
    args = [
        pltpu.with_memory_space_constraint(arg, pltpu.HBM) if i < fetched else arg
        for i, arg in enumerate(args)
    ]
    spaces = [pl.ANY] * fetched + [pltpu.VMEM] * (count - fetched)
    run = kernel
    if after is not None:
        if in_hbm:
            after = pltpu.with_memory_space_constraint(after, pltpu.HBM)
        args, spaces = args + [after], spaces + [pl.ANY]

        def run(*refs):
            kernel(*refs[:count], *refs[count + 1 :])

    scratch = list(scratch) + [pltpu.VMEM(arg.shape, arg.dtype) for arg in args[:fetched]]
    if fetched:
        scratch.append(pltpu.SemaphoreType.DMA((fetched,)))
    return pl.pallas_call(
        run,
        out_shape=out_shape,
        in_specs=[pl.BlockSpec(memory_space=space) for space in spaces],
        scratch_shapes=scratch,
        out_specs=jax.tree.map(lambda _: pl.BlockSpec(memory_space=pltpu.VMEM), out_shape),
        compiler_params=pltpu.CompilerParams(vmem_limit_bytes=VMEM_BYTES),
        cost_estimate=pl.CostEstimate(
            flops=flops, bytes_accessed=1000000, transcendentals=0
        ),
    )(*args)


def stack_kernel(*refs):
    for i, part_ref in enumerate(refs[:-1]):
        refs[-1][i] = part_ref[...]


def bundle_kernel(shifts, mine_ref, *refs):
    out_ref = refs[-1]
    rows = refs[0].shape[1]
    member = lax.axis_index("fsdp")
    parts = [part_ref.at[i] for part_ref in refs[:-1] for i in range(part_ref.shape[0])]
    for shift, part_ref in zip(shifts, parts):
        out_ref[aligned(jnp.bitwise_xor(member, shift), rows), :] = part_ref[...]
    out_ref[len(parts) * rows :, :] = mine_ref[...]


def backward_kernel(
    positions_hbm, frequency_hbm, counts_hbm, ratios_hbm, cotangent_hbm, tokens_hbm,
    gain_hbm, weight_hbm,
    normed_ref, cosines_ref, sines_ref, both_ref, given_ref, folded_ref,
    positions_ref, frequency_ref, counts_ref, ratios_ref, cotangent_ref, tokens_ref,
    gain_ref, weight_ref,
    semaphores,
):
    copies = fetch(
        (
            positions_hbm, frequency_hbm, counts_hbm, ratios_hbm, cotangent_hbm, tokens_hbm,
            gain_hbm, weight_hbm,
        ),
        (
            positions_ref, frequency_ref, counts_ref, ratios_ref, cotangent_ref, tokens_ref,
            gain_ref, weight_ref,
        ),
        semaphores,
    )
    rows, width = tokens_ref.shape
    core = lax.axis_index("core")
    domain = lax.axis_index("outer") * 2 + core
    member = lax.axis_index("fsdp")

    for copy in copies[:5]:
        copy.wait()
    lines = positions_ref[...].astype(jnp.float32)
    lanes = lax.broadcasted_iota(jnp.int32, (lines.shape[1], HD), 1)
    left = lanes < HD // 2
    first, second = to_column(lines[0:1, :]), to_column(lines[1:2, :])
    sines, cosines = sine_cosine(jnp.where(left, first, second) * frequency_ref[...])
    turned_sines, turned_cosines = pltpu.roll(sines, HD // 2, 1), pltpu.roll(cosines, HD // 2, 1)
    cosines = jnp.concatenate(
        [jnp.where(left, cosines, turned_cosines), jnp.where(left, turned_cosines, cosines)]
    )
    sines = jnp.concatenate(
        [jnp.where(left, -sines, turned_sines), jnp.where(left, -turned_sines, sines)]
    )
    cosines_ref[...] = cosines
    sines_ref[...] = sines

    counts = counts_ref[...].astype(jnp.float32)
    ratios = ratios_ref[...].astype(jnp.float32)
    at_domain = lax.broadcasted_iota(jnp.int32, counts.shape, 0) == domain
    at_member = lax.broadcasted_iota(jnp.int32, counts.shape, 1) == member
    ratio_at = lax.broadcasted_iota(jnp.int32, ratios.shape, 1) == domain
    live_total = full_sum(counts) * float(BLOCK)
    own_rows = full_sum(jnp.where(at_domain, counts, 0.0)) * float(BLOCK)
    own_live = full_sum(jnp.where(at_domain & at_member, counts, 0.0)) * float(BLOCK)
    own_ratio = full_sum(jnp.where(ratio_at, ratios, 0.0))
    factor = own_ratio / full_sum(ratios) * live_total / own_rows
    row_ids = lax.broadcasted_iota(jnp.int32, (rows, 1), 0).astype(jnp.float32)
    row_factor = jnp.where(row_ids < own_live, factor, 0.0)

    weighted = cotangent_ref[...].astype(jnp.float32) * row_factor
    key_width = KVH * HD
    turned = []
    for head in range(KVH):
        part = weighted[:, head * HD : (head + 1) * HD]
        turned.append(part * cosines - pltpu.roll(part, HD // 2, 1) * sines)
    keys = jnp.concatenate(turned, axis=1).astype(jnp.bfloat16)
    values = weighted[:, key_width:].astype(jnp.bfloat16)
    keep = jnp.where(core == 0, keys, values)
    give = jnp.where(core == 0, values, keys)
    half = keep.shape[1]
    both_ref[:, :half] = keep
    both_ref[:, half:] = give

    copies[5].wait()
    step = 32
    for start in range(0, rows, step):
        block = tokens_ref[start : start + step, :].astype(jnp.float32)
        mean_square = jnp.sum(block * block, axis=1, keepdims=True) * (1.0 / width)
        normed_ref[start : start + step, :] = (
            block * lax.rsqrt(mean_square + 1e-06)
        ).astype(jnp.bfloat16)

    for start in range(0, given_ref.shape[0], CHUNK):
        at = slice(start, start + CHUNK)
        given_ref[at, :] = transposed_dot(normed_ref[:, at], give).astype(jnp.bfloat16)

    columns = pl.ds(pl.multiple_of(core * half, half), half)
    copies[6].wait()
    gains = to_column(gain_ref[...].astype(jnp.float32).reshape(1, -1))
    copies[7].wait()
    folded = weight_ref[:, columns].astype(jnp.float32) * gains
    folded_ref[...] = folded.astype(jnp.bfloat16)


def rest_kernel(normed_ref, both_ref, own_ref, given_ref):
    width, half = own_ref.shape
    done = width - given_ref.shape[0]
    keep, both = both_ref[:, :half], both_ref[...]
    for start in range(0, width, CHUNK):
        at = slice(start, start + CHUNK)
        if start < done:
            own_ref[at, :] = transposed_dot(normed_ref[:, at], keep)
            continue
        result = transposed_dot(normed_ref[:, at], both)
        own_ref[at, :] = result[:, :half]
        given_ref[start - done : start - done + CHUNK, :] = result[:, half:].astype(jnp.bfloat16)


def aligned(index, size):
    return pl.ds(pl.multiple_of(index * size, size), size)


def total(kept, taken):
    return kept + taken.astype(jnp.float32)


def pair_kernel(own_ref, first_ref, second_ref, *out_refs):
    count, rows, _ = out_refs[0].shape
    first_count = first_ref.shape[0] // (4 * rows)
    y, x = lax.axis_index("outer"), lax.axis_index("fsdp") % 2
    for (away_y, away_x), out_ref in zip(((0, 0), (1, 1), (0, 1), (1, 0)), out_refs):
        to_y, to_x = jnp.bitwise_xor(y, away_y), jnp.bitwise_xor(x, away_x)
        for i in range(count):
            at = aligned(4 * i + 2 * to_x + to_y, rows)
            in_first = i < first_count
            taken_ref = first_ref if in_first else second_ref
            taken_at = 4 * (i if in_first else i - first_count) + 2 * to_x + to_y
            taken_at = aligned(taken_at, rows)
            out_ref[i] = total(own_ref[at, :], taken_ref[taken_at, :]).astype(out_ref.dtype)


def z_kernel(kept_ref, first_ref, second_ref, third_ref, *out_refs):
    z = lax.axis_index("fsdp") // 2
    for shift, out_ref in enumerate(out_refs):
        at = jnp.bitwise_xor(z, shift)
        result = total(kept_ref[at], first_ref[at])
        result = total(total(result, second_ref[at]), third_ref[at])
        out_ref[...] = result.astype(out_ref.dtype)


def last_kernel(own_ref, *refs):
    result = own_ref[...]
    for taken_ref in refs[:-1]:
        result = total(result, taken_ref[...])
    refs[-1][...] = result.astype(jnp.bfloat16)


def finish_kernel(counts_ref, gain_ref, weight_ref, *refs):
    parts, (weight_grad_ref, gain_grad_ref, sum_ref) = refs[:-3], refs[-3:]
    rows, half = parts[0].shape
    y, core = lax.axis_index("outer"), lax.axis_index("core")
    live_total = full_sum(counts_ref[...].astype(jnp.float32)) * float(BLOCK)
    scale = 1.0 / jnp.sqrt(live_total)
    gains = to_column(gain_ref[...].astype(jnp.float32).reshape(1, -1)) * scale
    shifts = (0, 1) if len(parts) == 2 else (0, 1, 2, 3)
    for shift, part_ref in zip(shifts, parts):
        at_y = 0 if len(parts) == 2 else jnp.bitwise_xor(y, shift // 2)
        at = jnp.bitwise_xor(core, shift % 2)
        tail = slice(part_ref.shape[0] - rows, None)
        sum_ref[aligned(at_y, rows), aligned(at, half)] = part_ref[tail, :].astype(jnp.float32)
    result = sum_ref[...]
    weight_grad_ref[...] = result * gains
    dots = jnp.sum(result * weight_ref[...].astype(jnp.float32), axis=1, keepdims=True)
    gain_grad_ref[...] = to_line(dots * scale).reshape(-1)


def forward_kernel(normed_ref, own_ref, other_ref, cosines_ref, sines_ref, out_ref):
    core = lax.axis_index("core")
    normed = normed_ref[...]
    width = normed.shape[1]
    own = jnp.dot(normed, own_ref[:width, :], preferred_element_type=jnp.float32)
    other = jnp.dot(normed, other_ref[:width, :], preferred_element_type=jnp.float32)
    keys = jnp.where(core == 0, own, other)
    values = jnp.where(core == 0, other, own)
    cosines, sines = cosines_ref[...], sines_ref[...]
    for head in range(KVH):
        part = keys[:, head * HD : (head + 1) * HD]
        out_ref[:, head * HD : (head + 1) * HD] = (
            part * cosines + pltpu.roll(part, HD // 2, 1) * sines
        ).astype(jnp.bfloat16)
    out_ref[:, KVH * HD :] = values.astype(jnp.bfloat16)


def exchange(value, axes, count, shift):
    return lax.ppermute(value, axes, [(i, i ^ shift) for i in range(count)])


def sum_on_cube(own, first, second, shard):
    width, half = own.shape
    f32, bf16 = jnp.float32, jnp.bfloat16
    shape = jax.ShapeDtypeStruct
    rows = shard // 2
    kept, *given = call(
        pair_kernel,
        (shape((4, rows, half), f32),) + (shape((4, rows, half), bf16),) * 3,
        (own, first, second),
    )
    pair_done = kept
    taken = [
        exchange(given[0], ("outer", "fsdp"), 16, 9),
        exchange(given[1], "fsdp", 8, 1),
        exchange(given[2], "outer", 2, 1),
    ]
    first_xy, second_xy, third_xy = taken
    kept, *given = call(
        z_kernel,
        (shape((rows, half), f32),) + (shape((rows, half), bf16),) * 3,
        (kept, *taken),
        flops=2 * 10**9,
    )
    taken = [exchange(given[i], "fsdp", 8, 2 * i + 2) for i in (1, 2, 0)]
    mine = call(last_kernel, shape((rows, half), bf16), (kept, *taken))
    return mine, (pair_done, pair_done, pair_done, mine)


def gather_on_cube(folded, steps):
    shard, half = folded.shape
    shape = jax.ShapeDtypeStruct

    def over(part, shift):
        return exchange(part, "fsdp", 8, shift)

    def stack(*parts, after):
        out = shape((len(parts), shard, half), folded.dtype)
        return call(stack_kernel, out, parts, after=after)

    near, far = over(folded, 2), over(folded, 4)
    both = over(stack(far, after=steps[0])[0], 2)
    low = stack(folded, near, after=steps[1])
    high = stack(far, both, after=steps[2])
    shifts = (0, 2, 4, 6, 1, 3, 5, 7)
    mine = steps[3]
    return call(
        functools.partial(bundle_kernel, shifts),
        shape((8 * shard + mine.shape[0], half), folded.dtype),
        (mine, low, high, over(low, 1), over(high, 1)),
    )


def body(outer, members, tokens, gain, kv_weight, positions, cotangent, counts, ratios):
    domains = 2 * outer
    rows, width = tokens.shape
    shard, columns = kv_weight.shape
    half = columns // 2
    f32, bf16 = jnp.float32, jnp.bfloat16
    shape = jax.ShapeDtypeStruct
    on_cube = outer == 2 and members == 8 and shard % 32 == 0

    exponents = np.arange(HD, dtype=np.float64) % (HD // 2) * (2.0 / HD)
    frequency = jnp.asarray(np.power(1000000.0, -exponents).astype(np.float32))
    normed, cosines, sines, both, given, folded = call(
        backward_kernel,
        (
            shape((rows, width), bf16),
            shape((rows, HD), f32),
            shape((rows, HD), f32),
            shape((rows, columns), bf16),
            shape((width - width // 4, half), bf16),
            shape((shard, half), bf16),
        ),
        (
            positions.reshape(rows // 128, 128),
            frequency.reshape(1, HD),
            counts,
            ratios.reshape(1, domains),
            cotangent,
            tokens,
            gain,
            kv_weight,
        ),
        fetched=8,
    )
    first = exchange(given, "core", 2, 1)
    own, given = call(
        rest_kernel, (shape((width, half), f32), shape((width // 4, half), bf16)), (normed, both)
    )
    second = exchange(given, "core", 2, 1)
    if on_cube:
        mine, steps = sum_on_cube(own, first, second, shard)
        own_half = gather_on_cube(folded, steps)
        other_half = exchange(own_half, "core", 2, 1)
        sums = [mine, other_half] + [exchange(mine, ("outer", "core"), 4, i) for i in (2, 3)]
    else:
        pair = own + jnp.concatenate([first, second]).astype(f32)
        pair = lax.psum_scatter(pair, "fsdp", scatter_dimension=0, tiled=True)
        mine = lax.psum(pair, "outer")
        own_half = lax.all_gather(folded, "fsdp", axis=0, tiled=True)
        other_half = exchange(own_half, "core", 2, 1)
        sums = [mine, exchange(mine, "core", 2, 1)]
    keys_out = call(
        forward_kernel,
        shape((rows, columns), bf16),
        (normed, own_half, other_half, cosines, sines),
        after=mine,
    )
    weight_grad, gain_grad = call(
        finish_kernel,
        (shape((shard, columns), f32), shape((shard,), f32)),
        (counts, gain, kv_weight, *sums),
        scratch=[pltpu.VMEM((shard, columns), f32)],
        after=keys_out,
        in_hbm=True,
    )
    return (keys_out, weight_grad, gain_grad)


def solution(mesh):
    domains, members = mesh.shape["dom"], mesh.shape["fsdp"]
    outer = domains // 2
    split = Mesh(mesh.devices.reshape(outer, 2, members), EVERY)
    return jax.shard_map(
        functools.partial(body, outer, members),
        mesh=split,
        in_specs=(
            P(EVERY, None),
            P("fsdp"),
            P("fsdp", None),
            P(EVERY),
            P(EVERY, None),
            P(),
            P(),
        ),
        out_specs=(P(EVERY, None), P("fsdp", None), P("fsdp")),
        check_vma=False,
    )
```

```python
import functools

import jax
import jax.numpy as jnp
import numpy as np
from jax import lax
from jax.experimental import pallas as pl
from jax.experimental.pallas import tpu as pltpu
from jax.sharding import Mesh
from jax.sharding import PartitionSpec as P

KVH = 2
HD = 128
BLOCK = 128
CHUNK = 384
EVERY = ("outer", "core", "fsdp")
VMEM_BYTES = 32 * 1024 * 1024


def to_column(line):
    n = line.shape[1]
    rows = lax.broadcasted_iota(jnp.int32, (n, n), 0)
    lanes = lax.broadcasted_iota(jnp.int32, (n, n), 1)
    spread = jnp.broadcast_to(line, (n, n))
    return jnp.sum(jnp.where(rows == lanes, spread, 0.0), axis=1, keepdims=True)


def to_line(column):
    n = column.shape[0]
    rows = lax.broadcasted_iota(jnp.int32, (n, n), 0)
    lanes = lax.broadcasted_iota(jnp.int32, (n, n), 1)
    spread = jnp.broadcast_to(column, (n, n))
    return jnp.sum(jnp.where(rows == lanes, spread, 0.0), axis=0, keepdims=True)


def sine_cosine(angles):
    turns = jnp.floor(angles * (2.0 / np.pi) + 0.5)
    rest = angles - turns * 1.5703125
    rest = rest - turns * 4.837512969970703125e-4
    rest = rest - turns * 7.54978995489188216e-8
    square = rest * rest
    sine = (-1.9515295891e-4 * square + 8.3321608736e-3) * square - 1.6666654611e-1
    sine = sine * square * rest + rest
    cosine = (2.443315711809948e-5 * square - 1.388731625493765e-3) * square
    cosine = (cosine + 4.166664568298827e-2) * square * square - 0.5 * square + 1.0
    quarter = turns.astype(jnp.int32) & 3
    odd = (quarter & 1) == 1
    sines, cosines = jnp.where(odd, cosine, sine), jnp.where(odd, sine, cosine)
    sines = jnp.where(quarter >= 2, -sines, sines)
    cosines = jnp.where(((quarter + 1) & 2) == 2, -cosines, cosines)
    return sines, cosines


def transposed_dot(left, right):
    return lax.dot_general(
        left, right, (((0,), (0,)), ((), ())), preferred_element_type=jnp.float32
    )


def full_sum(values):
    return jnp.sum(jnp.sum(values, axis=1, keepdims=True), axis=0, keepdims=True)


def fetch(sources, buffers, semaphores):
    copies = []
    for i, (source, buffer) in enumerate(zip(sources, buffers)):
        copy = pltpu.make_async_copy(source, buffer, semaphores.at[i])
        copy.start()
        copies.append(copy)
    return copies


def call(kernel, out_shape, args, after=None, in_hbm=False, fetched=0, scratch=(), flops=0):
    count = len(args)
    args = [
        pltpu.with_memory_space_constraint(arg, pltpu.HBM) if i < fetched else arg
        for i, arg in enumerate(args)
    ]
    spaces = [pl.ANY] * fetched + [pltpu.VMEM] * (count - fetched)
    run = kernel
    if after is not None:
        if in_hbm:
            after = pltpu.with_memory_space_constraint(after, pltpu.HBM)
        args, spaces = args + [after], spaces + [pl.ANY]

        def run(*refs):
            kernel(*refs[:count], *refs[count + 1 :])

    scratch = list(scratch) + [pltpu.VMEM(arg.shape, arg.dtype) for arg in args[:fetched]]
    if fetched:
        scratch.append(pltpu.SemaphoreType.DMA((fetched,)))
    return pl.pallas_call(
        run,
        out_shape=out_shape,
        in_specs=[pl.BlockSpec(memory_space=space) for space in spaces],
        scratch_shapes=scratch,
        out_specs=jax.tree.map(lambda _: pl.BlockSpec(memory_space=pltpu.VMEM), out_shape),
        compiler_params=pltpu.CompilerParams(vmem_limit_bytes=VMEM_BYTES),
        cost_estimate=pl.CostEstimate(
            flops=flops, bytes_accessed=1000000, transcendentals=0
        ),
    )(*args)


def stack_kernel(*refs):
    for i, part_ref in enumerate(refs[:-1]):
        refs[-1][i] = part_ref[...]


def scale_kernel(counts_ref, gain_ref, gains_ref, scale_ref):
    live_total = full_sum(counts_ref[...].astype(jnp.float32)) * float(BLOCK)
    scale_ref[...] = 1.0 / jnp.sqrt(live_total)
    gains_ref[...] = to_column(gain_ref[...].astype(jnp.float32).reshape(1, -1)) * scale_ref[...]


def stack_scale_kernel(counts_ref, gain_ref, first_ref, second_ref, *refs):
    out_ref, gains_ref, scale_ref = refs
    stack_kernel(first_ref, second_ref, out_ref)
    scale_kernel(counts_ref, gain_ref, gains_ref, scale_ref)


def bundle_kernel(shifts, mine_ref, *refs):
    out_ref = refs[-1]
    rows = refs[0].shape[1]
    member = lax.axis_index("fsdp")
    parts = [part_ref.at[i] for part_ref in refs[:-1] for i in range(part_ref.shape[0])]
    for shift, part_ref in zip(shifts, parts):
        out_ref[aligned(jnp.bitwise_xor(member, shift), rows), :] = part_ref[...]
    out_ref[len(parts) * rows :, :] = mine_ref[...]


def backward_kernel(
    positions_hbm, frequency_hbm, counts_hbm, ratios_hbm, cotangent_hbm, tokens_hbm,
    gain_hbm, weight_hbm,
    normed_ref, cosines_ref, sines_ref, both_ref, given_ref, folded_ref,
    positions_ref, frequency_ref, counts_ref, ratios_ref, cotangent_ref, tokens_ref,
    gain_ref, weight_ref,
    semaphores,
):
    copies = fetch(
        (
            positions_hbm, frequency_hbm, counts_hbm, ratios_hbm, cotangent_hbm, tokens_hbm,
            gain_hbm, weight_hbm,
        ),
        (
            positions_ref, frequency_ref, counts_ref, ratios_ref, cotangent_ref, tokens_ref,
            gain_ref, weight_ref,
        ),
        semaphores,
    )
    rows, width = tokens_ref.shape
    core = lax.axis_index("core")
    domain = lax.axis_index("outer") * 2 + core
    member = lax.axis_index("fsdp")

    for copy in copies[:5]:
        copy.wait()
    lines = positions_ref[...].astype(jnp.float32)
    lanes = lax.broadcasted_iota(jnp.int32, (lines.shape[1], HD), 1)
    left = lanes < HD // 2
    first, second = to_column(lines[0:1, :]), to_column(lines[1:2, :])
    sines, cosines = sine_cosine(jnp.where(left, first, second) * frequency_ref[...])
    turned_sines, turned_cosines = pltpu.roll(sines, HD // 2, 1), pltpu.roll(cosines, HD // 2, 1)
    cosines = jnp.concatenate(
        [jnp.where(left, cosines, turned_cosines), jnp.where(left, turned_cosines, cosines)]
    )
    sines = jnp.concatenate(
        [jnp.where(left, -sines, turned_sines), jnp.where(left, -turned_sines, sines)]
    )
    cosines_ref[...] = cosines
    sines_ref[...] = sines

    counts = counts_ref[...].astype(jnp.float32)
    ratios = ratios_ref[...].astype(jnp.float32)
    at_domain = lax.broadcasted_iota(jnp.int32, counts.shape, 0) == domain
    at_member = lax.broadcasted_iota(jnp.int32, counts.shape, 1) == member
    ratio_at = lax.broadcasted_iota(jnp.int32, ratios.shape, 1) == domain
    live_total = full_sum(counts) * float(BLOCK)
    own_rows = full_sum(jnp.where(at_domain, counts, 0.0)) * float(BLOCK)
    own_live = full_sum(jnp.where(at_domain & at_member, counts, 0.0)) * float(BLOCK)
    own_ratio = full_sum(jnp.where(ratio_at, ratios, 0.0))
    factor = own_ratio / full_sum(ratios) * live_total / own_rows
    row_ids = lax.broadcasted_iota(jnp.int32, (rows, 1), 0).astype(jnp.float32)
    row_factor = jnp.where(row_ids < own_live, factor, 0.0)

    weighted = cotangent_ref[...].astype(jnp.float32) * row_factor
    key_width = KVH * HD
    turned = []
    for head in range(KVH):
        part = weighted[:, head * HD : (head + 1) * HD]
        turned.append(part * cosines - pltpu.roll(part, HD // 2, 1) * sines)
    keys = jnp.concatenate(turned, axis=1).astype(jnp.bfloat16)
    values = weighted[:, key_width:].astype(jnp.bfloat16)
    keep = jnp.where(core == 0, keys, values)
    give = jnp.where(core == 0, values, keys)
    half = keep.shape[1]
    both_ref[:, :half] = keep
    both_ref[:, half:] = give

    copies[5].wait()
    step = 32
    for start in range(0, rows, step):
        block = tokens_ref[start : start + step, :].astype(jnp.float32)
        mean_square = jnp.sum(block * block, axis=1, keepdims=True) * (1.0 / width)
        normed_ref[start : start + step, :] = (
            block * lax.rsqrt(mean_square + 1e-06)
        ).astype(jnp.bfloat16)

    for start in range(0, given_ref.shape[0], CHUNK):
        at = slice(start, start + CHUNK)
        given_ref[at, :] = transposed_dot(normed_ref[:, at], give).astype(jnp.bfloat16)

    columns = pl.ds(pl.multiple_of(core * half, half), half)
    copies[6].wait()
    gains = to_column(gain_ref[...].astype(jnp.float32).reshape(1, -1))
    copies[7].wait()
    folded = weight_ref[:, columns].astype(jnp.float32) * gains
    folded_ref[...] = folded.astype(jnp.bfloat16)


def rest_kernel(normed_ref, both_ref, own_ref, given_ref):
    width, half = own_ref.shape
    done = width - given_ref.shape[0]
    keep, both = both_ref[:, :half], both_ref[...]
    for start in range(0, width, CHUNK):
        at = slice(start, start + CHUNK)
        if start < done:
            own_ref[at, :] = transposed_dot(normed_ref[:, at], keep)
            continue
        result = transposed_dot(normed_ref[:, at], both)
        own_ref[at, :] = result[:, :half]
        given_ref[start - done : start - done + CHUNK, :] = result[:, half:].astype(jnp.bfloat16)


def aligned(index, size):
    return pl.ds(pl.multiple_of(index * size, size), size)


def total(kept, taken):
    return kept + taken.astype(jnp.float32)


def pair_kernel(own_ref, first_ref, second_ref, *out_refs):
    count, rows, _ = out_refs[0].shape
    first_count = first_ref.shape[0] // (4 * rows)
    y, x = lax.axis_index("outer"), lax.axis_index("fsdp") % 2
    for (away_y, away_x), out_ref in zip(((0, 0), (1, 1), (0, 1), (1, 0)), out_refs):
        to_y, to_x = jnp.bitwise_xor(y, away_y), jnp.bitwise_xor(x, away_x)
        for i in range(count):
            at = aligned(4 * i + 2 * to_x + to_y, rows)
            in_first = i < first_count
            taken_ref = first_ref if in_first else second_ref
            taken_at = 4 * (i if in_first else i - first_count) + 2 * to_x + to_y
            taken_at = aligned(taken_at, rows)
            out_ref[i] = total(own_ref[at, :], taken_ref[taken_at, :]).astype(out_ref.dtype)


def z_kernel(kept_ref, first_ref, second_ref, third_ref, *out_refs):
    z = lax.axis_index("fsdp") // 2
    for shift, out_ref in enumerate(out_refs):
        at = jnp.bitwise_xor(z, shift)
        result = total(kept_ref[at], first_ref[at])
        result = total(total(result, second_ref[at]), third_ref[at])
        out_ref[...] = result.astype(out_ref.dtype)


def last_kernel(own_ref, *refs):
    result = own_ref[...]
    for taken_ref in refs[:-1]:
        result = total(result, taken_ref[...])
    refs[-1][...] = result.astype(jnp.bfloat16)


def finish_kernel(gains_ref, scale_ref, weight_ref, *refs):
    parts, (weight_grad_ref, gain_grad_ref, sum_ref) = refs[:-3], refs[-3:]
    rows, half = parts[0].shape
    y, core = lax.axis_index("outer"), lax.axis_index("core")
    shifts = (0, 1) if len(parts) == 2 else (0, 1, 2, 3)
    for shift, part_ref in zip(shifts, parts):
        at_y = 0 if len(parts) == 2 else jnp.bitwise_xor(y, shift // 2)
        at = jnp.bitwise_xor(core, shift % 2)
        tail = slice(part_ref.shape[0] - rows, None)
        sum_ref[aligned(at_y, rows), aligned(at, half)] = part_ref[tail, :].astype(jnp.float32)
    result = sum_ref[...]
    weight_grad_ref[...] = result * gains_ref[...]
    dots = jnp.sum(result * weight_ref[...].astype(jnp.float32), axis=1, keepdims=True)
    gain_grad_ref[...] = to_line(dots * scale_ref[...]).reshape(-1)


def forward_kernel(normed_ref, own_ref, other_ref, cosines_ref, sines_ref, out_ref):
    core = lax.axis_index("core")
    normed = normed_ref[...]
    width = normed.shape[1]
    own = jnp.dot(normed, own_ref[:width, :], preferred_element_type=jnp.float32)
    other = jnp.dot(normed, other_ref[:width, :], preferred_element_type=jnp.float32)
    keys = jnp.where(core == 0, own, other)
    values = jnp.where(core == 0, other, own)
    cosines, sines = cosines_ref[...], sines_ref[...]
    for head in range(KVH):
        part = keys[:, head * HD : (head + 1) * HD]
        out_ref[:, head * HD : (head + 1) * HD] = (
            part * cosines + pltpu.roll(part, HD // 2, 1) * sines
        ).astype(jnp.bfloat16)
    out_ref[:, KVH * HD :] = values.astype(jnp.bfloat16)


def scale_shapes(shard):
    return (
        jax.ShapeDtypeStruct((shard, 1), jnp.float32),
        jax.ShapeDtypeStruct((1, 1), jnp.float32),
    )


def exchange(value, axes, count, shift):
    return lax.ppermute(value, axes, [(i, i ^ shift) for i in range(count)])


def sum_on_cube(own, first, second, shard):
    width, half = own.shape
    f32, bf16 = jnp.float32, jnp.bfloat16
    shape = jax.ShapeDtypeStruct
    rows = shard // 2
    kept, *given = call(
        pair_kernel,
        (shape((4, rows, half), f32),) + (shape((4, rows, half), bf16),) * 3,
        (own, first, second),
    )
    pair_done = kept
    taken = [
        exchange(given[0], ("outer", "fsdp"), 16, 9),
        exchange(given[1], "fsdp", 8, 1),
        exchange(given[2], "outer", 2, 1),
    ]
    first_xy, second_xy, third_xy = taken
    kept, *given = call(
        z_kernel,
        (shape((rows, half), f32),) + (shape((rows, half), bf16),) * 3,
        (kept, *taken),
        flops=2 * 10**9,
    )
    taken = [exchange(given[i], "fsdp", 8, 2 * i + 2) for i in (1, 2, 0)]
    mine = call(last_kernel, shape((rows, half), bf16), (kept, *taken))
    return mine, (pair_done, pair_done, pair_done, mine)


def gather_on_cube(folded, counts, gain, steps):
    shard, half = folded.shape
    shape = jax.ShapeDtypeStruct

    def over(part, shift):
        return exchange(part, "fsdp", 8, shift)

    def stack(*parts, after):
        out = shape((len(parts), shard, half), folded.dtype)
        return call(stack_kernel, out, parts, after=after)

    near, far = over(folded, 2), over(folded, 4)
    both = over(stack(far, after=steps[0])[0], 2)
    low, gains, scale = call(
        stack_scale_kernel,
        (shape((2, shard, half), folded.dtype),) + scale_shapes(shard),
        (counts, gain, folded, near),
        after=steps[1],
    )
    high = stack(far, both, after=steps[2])
    shifts = (0, 2, 4, 6, 1, 3, 5, 7)
    mine = steps[3]
    own_half = call(
        functools.partial(bundle_kernel, shifts),
        shape((8 * shard + mine.shape[0], half), folded.dtype),
        (mine, low, high, over(low, 1), over(high, 1)),
    )
    return own_half, gains, scale


def body(outer, members, tokens, gain, kv_weight, positions, cotangent, counts, ratios):
    domains = 2 * outer
    rows, width = tokens.shape
    shard, columns = kv_weight.shape
    half = columns // 2
    f32, bf16 = jnp.float32, jnp.bfloat16
    shape = jax.ShapeDtypeStruct
    on_cube = outer == 2 and members == 8 and shard % 32 == 0

    exponents = np.arange(HD, dtype=np.float64) % (HD // 2) * (2.0 / HD)
    frequency = jnp.asarray(np.power(1000000.0, -exponents).astype(np.float32))
    normed, cosines, sines, both, given, folded = call(
        backward_kernel,
        (
            shape((rows, width), bf16),
            shape((rows, HD), f32),
            shape((rows, HD), f32),
            shape((rows, columns), bf16),
            shape((width - width // 4, half), bf16),
            shape((shard, half), bf16),
        ),
        (
            positions.reshape(rows // 128, 128),
            frequency.reshape(1, HD),
            counts,
            ratios.reshape(1, domains),
            cotangent,
            tokens,
            gain,
            kv_weight,
        ),
        fetched=8,
    )
    first = exchange(given, "core", 2, 1)
    own, given = call(
        rest_kernel, (shape((width, half), f32), shape((width // 4, half), bf16)), (normed, both)
    )
    second = exchange(given, "core", 2, 1)
    if on_cube:
        mine, steps = sum_on_cube(own, first, second, shard)
        own_half, gains, scale = gather_on_cube(folded, counts, gain, steps)
        other_half = exchange(own_half, "core", 2, 1)
        sums = [mine, other_half] + [exchange(mine, ("outer", "core"), 4, i) for i in (2, 3)]
    else:
        pair = own + jnp.concatenate([first, second]).astype(f32)
        pair = lax.psum_scatter(pair, "fsdp", scatter_dimension=0, tiled=True)
        mine = lax.psum(pair, "outer")
        own_half = lax.all_gather(folded, "fsdp", axis=0, tiled=True)
        other_half = exchange(own_half, "core", 2, 1)
        sums = [mine, exchange(mine, "core", 2, 1)]
        gains, scale = call(scale_kernel, scale_shapes(shard), (counts, gain))
    keys_out = call(
        forward_kernel,
        shape((rows, columns), bf16),
        (normed, own_half, other_half, cosines, sines),
        after=mine,
    )
    weight_grad, gain_grad = call(
        finish_kernel,
        (shape((shard, columns), f32), shape((shard,), f32)),
        (gains, scale, kv_weight, *sums),
        scratch=[pltpu.VMEM((shard, columns), f32)],
        after=keys_out,
        in_hbm=True,
    )
    return (keys_out, weight_grad, gain_grad)


def solution(mesh):
    domains, members = mesh.shape["dom"], mesh.shape["fsdp"]
    outer = domains // 2
    split = Mesh(mesh.devices.reshape(outer, 2, members), EVERY)
    return jax.shard_map(
        functools.partial(body, outer, members),
        mesh=split,
        in_specs=(
            P(EVERY, None),
            P("fsdp"),
            P("fsdp", None),
            P(EVERY),
            P(EVERY, None),
            P(),
            P(),
        ),
        out_specs=(P(EVERY, None), P("fsdp", None), P("fsdp")),
        check_vma=False,
    )
```

```python
import functools

import jax
import jax.numpy as jnp
import numpy as np
from jax import lax
from jax.experimental import pallas as pl
from jax.experimental.pallas import tpu as pltpu
from jax.sharding import Mesh
from jax.sharding import PartitionSpec as P

KVH = 2
HD = 128
BLOCK = 128
CHUNK = 384
EVERY = ("outer", "core", "fsdp")
VMEM_BYTES = 32 * 1024 * 1024


def to_column(line):
    n = line.shape[1]
    rows = lax.broadcasted_iota(jnp.int32, (n, n), 0)
    lanes = lax.broadcasted_iota(jnp.int32, (n, n), 1)
    spread = jnp.broadcast_to(line, (n, n))
    return jnp.sum(jnp.where(rows == lanes, spread, 0.0), axis=1, keepdims=True)


def to_line(column):
    n = column.shape[0]
    rows = lax.broadcasted_iota(jnp.int32, (n, n), 0)
    lanes = lax.broadcasted_iota(jnp.int32, (n, n), 1)
    spread = jnp.broadcast_to(column, (n, n))
    return jnp.sum(jnp.where(rows == lanes, spread, 0.0), axis=0, keepdims=True)


def sine_cosine(angles):
    turns = jnp.floor(angles * (2.0 / np.pi) + 0.5)
    rest = angles - turns * 1.5703125
    rest = rest - turns * 4.837512969970703125e-4
    rest = rest - turns * 7.54978995489188216e-8
    square = rest * rest
    sine = (-1.9515295891e-4 * square + 8.3321608736e-3) * square - 1.6666654611e-1
    sine = sine * square * rest + rest
    cosine = (2.443315711809948e-5 * square - 1.388731625493765e-3) * square
    cosine = (cosine + 4.166664568298827e-2) * square * square - 0.5 * square + 1.0
    quarter = turns.astype(jnp.int32) & 3
    odd = (quarter & 1) == 1
    sines, cosines = jnp.where(odd, cosine, sine), jnp.where(odd, sine, cosine)
    sines = jnp.where(quarter >= 2, -sines, sines)
    cosines = jnp.where(((quarter + 1) & 2) == 2, -cosines, cosines)
    return sines, cosines


def transposed_dot(left, right):
    return lax.dot_general(
        left, right, (((0,), (0,)), ((), ())), preferred_element_type=jnp.float32
    )


def full_sum(values):
    return jnp.sum(jnp.sum(values, axis=1, keepdims=True), axis=0, keepdims=True)


def fetch(sources, buffers, semaphores):
    copies = []
    for i, (source, buffer) in enumerate(zip(sources, buffers)):
        copy = pltpu.make_async_copy(source, buffer, semaphores.at[i])
        copy.start()
        copies.append(copy)
    return copies


def call(kernel, out_shape, args, after=None, in_hbm=False, fetched=0, scratch=(), flops=0):
    count = len(args)
    args = [
        pltpu.with_memory_space_constraint(arg, pltpu.HBM) if i < fetched else arg
        for i, arg in enumerate(args)
    ]
    spaces = [pl.ANY] * fetched + [pltpu.VMEM] * (count - fetched)
    run = kernel
    if after is not None:
        if in_hbm:
            after = pltpu.with_memory_space_constraint(after, pltpu.HBM)
        args, spaces = args + [after], spaces + [pl.ANY]

        def run(*refs):
            kernel(*refs[:count], *refs[count + 1 :])

    scratch = list(scratch) + [pltpu.VMEM(arg.shape, arg.dtype) for arg in args[:fetched]]
    if fetched:
        scratch.append(pltpu.SemaphoreType.DMA((fetched,)))
    return pl.pallas_call(
        run,
        out_shape=out_shape,
        in_specs=[pl.BlockSpec(memory_space=space) for space in spaces],
        scratch_shapes=scratch,
        out_specs=jax.tree.map(lambda _: pl.BlockSpec(memory_space=pltpu.VMEM), out_shape),
        compiler_params=pltpu.CompilerParams(vmem_limit_bytes=VMEM_BYTES),
        cost_estimate=pl.CostEstimate(
            flops=flops, bytes_accessed=1000000, transcendentals=0
        ),
    )(*args)


def stack_kernel(*refs):
    for i, part_ref in enumerate(refs[:-1]):
        refs[-1][i] = part_ref[...]


def bundle_kernel(shifts, mine_ref, *refs):
    out_ref = refs[-1]
    rows = refs[0].shape[1]
    member = lax.axis_index("fsdp")
    parts = [part_ref.at[i] for part_ref in refs[:-1] for i in range(part_ref.shape[0])]
    for shift, part_ref in zip(shifts, parts):
        out_ref[aligned(jnp.bitwise_xor(member, shift), rows), :] = part_ref[...]
    out_ref[len(parts) * rows :, :] = mine_ref[...]


def backward_kernel(
    positions_hbm, frequency_hbm, counts_hbm, ratios_hbm, cotangent_hbm, tokens_hbm,
    gain_hbm, weight_hbm,
    normed_ref, cosines_ref, sines_ref, both_ref, given_ref, folded_ref,
    positions_ref, frequency_ref, counts_ref, ratios_ref, cotangent_ref, tokens_ref,
    gain_ref, weight_ref,
    semaphores,
):
    copies = fetch(
        (
            positions_hbm, frequency_hbm, counts_hbm, ratios_hbm, cotangent_hbm, tokens_hbm,
            gain_hbm, weight_hbm,
        ),
        (
            positions_ref, frequency_ref, counts_ref, ratios_ref, cotangent_ref, tokens_ref,
            gain_ref, weight_ref,
        ),
        semaphores,
    )
    rows, width = tokens_ref.shape
    core = lax.axis_index("core")
    domain = lax.axis_index("outer") * 2 + core
    member = lax.axis_index("fsdp")

    for copy in copies[:5]:
        copy.wait()
    lines = positions_ref[...].astype(jnp.float32)
    lanes = lax.broadcasted_iota(jnp.int32, (lines.shape[1], HD), 1)
    left = lanes < HD // 2
    first, second = to_column(lines[0:1, :]), to_column(lines[1:2, :])
    sines, cosines = sine_cosine(jnp.where(left, first, second) * frequency_ref[...])
    turned_sines, turned_cosines = pltpu.roll(sines, HD // 2, 1), pltpu.roll(cosines, HD // 2, 1)
    cosines = jnp.concatenate(
        [jnp.where(left, cosines, turned_cosines), jnp.where(left, turned_cosines, cosines)]
    )
    sines = jnp.concatenate(
        [jnp.where(left, -sines, turned_sines), jnp.where(left, -turned_sines, sines)]
    )
    cosines_ref[...] = cosines
    sines_ref[...] = sines

    counts = counts_ref[...].astype(jnp.float32)
    ratios = ratios_ref[...].astype(jnp.float32)
    at_domain = lax.broadcasted_iota(jnp.int32, counts.shape, 0) == domain
    at_member = lax.broadcasted_iota(jnp.int32, counts.shape, 1) == member
    ratio_at = lax.broadcasted_iota(jnp.int32, ratios.shape, 1) == domain
    live_total = full_sum(counts) * float(BLOCK)
    own_rows = full_sum(jnp.where(at_domain, counts, 0.0)) * float(BLOCK)
    own_live = full_sum(jnp.where(at_domain & at_member, counts, 0.0)) * float(BLOCK)
    own_ratio = full_sum(jnp.where(ratio_at, ratios, 0.0))
    factor = own_ratio / full_sum(ratios) * live_total / own_rows
    row_ids = lax.broadcasted_iota(jnp.int32, (rows, 1), 0).astype(jnp.float32)
    row_factor = jnp.where(row_ids < own_live, factor, 0.0)

    weighted = cotangent_ref[...].astype(jnp.float32) * row_factor
    key_width = KVH * HD
    turned = []
    for head in range(KVH):
        part = weighted[:, head * HD : (head + 1) * HD]
        turned.append(part * cosines - pltpu.roll(part, HD // 2, 1) * sines)
    keys = jnp.concatenate(turned, axis=1).astype(jnp.bfloat16)
    values = weighted[:, key_width:].astype(jnp.bfloat16)
    keep = jnp.where(core == 0, keys, values)
    give = jnp.where(core == 0, values, keys)
    half = keep.shape[1]
    both_ref[:, :half] = keep
    both_ref[:, half:] = give

    copies[5].wait()
    step = 32
    for start in range(0, rows, step):
        block = tokens_ref[start : start + step, :].astype(jnp.float32)
        mean_square = jnp.sum(block * block, axis=1, keepdims=True) * (1.0 / width)
        normed_ref[start : start + step, :] = (
            block * lax.rsqrt(mean_square + 1e-06)
        ).astype(jnp.bfloat16)

    for start in range(0, given_ref.shape[0], CHUNK):
        at = slice(start, start + CHUNK)
        given_ref[at, :] = transposed_dot(normed_ref[:, at], give).astype(jnp.bfloat16)

    columns = pl.ds(pl.multiple_of(core * half, half), half)
    copies[6].wait()
    gains = to_column(gain_ref[...].astype(jnp.float32).reshape(1, -1))
    copies[7].wait()
    folded = weight_ref[:, columns].astype(jnp.float32) * gains
    folded_ref[...] = folded.astype(jnp.bfloat16)


def rest_kernel(normed_ref, both_ref, own_ref, given_ref):
    width, half = own_ref.shape
    done = width - given_ref.shape[0]
    keep, both = both_ref[:, :half], both_ref[...]
    for start in range(0, width, CHUNK):
        at = slice(start, start + CHUNK)
        if start < done:
            own_ref[at, :] = transposed_dot(normed_ref[:, at], keep)
            continue
        result = transposed_dot(normed_ref[:, at], both)
        own_ref[at, :] = result[:, :half]
        given_ref[start - done : start - done + CHUNK, :] = result[:, half:].astype(jnp.bfloat16)


def aligned(index, size):
    return pl.ds(pl.multiple_of(index * size, size), size)


def total(kept, taken):
    return kept + taken.astype(jnp.float32)


def pair_kernel(own_ref, first_ref, second_ref, *out_refs):
    count, rows, _ = out_refs[0].shape
    first_count = first_ref.shape[0] // (4 * rows)
    y, x = lax.axis_index("outer"), lax.axis_index("fsdp") % 2
    for (away_y, away_x), out_ref in zip(((0, 0), (1, 1), (0, 1), (1, 0)), out_refs):
        to_y, to_x = jnp.bitwise_xor(y, away_y), jnp.bitwise_xor(x, away_x)
        for i in range(count):
            at = aligned(4 * i + 2 * to_x + to_y, rows)
            in_first = i < first_count
            taken_ref = first_ref if in_first else second_ref
            taken_at = 4 * (i if in_first else i - first_count) + 2 * to_x + to_y
            taken_at = aligned(taken_at, rows)
            out_ref[i] = total(own_ref[at, :], taken_ref[taken_at, :]).astype(out_ref.dtype)


def z_kernel(kept_ref, first_ref, second_ref, third_ref, *out_refs):
    z = lax.axis_index("fsdp") // 2
    for shift, out_ref in enumerate(out_refs):
        at = jnp.bitwise_xor(z, shift)
        result = total(kept_ref[at], first_ref[at])
        result = total(total(result, second_ref[at]), third_ref[at])
        out_ref[...] = result.astype(out_ref.dtype)


def last_kernel(own_ref, *refs):
    result = own_ref[...]
    for taken_ref in refs[:-1]:
        result = total(result, taken_ref[...])
    refs[-1][...] = result.astype(jnp.bfloat16)


def finish_kernel(counts_ref, gain_ref, weight_ref, *refs):
    parts, (weight_grad_ref, gain_grad_ref, sum_ref) = refs[:-3], refs[-3:]
    rows, half = parts[0].shape
    y, core = lax.axis_index("outer"), lax.axis_index("core")
    live_total = full_sum(counts_ref[...].astype(jnp.float32)) * float(BLOCK)
    scale = 1.0 / jnp.sqrt(live_total)
    gains = to_column(gain_ref[...].astype(jnp.float32).reshape(1, -1)) * scale
    shifts = (0, 1) if len(parts) == 2 else (0, 1, 2, 3)
    for shift, part_ref in zip(shifts, parts):
        at_y = 0 if len(parts) == 2 else jnp.bitwise_xor(y, shift // 2)
        at = jnp.bitwise_xor(core, shift % 2)
        tail = slice(part_ref.shape[0] - rows, None)
        sum_ref[aligned(at_y, rows), aligned(at, half)] = part_ref[tail, :].astype(jnp.float32)
    result = sum_ref[...]
    weight_grad_ref[...] = result * gains
    dots = jnp.sum(result * weight_ref[...].astype(jnp.float32), axis=1, keepdims=True)
    gain_grad_ref[...] = to_line(dots * scale).reshape(-1)


def forward_kernel(normed_ref, own_ref, other_ref, cosines_ref, sines_ref, out_ref):
    core = lax.axis_index("core")
    normed = normed_ref[...]
    width = normed.shape[1]
    own = jnp.dot(normed, own_ref[:width, :], preferred_element_type=jnp.float32)
    other = jnp.dot(normed, other_ref[:width, :], preferred_element_type=jnp.float32)
    keys = jnp.where(core == 0, own, other)
    values = jnp.where(core == 0, other, own)
    cosines, sines = cosines_ref[...], sines_ref[...]
    for head in range(KVH):
        part = keys[:, head * HD : (head + 1) * HD]
        out_ref[:, head * HD : (head + 1) * HD] = (
            part * cosines + pltpu.roll(part, HD // 2, 1) * sines
        ).astype(jnp.bfloat16)
    out_ref[:, KVH * HD :] = values.astype(jnp.bfloat16)


def exchange(value, axes, count, shift):
    return lax.ppermute(value, axes, [(i, i ^ shift) for i in range(count)])


def sum_on_cube(own, first, second, shard):
    width, half = own.shape
    f32, bf16 = jnp.float32, jnp.bfloat16
    shape = jax.ShapeDtypeStruct
    rows = shard // 2
    kept, *given = call(
        pair_kernel,
        (shape((4, rows, half), f32),) + (shape((4, rows, half), bf16),) * 3,
        (own, first, second),
    )
    pair_done = kept
    taken = [
        exchange(given[0], ("outer", "fsdp"), 16, 9),
        exchange(given[1], "fsdp", 8, 1),
        exchange(given[2], "outer", 2, 1),
    ]
    first_xy, second_xy, third_xy = taken
    kept, *given = call(
        z_kernel,
        (shape((rows, half), f32),) + (shape((rows, half), bf16),) * 3,
        (kept, *taken),
        flops=2 * 10**9,
    )
    taken = [exchange(given[i], "fsdp", 8, 2 * i + 2) for i in (2, 1, 0)]
    mine = call(last_kernel, shape((rows, half), bf16), (kept, *taken))
    return mine, (pair_done, pair_done, pair_done, mine)


def gather_on_cube(folded, steps):
    shard, half = folded.shape
    shape = jax.ShapeDtypeStruct

    def over(part, shift):
        return exchange(part, "fsdp", 8, shift)

    def stack(*parts, after):
        out = shape((len(parts), shard, half), folded.dtype)
        return call(stack_kernel, out, parts, after=after)

    near, far = over(folded, 2), over(folded, 4)
    both = over(stack(far, after=steps[0])[0], 2)
    low = stack(folded, near, after=steps[1])
    high = stack(far, both, after=steps[2])
    shifts = (0, 2, 4, 6, 1, 3, 5, 7)
    mine = steps[3]
    return call(
        functools.partial(bundle_kernel, shifts),
        shape((8 * shard + mine.shape[0], half), folded.dtype),
        (mine, low, high, over(low, 1), over(high, 1)),
    )


def body(outer, members, tokens, gain, kv_weight, positions, cotangent, counts, ratios):
    domains = 2 * outer
    rows, width = tokens.shape
    shard, columns = kv_weight.shape
    half = columns // 2
    f32, bf16 = jnp.float32, jnp.bfloat16
    shape = jax.ShapeDtypeStruct
    on_cube = outer == 2 and members == 8 and shard % 32 == 0

    exponents = np.arange(HD, dtype=np.float64) % (HD // 2) * (2.0 / HD)
    frequency = jnp.asarray(np.power(1000000.0, -exponents).astype(np.float32))
    normed, cosines, sines, both, given, folded = call(
        backward_kernel,
        (
            shape((rows, width), bf16),
            shape((rows, HD), f32),
            shape((rows, HD), f32),
            shape((rows, columns), bf16),
            shape((width - width // 4, half), bf16),
            shape((shard, half), bf16),
        ),
        (
            positions.reshape(rows // 128, 128),
            frequency.reshape(1, HD),
            counts,
            ratios.reshape(1, domains),
            cotangent,
            tokens,
            gain,
            kv_weight,
        ),
        fetched=8,
    )
    first = exchange(given, "core", 2, 1)
    own, given = call(
        rest_kernel, (shape((width, half), f32), shape((width // 4, half), bf16)), (normed, both)
    )
    second = exchange(given, "core", 2, 1)
    if on_cube:
        mine, steps = sum_on_cube(own, first, second, shard)
        own_half = gather_on_cube(folded, steps)
        other_half = exchange(own_half, "core", 2, 1)
        sums = [mine, other_half] + [exchange(mine, ("outer", "core"), 4, i) for i in (2, 3)]
    else:
        pair = own + jnp.concatenate([first, second]).astype(f32)
        pair = lax.psum_scatter(pair, "fsdp", scatter_dimension=0, tiled=True)
        mine = lax.psum(pair, "outer")
        own_half = lax.all_gather(folded, "fsdp", axis=0, tiled=True)
        other_half = exchange(own_half, "core", 2, 1)
        sums = [mine, exchange(mine, "core", 2, 1)]
    keys_out = call(
        forward_kernel,
        shape((rows, columns), bf16),
        (normed, own_half, other_half, cosines, sines),
        after=mine,
    )
    weight_grad, gain_grad = call(
        finish_kernel,
        (shape((shard, columns), f32), shape((shard,), f32)),
        (counts, gain, kv_weight, *sums),
        scratch=[pltpu.VMEM((shard, columns), f32)],
        after=keys_out,
        in_hbm=True,
    )
    return (keys_out, weight_grad, gain_grad)


def solution(mesh):
    domains, members = mesh.shape["dom"], mesh.shape["fsdp"]
    outer = domains // 2
    split = Mesh(mesh.devices.reshape(outer, 2, members), EVERY)
    return jax.shard_map(
        functools.partial(body, outer, members),
        mesh=split,
        in_specs=(
            P(EVERY, None),
            P("fsdp"),
            P("fsdp", None),
            P(EVERY),
            P(EVERY, None),
            P(),
            P(),
        ),
        out_specs=(P(EVERY, None), P("fsdp", None), P("fsdp")),
        check_vma=False,
    )
```

```python
import functools

import jax
import jax.numpy as jnp
import numpy as np
from jax import lax
from jax.experimental import pallas as pl
from jax.experimental.pallas import tpu as pltpu
from jax.sharding import Mesh
from jax.sharding import PartitionSpec as P

KVH = 2
HD = 128
BLOCK = 128
CHUNK = 384
EVERY = ("outer", "core", "fsdp")
VMEM_BYTES = 32 * 1024 * 1024


def to_column(line):
    n = line.shape[1]
    rows = lax.broadcasted_iota(jnp.int32, (n, n), 0)
    lanes = lax.broadcasted_iota(jnp.int32, (n, n), 1)
    spread = jnp.broadcast_to(line, (n, n))
    return jnp.sum(jnp.where(rows == lanes, spread, 0.0), axis=1, keepdims=True)


def to_line(column):
    n = column.shape[0]
    rows = lax.broadcasted_iota(jnp.int32, (n, n), 0)
    lanes = lax.broadcasted_iota(jnp.int32, (n, n), 1)
    spread = jnp.broadcast_to(column, (n, n))
    return jnp.sum(jnp.where(rows == lanes, spread, 0.0), axis=0, keepdims=True)


def sine_cosine(angles):
    turns = jnp.floor(angles * (2.0 / np.pi) + 0.5)
    rest = angles - turns * 1.5703125
    rest = rest - turns * 4.837512969970703125e-4
    rest = rest - turns * 7.54978995489188216e-8
    square = rest * rest
    sine = (-1.9515295891e-4 * square + 8.3321608736e-3) * square - 1.6666654611e-1
    sine = sine * square * rest + rest
    cosine = (2.443315711809948e-5 * square - 1.388731625493765e-3) * square
    cosine = (cosine + 4.166664568298827e-2) * square * square - 0.5 * square + 1.0
    quarter = turns.astype(jnp.int32) & 3
    odd = (quarter & 1) == 1
    sines, cosines = jnp.where(odd, cosine, sine), jnp.where(odd, sine, cosine)
    sines = jnp.where(quarter >= 2, -sines, sines)
    cosines = jnp.where(((quarter + 1) & 2) == 2, -cosines, cosines)
    return sines, cosines


def transposed_dot(left, right):
    return lax.dot_general(
        left, right, (((0,), (0,)), ((), ())), preferred_element_type=jnp.float32
    )


def full_sum(values):
    return jnp.sum(jnp.sum(values, axis=1, keepdims=True), axis=0, keepdims=True)


def fetch(sources, buffers, semaphores):
    copies = []
    for i, (source, buffer) in enumerate(zip(sources, buffers)):
        copy = pltpu.make_async_copy(source, buffer, semaphores.at[i])
        copy.start()
        copies.append(copy)
    return copies


def call(kernel, out_shape, args, after=None, in_hbm=False, fetched=0, scratch=(), flops=0):
    count = len(args)
    args = [
        pltpu.with_memory_space_constraint(arg, pltpu.HBM) if i < fetched else arg
        for i, arg in enumerate(args)
    ]
    spaces = [pl.ANY] * fetched + [pltpu.VMEM] * (count - fetched)
    run = kernel
    if after is not None:
        if in_hbm:
            after = pltpu.with_memory_space_constraint(after, pltpu.HBM)
        args, spaces = args + [after], spaces + [pl.ANY]

        def run(*refs):
            kernel(*refs[:count], *refs[count + 1 :])

    scratch = list(scratch) + [pltpu.VMEM(arg.shape, arg.dtype) for arg in args[:fetched]]
    if fetched:
        scratch.append(pltpu.SemaphoreType.DMA((fetched,)))
    return pl.pallas_call(
        run,
        out_shape=out_shape,
        in_specs=[pl.BlockSpec(memory_space=space) for space in spaces],
        scratch_shapes=scratch,
        out_specs=jax.tree.map(lambda _: pl.BlockSpec(memory_space=pltpu.VMEM), out_shape),
        compiler_params=pltpu.CompilerParams(vmem_limit_bytes=VMEM_BYTES),
        cost_estimate=pl.CostEstimate(
            flops=flops, bytes_accessed=1000000, transcendentals=0
        ),
    )(*args)


def stack_kernel(*refs):
    for i, part_ref in enumerate(refs[:-1]):
        refs[-1][i] = part_ref[...]


def bundle_kernel(shifts, mine_ref, *refs):
    out_ref = refs[-1]
    rows = refs[0].shape[1]
    member = lax.axis_index("fsdp")
    parts = [part_ref.at[i] for part_ref in refs[:-1] for i in range(part_ref.shape[0])]
    for shift, part_ref in zip(shifts, parts):
        out_ref[aligned(jnp.bitwise_xor(member, shift), rows), :] = part_ref[...]
    out_ref[len(parts) * rows :, :] = mine_ref[...]


def backward_kernel(
    positions_hbm, frequency_hbm, counts_hbm, ratios_hbm, cotangent_hbm, tokens_hbm,
    gain_hbm, weight_hbm,
    normed_ref, cosines_ref, sines_ref, both_ref, given_ref, folded_ref,
    positions_ref, frequency_ref, counts_ref, ratios_ref, cotangent_ref, tokens_ref,
    gain_ref, weight_ref,
    semaphores,
):
    copies = fetch(
        (
            positions_hbm, frequency_hbm, counts_hbm, ratios_hbm, cotangent_hbm, tokens_hbm,
            gain_hbm, weight_hbm,
        ),
        (
            positions_ref, frequency_ref, counts_ref, ratios_ref, cotangent_ref, tokens_ref,
            gain_ref, weight_ref,
        ),
        semaphores,
    )
    rows, width = tokens_ref.shape
    core = lax.axis_index("core")
    domain = lax.axis_index("outer") * 2 + core
    member = lax.axis_index("fsdp")

    for copy in copies[:5]:
        copy.wait()
    lines = positions_ref[...].astype(jnp.float32)
    lanes = lax.broadcasted_iota(jnp.int32, (lines.shape[1], HD), 1)
    left = lanes < HD // 2
    first, second = to_column(lines[0:1, :]), to_column(lines[1:2, :])
    sines, cosines = sine_cosine(jnp.where(left, first, second) * frequency_ref[...])
    turned_sines, turned_cosines = pltpu.roll(sines, HD // 2, 1), pltpu.roll(cosines, HD // 2, 1)
    cosines = jnp.concatenate(
        [jnp.where(left, cosines, turned_cosines), jnp.where(left, turned_cosines, cosines)]
    )
    sines = jnp.concatenate(
        [jnp.where(left, -sines, turned_sines), jnp.where(left, -turned_sines, sines)]
    )
    cosines_ref[...] = cosines
    sines_ref[...] = sines

    counts = counts_ref[...].astype(jnp.float32)
    ratios = ratios_ref[...].astype(jnp.float32)
    at_domain = lax.broadcasted_iota(jnp.int32, counts.shape, 0) == domain
    at_member = lax.broadcasted_iota(jnp.int32, counts.shape, 1) == member
    ratio_at = lax.broadcasted_iota(jnp.int32, ratios.shape, 1) == domain
    live_total = full_sum(counts) * float(BLOCK)
    own_rows = full_sum(jnp.where(at_domain, counts, 0.0)) * float(BLOCK)
    own_live = full_sum(jnp.where(at_domain & at_member, counts, 0.0)) * float(BLOCK)
    own_ratio = full_sum(jnp.where(ratio_at, ratios, 0.0))
    factor = own_ratio / full_sum(ratios) * live_total / own_rows
    row_ids = lax.broadcasted_iota(jnp.int32, (rows, 1), 0).astype(jnp.float32)
    row_factor = jnp.where(row_ids < own_live, factor, 0.0)

    weighted = cotangent_ref[...].astype(jnp.float32) * row_factor
    key_width = KVH * HD
    turned = []
    for head in range(KVH):
        part = weighted[:, head * HD : (head + 1) * HD]
        turned.append(part * cosines - pltpu.roll(part, HD // 2, 1) * sines)
    keys = jnp.concatenate(turned, axis=1).astype(jnp.bfloat16)
    values = weighted[:, key_width:].astype(jnp.bfloat16)
    keep = jnp.where(core == 0, keys, values)
    give = jnp.where(core == 0, values, keys)
    half = keep.shape[1]
    both_ref[:, :half] = keep
    both_ref[:, half:] = give

    copies[5].wait()
    step = 32
    for start in range(0, rows, step):
        block = tokens_ref[start : start + step, :].astype(jnp.float32)
        mean_square = jnp.sum(block * block, axis=1, keepdims=True) * (1.0 / width)
        normed_ref[start : start + step, :] = (
            block * lax.rsqrt(mean_square + 1e-06)
        ).astype(jnp.bfloat16)

    for start in range(0, given_ref.shape[0], CHUNK):
        at = slice(start, start + CHUNK)
        given_ref[at, :] = transposed_dot(normed_ref[:, at], give).astype(jnp.bfloat16)

    columns = pl.ds(pl.multiple_of(core * half, half), half)
    copies[6].wait()
    gains = to_column(gain_ref[...].astype(jnp.float32).reshape(1, -1))
    copies[7].wait()
    folded = weight_ref[:, columns].astype(jnp.float32) * gains
    folded_ref[...] = folded.astype(jnp.bfloat16)


def rest_kernel(normed_ref, both_ref, own_ref, given_ref):
    width, half = own_ref.shape
    done = width - given_ref.shape[0]
    keep, both = both_ref[:, :half], both_ref[...]
    for start in range(0, width, CHUNK):
        at = slice(start, start + CHUNK)
        if start < done:
            own_ref[at, :] = transposed_dot(normed_ref[:, at], keep)
            continue
        result = transposed_dot(normed_ref[:, at], both)
        own_ref[at, :] = result[:, :half]
        given_ref[start - done : start - done + CHUNK, :] = result[:, half:].astype(jnp.bfloat16)


def aligned(index, size):
    return pl.ds(pl.multiple_of(index * size, size), size)


def total(kept, taken):
    return kept + taken.astype(jnp.float32)


def pair_kernel(own_ref, first_ref, second_ref, *out_refs):
    count, rows, _ = out_refs[0].shape
    first_count = first_ref.shape[0] // (4 * rows)
    y, x = lax.axis_index("outer"), lax.axis_index("fsdp") % 2
    for (away_y, away_x), out_ref in zip(((0, 0), (1, 1), (0, 1), (1, 0)), out_refs):
        to_y, to_x = jnp.bitwise_xor(y, away_y), jnp.bitwise_xor(x, away_x)
        for i in range(count):
            at = aligned(4 * i + 2 * to_x + to_y, rows)
            in_first = i < first_count
            taken_ref = first_ref if in_first else second_ref
            taken_at = 4 * (i if in_first else i - first_count) + 2 * to_x + to_y
            taken_at = aligned(taken_at, rows)
            out_ref[i] = total(own_ref[at, :], taken_ref[taken_at, :]).astype(out_ref.dtype)


def z_kernel(kept_ref, first_ref, second_ref, third_ref, *out_refs):
    z = lax.axis_index("fsdp") // 2
    for shift, out_ref in enumerate(out_refs):
        at = jnp.bitwise_xor(z, shift)
        result = total(kept_ref[at], first_ref[at])
        result = total(total(result, second_ref[at]), third_ref[at])
        out_ref[...] = result.astype(out_ref.dtype)


def last_kernel(own_ref, *refs):
    result = own_ref[...]
    for taken_ref in refs[:-1]:
        result = total(result, taken_ref[...])
    refs[-1][...] = result.astype(jnp.bfloat16)


def finish_kernel(counts_ref, gain_ref, weight_ref, *refs):
    parts, (weight_grad_ref, gain_grad_ref, sum_ref) = refs[:-3], refs[-3:]
    rows, half = parts[0].shape
    y, core = lax.axis_index("outer"), lax.axis_index("core")
    live_total = full_sum(counts_ref[...].astype(jnp.float32)) * float(BLOCK)
    scale = 1.0 / jnp.sqrt(live_total)
    gains = to_column(gain_ref[...].astype(jnp.float32).reshape(1, -1)) * scale
    shifts = (0, 1) if len(parts) == 2 else (0, 1, 3, 2)
    for shift, part_ref in zip(shifts, parts):
        at_y = 0 if len(parts) == 2 else jnp.bitwise_xor(y, shift // 2)
        at = jnp.bitwise_xor(core, shift % 2)
        tail = slice(part_ref.shape[0] - rows, None)
        sum_ref[aligned(at_y, rows), aligned(at, half)] = part_ref[tail, :].astype(jnp.float32)
    result = sum_ref[...]
    weight_grad_ref[...] = result * gains
    dots = jnp.sum(result * weight_ref[...].astype(jnp.float32), axis=1, keepdims=True)
    gain_grad_ref[...] = to_line(dots * scale).reshape(-1)


def forward_kernel(normed_ref, own_ref, other_ref, cosines_ref, sines_ref, out_ref):
    core = lax.axis_index("core")
    normed = normed_ref[...]
    width = normed.shape[1]
    own = jnp.dot(normed, own_ref[:width, :], preferred_element_type=jnp.float32)
    other = jnp.dot(normed, other_ref[:width, :], preferred_element_type=jnp.float32)
    keys = jnp.where(core == 0, own, other)
    values = jnp.where(core == 0, other, own)
    cosines, sines = cosines_ref[...], sines_ref[...]
    for head in range(KVH):
        part = keys[:, head * HD : (head + 1) * HD]
        out_ref[:, head * HD : (head + 1) * HD] = (
            part * cosines + pltpu.roll(part, HD // 2, 1) * sines
        ).astype(jnp.bfloat16)
    out_ref[:, KVH * HD :] = values.astype(jnp.bfloat16)


def exchange(value, axes, count, shift):
    return lax.ppermute(value, axes, [(i, i ^ shift) for i in range(count)])


def sum_on_cube(own, first, second, shard):
    width, half = own.shape
    f32, bf16 = jnp.float32, jnp.bfloat16
    shape = jax.ShapeDtypeStruct
    rows = shard // 2
    kept, *given = call(
        pair_kernel,
        (shape((4, rows, half), f32),) + (shape((4, rows, half), bf16),) * 3,
        (own, first, second),
    )
    pair_done = kept
    taken = [
        exchange(given[0], ("outer", "fsdp"), 16, 9),
        exchange(given[1], "fsdp", 8, 1),
        exchange(given[2], "outer", 2, 1),
    ]
    first_xy, second_xy, third_xy = taken
    kept, *given = call(
        z_kernel,
        (shape((rows, half), f32),) + (shape((rows, half), bf16),) * 3,
        (kept, *taken),
        flops=2 * 10**9,
    )
    taken = [exchange(given[i], "fsdp", 8, 2 * i + 2) for i in (2, 1, 0)]
    mine = call(last_kernel, shape((rows, half), bf16), (kept, *taken))
    return mine, (pair_done, pair_done, pair_done, mine)


def gather_on_cube(folded, steps):
    shard, half = folded.shape
    shape = jax.ShapeDtypeStruct

    def over(part, shift):
        return exchange(part, "fsdp", 8, shift)

    def stack(*parts, after):
        out = shape((len(parts), shard, half), folded.dtype)
        return call(stack_kernel, out, parts, after=after)

    near, far = over(folded, 2), over(folded, 4)
    both = over(stack(far, after=steps[0])[0], 2)
    low = stack(folded, near, after=steps[1])
    high = stack(far, both, after=steps[2])
    shifts = (0, 2, 4, 6, 1, 3, 5, 7)
    mine = steps[3]
    return call(
        functools.partial(bundle_kernel, shifts),
        shape((8 * shard + mine.shape[0], half), folded.dtype),
        (mine, low, high, over(low, 1), over(high, 1)),
    )


def body(outer, members, tokens, gain, kv_weight, positions, cotangent, counts, ratios):
    domains = 2 * outer
    rows, width = tokens.shape
    shard, columns = kv_weight.shape
    half = columns // 2
    f32, bf16 = jnp.float32, jnp.bfloat16
    shape = jax.ShapeDtypeStruct
    on_cube = outer == 2 and members == 8 and shard % 32 == 0

    exponents = np.arange(HD, dtype=np.float64) % (HD // 2) * (2.0 / HD)
    frequency = jnp.asarray(np.power(1000000.0, -exponents).astype(np.float32))
    normed, cosines, sines, both, given, folded = call(
        backward_kernel,
        (
            shape((rows, width), bf16),
            shape((rows, HD), f32),
            shape((rows, HD), f32),
            shape((rows, columns), bf16),
            shape((width - width // 4, half), bf16),
            shape((shard, half), bf16),
        ),
        (
            positions.reshape(rows // 128, 128),
            frequency.reshape(1, HD),
            counts,
            ratios.reshape(1, domains),
            cotangent,
            tokens,
            gain,
            kv_weight,
        ),
        fetched=8,
    )
    first = exchange(given, "core", 2, 1)
    own, given = call(
        rest_kernel, (shape((width, half), f32), shape((width // 4, half), bf16)), (normed, both)
    )
    second = exchange(given, "core", 2, 1)
    if on_cube:
        mine, steps = sum_on_cube(own, first, second, shard)
        own_half = gather_on_cube(folded, steps)
        other_half = exchange(own_half, "core", 2, 1)
        sums = [mine, other_half] + [exchange(mine, ("outer", "core"), 4, i) for i in (3, 2)]
    else:
        pair = own + jnp.concatenate([first, second]).astype(f32)
        pair = lax.psum_scatter(pair, "fsdp", scatter_dimension=0, tiled=True)
        mine = lax.psum(pair, "outer")
        own_half = lax.all_gather(folded, "fsdp", axis=0, tiled=True)
        other_half = exchange(own_half, "core", 2, 1)
        sums = [mine, exchange(mine, "core", 2, 1)]
    keys_out = call(
        forward_kernel,
        shape((rows, columns), bf16),
        (normed, own_half, other_half, cosines, sines),
        after=mine,
    )
    weight_grad, gain_grad = call(
        finish_kernel,
        (shape((shard, columns), f32), shape((shard,), f32)),
        (counts, gain, kv_weight, *sums),
        scratch=[pltpu.VMEM((shard, columns), f32)],
        after=keys_out,
        in_hbm=True,
    )
    return (keys_out, weight_grad, gain_grad)


def solution(mesh):
    domains, members = mesh.shape["dom"], mesh.shape["fsdp"]
    outer = domains // 2
    split = Mesh(mesh.devices.reshape(outer, 2, members), EVERY)
    return jax.shard_map(
        functools.partial(body, outer, members),
        mesh=split,
        in_specs=(
            P(EVERY, None),
            P("fsdp"),
            P("fsdp", None),
            P(EVERY),
            P(EVERY, None),
            P(),
            P(),
        ),
        out_specs=(P(EVERY, None), P("fsdp", None), P("fsdp")),
        check_vma=False,
    )
```
